32 devices in a mesh: tm: 8 (over z, y), clip: 4 (over x, core).
Axes of the slice: x: 2, y: 2, z: 4, core: 2. Of those that a mesh axis runs over, the one named last changes fastest.
Arguments:
- student_query: bfloat16 [4096, 1024], P('tm', 'clip'), may hold values from -12 to 12
- teacher_key: bfloat16 [16384, 1024], P('tm', 'clip'), may hold values from -1000 to 1000
- teacher_value: bfloat16 [16384, 1024], P('tm', 'clip'), may hold values from -12 to 12
- clip_order: int32 [16384], replicated, may hold values from 0 to 16383, as said below
- band_start: int32 [128], P('tm'), may hold values from -16 to -1
- band_end: int32 [128], P('tm'), may hold values from 1 to 16
- output_weight: bfloat16 [1024, 1024], P('clip'), may hold values from -0.1875 to 0.1875
- cotangent: bfloat16 [4096, 1024], P('tm', 'clip'), may hold values from -6 to 6
Outputs:
- joined: bfloat16 [4096, 1024], P('tm', 'clip')
- grad_query: bfloat16 [4096, 1024], P('tm', 'clip')
- grad_output_weight: float32 [1024, 1024], P('clip')
The draws below stay inside these ranges and needn't reach their ends.
Inputs may be any that keep to these rules, and one draw needn't show every extreme that they name: clip_order is a permutation. For a time row t of time shard j = t // 2048, clip_order[t] % 2048 lies in [j * 256, (j + 1) * 256): every input shard holds exactly 256 rows of every time shard, as one run.
All inputs are finite; a program needn't handle non-finite values.
Results may differ from the reference program's by a relative error of at most 0.0094.
Values may be sent and summed in bfloat16 or wider, within the bound.
No kernel may reach another device: no remote copies, remote signals or barrier semaphores. Data moves between devices by JAX's collectives and lax.ppermute only.
A program may use at most 128 MiB of HBM per device.

```python
import math
import jax
import jax.numpy as jnp
from jax import lax

D = 1024
HEADS = 16
HDIM = 64
SBLK = 32
TBLK = 128
TROWS_DEV = 2048
REACH = 16
TS = 4096
TT = 16384
NSB = 128


def shuffle_one(stream_piece):
    return jax.random.permutation(stream_piece, TROWS_DEV)


def order_table(base_key):
    stream = jax.random.fold_in(base_key, 5)
    shard_count = TT // TROWS_DEV
    streams = jax.random.split(stream, shard_count)
    shuffled = jax.vmap(shuffle_one)(streams).astype(jnp.int32)
    portion = TROWS_DEV // shard_count
    target = jnp.arange(shard_count, dtype=jnp.int32)[:, None]
    placed = shuffled // portion * TROWS_DEV + target * portion + shuffled % portion
    return placed.reshape(TT).astype(jnp.int32)


def query_table(base_key):
    stream = jax.random.fold_in(base_key, 11)
    return jnp.clip(2.0 * jax.random.normal(stream, (TS, D), jnp.float32), -12.0, 12.0)


def band_table(base_key):
    streams = jax.random.split(jax.random.fold_in(base_key, 3), 5)
    regions = NSB // REACH
    region_width = jax.random.randint(streams[0], (regions,), 1, REACH + 1)
    block_width = jnp.repeat(region_width, REACH, total_repeat_length=NSB)
    starts = -(1 + jax.random.randint(streams[1], (NSB,), 0, 1 << 20) % block_width)
    ends = 1 + jax.random.randint(streams[2], (NSB,), 0, 1 << 20) % block_width
    blocks = jnp.arange(NSB, dtype=jnp.int32)
    starts = jnp.where(blocks == jax.random.randint(streams[3], (), 0, NSB), -REACH, starts)
    ends = jnp.where(blocks == jax.random.randint(streams[4], (), 0, NSB), REACH, ends)
    return (starts.astype(jnp.int32), ends.astype(jnp.int32))


def draw_student_query(key, part):
    return query_table(key).astype(jnp.bfloat16)


def draw_clip_order(key, part):
    return order_table(key)


def draw_band_start(key, part):
    return band_table(key)[0]


def draw_band_end(key, part):
    return band_table(key)[1]


def draw_teacher_key(key, part):
    stream = jax.random.fold_in(key, 13)
    return jnp.clip(jax.random.normal(stream, (TT, D), jnp.float32), -6.0, 6.0).astype(jnp.bfloat16)


def block_levels(key, shape, pieces, low, top_value):
    def one(position, shards_of):
        heights = jax.random.uniform(jax.random.fold_in(jax.random.fold_in(key, 6), position), (shards_of,), jnp.float32, low / len(pieces), top_value / len(pieces))
        return jnp.repeat(jnp.exp(heights), shape[position] // shards_of).reshape((-1,) + (1,) * (len(shape) - position - 1))

    gain = one(*pieces[0])
    for cut in pieces[1:]:
        gain = gain * one(*cut)
    return gain


def centred(stream_key, shape, scale, reach, cuts=(), kind=jnp.bfloat16):
    loudness = block_levels(stream_key, shape, cuts, -0.22, 0.18) if cuts else 1.0
    values = jax.random.normal(stream_key, shape, jnp.float32) * scale * loudness
    return jnp.minimum(jnp.maximum(values, -reach), reach).astype(kind)


def setup_inputs(seed: int = 0) -> dict:
    splits = jax.random.split(jax.random.key(seed), 9)
    student_query = draw_student_query(jax.random.fold_in(splits[8], 71), 0)
    teacher_key = draw_teacher_key(jax.random.fold_in(splits[8], 71), 0)
    teacher_value = centred(splits[2], (TT, D), 2.0, 12.0, ((0, 8), (1, 4)))
    clip_order = draw_clip_order(jax.random.fold_in(splits[8], 71), 0)
    band_start = draw_band_start(jax.random.fold_in(splits[8], 71), 0)
    band_end = draw_band_end(jax.random.fold_in(splits[8], 71), 0)
    output_weight = centred(splits[6], (D, D), D ** -0.5, 0.1875, ((0, 4),))
    cotangent = centred(splits[7], (TS, D), 1.0, 6.0, ((0, 8), (1, 4)))
    return {"student_query": student_query, "teacher_key": teacher_key, "teacher_value": teacher_value, "clip_order": clip_order, "band_start": band_start, "band_end": band_end, "output_weight": output_weight, "cotangent": cotangent}


def reference(student_query, teacher_key, teacher_value, clip_order, band_start, band_end, output_weight, cotangent):
    key_time = teacher_key[clip_order]
    value_time = teacher_value[clip_order]
    margin = REACH * TBLK
    key_wide = jnp.pad(key_time, ((margin, margin), (0, 0)))
    value_wide = jnp.pad(value_time, ((margin, margin), (0, 0)))
    attn_grad = jnp.dot(cotangent, output_weight.T, preferred_element_type=jnp.float32).astype(jnp.bfloat16)
    window = (2 * REACH + 1) * TBLK
    scaling = 1.0 / math.sqrt(HDIM)

    def one_block(inputs):
        block_index, query_rows, grad_rows, start_off, end_off = inputs
        anchor = (block_index * TBLK).astype(jnp.int32)
        key_part = lax.dynamic_slice(key_wide, (anchor, jnp.int32(0)), (window, D)).astype(jnp.float32).reshape(window, HEADS, HDIM)
        value_part = lax.dynamic_slice(value_wide, (anchor, jnp.int32(0)), (window, D)).astype(jnp.float32).reshape(window, HEADS, HDIM)
        query_part = query_rows.astype(jnp.float32).reshape(SBLK, HEADS, HDIM)
        scores = jnp.einsum('qhd,khd->hqk', query_part, key_part) * scaling
        key_block = block_index - REACH + jnp.arange(window, dtype=jnp.int32) // TBLK
        valid = (key_block >= block_index + start_off) & (key_block <= block_index + end_off)
        valid = valid & (key_block >= 0) & (key_block < NSB)
        scores = jnp.where(valid[None, None, :], scores, -jnp.inf)
        row_max = lax.optimization_barrier(jnp.max(scores, axis=-1, keepdims=True))
        shifted = jnp.exp(scores - row_max)
        probs = shifted / lax.optimization_barrier(jnp.sum(shifted, axis=-1, keepdims=True))
        weights = lax.optimization_barrier(probs.astype(jnp.bfloat16)).astype(jnp.float32)
        head_out = jnp.einsum('hqk,khd->qhd', weights, value_part).astype(jnp.bfloat16)
        grad_part = grad_rows.astype(jnp.float32).reshape(SBLK, HEADS, HDIM)
        dprobs = jnp.einsum('qhd,khd->hqk', grad_part, value_part)
        delta = lax.optimization_barrier(jnp.sum(probs * dprobs, axis=-1, keepdims=True))
        dscores = lax.optimization_barrier((probs * (dprobs - delta) * scaling).astype(jnp.bfloat16)).astype(jnp.float32)
        query_grad = jnp.einsum('hqk,khd->qhd', dscores, key_part).astype(jnp.bfloat16)
        return (head_out.reshape(SBLK, D), query_grad.reshape(SBLK, D))
    attention, grad_query = lax.map(one_block, (jnp.arange(NSB, dtype=jnp.int32), student_query.reshape(NSB, SBLK, D), attn_grad.reshape(NSB, SBLK, D), band_start, band_end))
    attention = attention.reshape(TS, D)
    grad_query = grad_query.reshape(TS, D)
    joined = jnp.dot(attention, output_weight, preferred_element_type=jnp.float32).astype(jnp.bfloat16)
    grad_output_weight = jnp.dot(attention.T, cotangent, preferred_element_type=jnp.float32)
    return (joined, grad_query, grad_output_weight)
```

```python
import functools
import math

import jax
import jax.numpy as jnp
from jax import lax
from jax.experimental import pallas as pl
from jax.experimental.pallas import tpu as pltpu
from jax.sharding import PartitionSpec as P

HDIM = 64
SBLK = 32
TBLK = 128
TILE = 128
CHUNK = 512
NEG = -1e30
BF = jnp.bfloat16
F32 = jnp.float32
NT = (((1,), (1,)), ((), ()))
VMEM_LIMIT = 48 * 1024 * 1024


def params(*semantics):
    return pltpu.CompilerParams(
        dimension_semantics=semantics or None, vmem_limit_bytes=VMEM_LIMIT
    )


def cost(flops, nbytes, trans=0):
    return pl.CostEstimate(flops=flops, bytes_accessed=nbytes, transcendentals=trans)


def pack_kernel(slots, k_ref, v_ref, *outs):
    for half in range(2):
        for s in range(slots):
            c = (half * slots + s) * HDIM
            outs[s][0, half] = jnp.concatenate(
                [k_ref[:, c : c + HDIM], v_ref[:, c : c + HDIM]], axis=1
            )


def pack(keys, values, groups, slots):
    rows, feats = keys.shape
    part = rows // groups
    block = pl.BlockSpec((part, feats), lambda i: (i, 0))
    return pl.pallas_call(
        functools.partial(pack_kernel, slots),
        grid=(groups,),
        in_specs=[block, block],
        out_specs=[pl.BlockSpec((1, 2, part, 2 * HDIM), lambda i: (i, 0, 0, 0))] * slots,
        out_shape=[jax.ShapeDtypeStruct((groups, 2, part, 2 * HDIM), BF)] * slots,
        compiler_params=params("arbitrary"),
        cost_estimate=cost(0, 4 * rows * feats * 2),
    )(keys, values)


def order_kernel(rows_t, idx_ref, arr_ref, kv_ref, kvt_ref, arrt):
    rows = arrt.shape[1]

    @pl.when(pl.program_id(1) == 0)
    def _():
        arr = arr_ref[...].reshape(rows, 2 * HDIM)
        for j in range(0, rows, 256):
            arrt[:, j : j + 256] = arr[j : j + 256].T

    idx = idx_ref[0]
    iota = lax.broadcasted_iota(jnp.int32, (256, rows_t), 0)
    acc = jnp.zeros((2 * HDIM, rows_t), F32)
    for j in range(0, rows, 256):
        hot = jnp.where(iota == idx - j, 1.0, 0.0).astype(BF)
        acc += jnp.dot(arrt[:, j : j + 256], hot, preferred_element_type=F32)
    kvt_ref[...] = acc.astype(BF)
    kv_ref[...] = acc.T.astype(BF)


def put_in_order(arrived, index, rows):
    sources, twice, width = arrived.shape
    rows_t = 256
    steps = rows // rows_t
    index = index.reshape(2 * steps, 1, rows_t)
    return pl.pallas_call(
        functools.partial(order_kernel, rows_t),
        grid=(2, steps),
        in_specs=[
            pl.BlockSpec((1, 1, rows_t), lambda u, t: (u * steps + t, 0, 0)),
            pl.BlockSpec((sources, twice // 2, width), lambda u, t: (0, u, 0)),
        ],
        out_specs=[
            pl.BlockSpec((rows_t, width), lambda u, t: (u * steps + t, 0)),
            pl.BlockSpec((width, rows_t), lambda u, t: (0, u * steps + t)),
        ],
        out_shape=[
            jax.ShapeDtypeStruct((2 * rows, width), BF),
            jax.ShapeDtypeStruct((width, 2 * rows), BF),
        ],
        scratch_shapes=[pltpu.VMEM((width, rows), BF)],
        compiler_params=params("arbitrary", "arbitrary"),
        cost_estimate=cost(8 * rows * rows * width, 6 * rows * width * 2),
    )(index, arrived)


def student_kernel(slots, place_ref, *refs):
    pieces = refs[:8]
    w_ref, qmine_ref, qpeer_ref, full_ref, qga_ref, qgb_ref = refs[8:]
    half, clip = place_ref[0], place_ref[1]
    rows, cols = pieces[0].shape
    hw = slots * HDIM
    for dy in range(2):
        for dc in range(4):
            r = pl.multiple_of((half ^ dy) * rows, rows)
            c = pl.multiple_of((clip ^ dc) * cols, cols)
            full_ref[pl.ds(r, rows), pl.ds(c, cols)] = pieces[dy * 4 + dc][...]
    w = w_ref[pl.ds(pl.multiple_of(half * hw, hw), hw), :]
    qmine = qmine_ref[...]
    qown = jnp.where(half == 0, qmine[:, :hw], qmine[:, hw:])
    qpeer = qpeer_ref[...]
    for u, out in enumerate((qga_ref, qgb_ref)):
        g = lax.dot_general(
            full_ref[u * rows : (u + 1) * rows, :], w, NT, preferred_element_type=F32
        ).astype(BF)
        q = jnp.where(half == u, qown, qpeer) * BF(1.0 / math.sqrt(HDIM))
        parts = []
        for s in range(slots):
            parts += [q[:, s * HDIM : (s + 1) * HDIM], g[:, s * HDIM : (s + 1) * HDIM]]
        out[...] = jnp.concatenate(parts, axis=1)


def student_side(place, pieces, weight, qmine, qpeer, slots):
    rows, cols = qmine.shape
    width = 4 * cols
    vm = pl.BlockSpec(memory_space=pltpu.VMEM)
    return pl.pallas_call(
        functools.partial(student_kernel, slots),
        in_specs=[pl.BlockSpec(memory_space=pltpu.SMEM)] + [vm] * 11,
        out_specs=[vm] * 3,
        out_shape=[
            jax.ShapeDtypeStruct((2 * rows, width), BF),
            jax.ShapeDtypeStruct((rows, 2 * slots * HDIM), BF),
            jax.ShapeDtypeStruct((rows, 2 * slots * HDIM), BF),
        ],
        compiler_params=params(),
        cost_estimate=cost(4 * rows * width * slots * HDIM, 10 * rows * width),
    )(place, *pieces, weight, qmine, qpeer)


def split3(x):
    a = x.astype(BF).astype(F32)
    b = (x - a).astype(BF).astype(F32)
    c = (x - a - b).astype(BF).astype(F32)
    return [a, b, c]


def attend_kernel(slot, lohi_ref, qga_ref, qgb_ref, kv_ref, kvt_ref, outa_ref, outb_ref, s_ref, d_ref):
    rows = qga_ref.shape[0]
    keys = kv_ref.shape[0]
    nblk = TILE // SBLK
    cblk = CHUNK // TBLK
    lane = lax.broadcasted_iota(jnp.int32, (1, TILE), 1)
    rhs_lane = lax.broadcasted_iota(jnp.int32, (TILE, 2 * HDIM), 1)
    row_id = lax.broadcasted_iota(jnp.int32, (HDIM, TILE), 0)
    for u, (q_ref, o_ref) in enumerate(((qga_ref, outa_ref), (qgb_ref, outb_ref))):

        def tile(t, carry):
            base = u * (rows // SBLK) + t * nblk
            los = [lohi_ref[0, base + i] for i in range(nblk)]
            his = [lohi_ref[1, base + i] for i in range(nblk)]
            lo, hi = los[0], his[0]
            lo_lane = jnp.full((1, TILE), los[0])
            hi_lane = jnp.full((1, TILE), his[0])
            for i in range(1, nblk):
                lo = jnp.minimum(lo, los[i])
                hi = jnp.maximum(hi, his[i])
                lo_lane = jnp.where(lane < i * SBLK, lo_lane, los[i])
                hi_lane = jnp.where(lane < i * SBLK, hi_lane, his[i])
            first = jnp.maximum(lo, 0) // cblk
            last = (jnp.minimum(hi, keys // TBLK - 1) + cblk) // cblk
            r = pl.multiple_of(t * TILE, TILE)
            qg = q_ref[pl.ds(r, TILE), slot * 2 * HDIM : (slot + 1) * 2 * HDIM]
            zero = jnp.zeros_like(qg)
            rhs = jnp.concatenate(
                [jnp.where(rhs_lane < HDIM, qg, zero), jnp.where(rhs_lane < HDIM, zero, qg)], axis=0
            )

            def scores(c, m):
                k0 = pl.multiple_of(c * CHUNK, CHUNK)
                sd = lax.dot_general(
                    kv_ref[pl.ds(k0, CHUNK), :], rhs, NT, preferred_element_type=F32
                )
                d_ref[pl.ds(k0, CHUNK), :] = sd[:, TILE:]
                for b in range(cblk):
                    kb = c * cblk + b
                    ok = (lo_lane <= kb) & (hi_lane >= kb)
                    s = jnp.where(ok, sd[b * TBLK : (b + 1) * TBLK, :TILE], NEG)
                    s_ref[pl.ds(k0 + b * TBLK, TBLK), :] = s
                    m = jnp.maximum(m, jnp.max(s.reshape(TBLK // 8, 8, TILE), axis=0))
                return m

            m = lax.fori_loop(first, last, scores, jnp.full((8, TILE), NEG, F32))
            m = jnp.max(m, axis=0, keepdims=True)

            def expo(c, sums):
                l, dl = sums
                k0 = pl.multiple_of(c * CHUNK, CHUNK)
                p = jnp.exp(s_ref[pl.ds(k0, CHUNK), :] - m)
                s_ref[pl.ds(k0, CHUNK), :] = p
                l = l + jnp.sum(p.reshape(CHUNK // 8, 8, TILE), axis=0)
                pd = p * d_ref[pl.ds(k0, CHUNK), :]
                dl = dl + jnp.sum(pd.reshape(CHUNK // 8, 8, TILE), axis=0)
                return l, dl

            z8 = jnp.zeros((8, TILE), F32)
            l, dl = lax.fori_loop(first, last, expo, (z8, z8))
            l = jnp.sum(l, axis=0, keepdims=True)
            inv = 1.0 / jnp.maximum(l, 1e-30)
            delta = jnp.sum(dl, axis=0, keepdims=True) * inv

            def products(c, acc):
                k0 = pl.multiple_of(c * CHUNK, CHUNK)
                p = s_ref[pl.ds(k0, CHUNK), :]
                ds = p * (d_ref[pl.ds(k0, CHUNK), :] - delta)
                both = jnp.concatenate([p.astype(BF), ds.astype(BF)], axis=1)
                return acc + jnp.dot(
                    kvt_ref[:, pl.ds(k0, CHUNK)], both, preferred_element_type=F32
                )

            acc = lax.fori_loop(
                first, last, products, jnp.zeros((2 * HDIM, 2 * TILE), F32)
            )
            acc = acc * jnp.concatenate([inv, inv], axis=1)
            stats = jnp.where(row_id == 9, 1.0, 0.0)
            for i, piece in enumerate(split3(m) + split3(l) + split3(delta)):
                stats = jnp.where(row_id == i, piece, stats)
            right = jnp.concatenate([acc[:HDIM, TILE:], stats], axis=0)
            out = jnp.concatenate([acc[:, :TILE].T, right.T], axis=1)
            o_ref[pl.ds(r, TILE), :] = out.astype(o_ref.dtype)
            return carry

        lax.fori_loop(0, rows // TILE, tile, 0)


def attend(slot, lohi, qga, qgb, kv, kvt, out_dtype):
    rows = qga.shape[0]
    keys = kv.shape[0]
    vm = pl.BlockSpec(memory_space=pltpu.VMEM)
    return pl.pallas_call(
        functools.partial(attend_kernel, slot),
        in_specs=[pl.BlockSpec(memory_space=pltpu.SMEM)] + [vm] * 4,
        out_specs=[vm] * 2,
        out_shape=[jax.ShapeDtypeStruct((rows, 4 * HDIM), out_dtype)] * 2,
        scratch_shapes=[pltpu.VMEM((keys, TILE), F32), pltpu.VMEM((keys, TILE), F32)],
        compiler_params=params(),
        cost_estimate=cost(
            2 * rows * keys * 512, 4 * keys * 128 + 16 * rows * 256, rows * keys
        ),
    )(lohi, qga, qgb, kv, kvt)


def combine_kernel(groups, owna_ref, ownb_ref, rema_ref, remb_ref, cot_ref, oqa_ref, oqb_ref, pka_ref, pkb_ref, wg_ref):
    rows = owna_ref.shape[0]
    total = None
    for u, (own_ref, rem_ref, oq_ref, pk_ref) in enumerate(
        ((owna_ref, rema_ref, oqa_ref, pka_ref), (ownb_ref, remb_ref, oqb_ref, pkb_ref))
    ):
        own = own_ref[...]
        rem = rem_ref[...].astype(F32)

        def stat(x, i):
            c = 3 * HDIM + 3 * i
            return x[:, c : c + 1] + x[:, c + 1 : c + 2] + x[:, c + 2 : c + 3]

        flag = rem[:, 3 * HDIM + 9 : 3 * HDIM + 10]
        m_o, m_r = stat(own, 0), jnp.where(flag > 0.5, stat(rem, 0), NEG)
        l_o, l_r = stat(own, 1), stat(rem, 1)
        d_o, d_r = stat(own, 2), stat(rem, 2)
        top = jnp.maximum(m_o, m_r)
        w_o = l_o * jnp.exp(m_o - top)
        w_r = jnp.where(m_r > 0.5 * NEG, l_r * jnp.exp(m_r - top), 0.0)
        norm = 1.0 / (w_o + w_r)
        w_o, w_r = w_o * norm, w_r * norm
        delta = w_o * d_o + w_r * d_r
        attn = w_o * own[:, HDIM : 2 * HDIM] + w_r * rem[:, HDIM : 2 * HDIM]
        dq = w_o * (own[:, 2 * HDIM : 3 * HDIM] - (delta - d_o) * own[:, :HDIM])
        dq += w_r * (rem[:, 2 * HDIM : 3 * HDIM] - (delta - d_r) * rem[:, :HDIM])
        dq = dq * (1.0 / math.sqrt(HDIM))
        oq = jnp.concatenate([attn, dq], axis=1)
        oq_ref[...] = oq.astype(BF)
        attn = attn.astype(BF)
        pk_ref[...] = jnp.concatenate([attn[: rows // 2], attn[rows // 2 :]], axis=1)
        turned = oq.T[:HDIM].astype(BF)
        part = jnp.dot(
            turned, cot_ref[u * rows : (u + 1) * rows, :], preferred_element_type=F32
        )
        total = part if total is None else total + part
    total = total.astype(BF)
    step = total.shape[1] // groups
    for g in range(groups):
        wg_ref[g] = total[:, g * step : (g + 1) * step]


def combine(owna, ownb, rema, remb, cot_full, groups):
    rows = owna.shape[0]
    width = cot_full.shape[1]
    vm = pl.BlockSpec(memory_space=pltpu.VMEM)
    return pl.pallas_call(
        functools.partial(combine_kernel, groups),
        in_specs=[vm] * 5,
        out_specs=[vm] * 5,
        out_shape=[jax.ShapeDtypeStruct((rows, 2 * HDIM), BF)] * 2
        + [jax.ShapeDtypeStruct((rows // 2, 2 * HDIM), BF)] * 2
        + [jax.ShapeDtypeStruct((groups, HDIM, width // groups), BF)],
        compiler_params=params(),
        cost_estimate=cost(4 * rows * HDIM * width, 4 * rows * width + 24 * rows * 256),
    )(owna, ownb, rema, remb, cot_full)


def project_kernel(slots, place_ref, *refs):
    n = 8 * slots
    packed = refs[:n]
    mine = refs[n : n + 2 * slots]
    peer = refs[n + 2 * slots : n + 3 * slots]
    w_refs = refs[n + 3 * slots : n + 3 * slots + 4]
    joined_ref, gq_ref = refs[n + 3 * slots + 4 :]
    half = place_ref[0]
    first = half == 0
    own = [
        jnp.where(first, mine[2 * s][...], mine[2 * s + 1][...]) for s in range(slots)
    ]
    other = [peer[s][...] for s in range(slots)]

    def unpack(x):
        return jnp.concatenate([x[:, :HDIM], x[:, HDIM:]], axis=0)

    total = None
    for dc in range(4):
        if dc == 0:
            near = jnp.concatenate([x[:, :HDIM] for x in own], axis=1)
            far = jnp.concatenate([x[:, :HDIM] for x in other], axis=1)
        else:
            near = jnp.concatenate([unpack(packed[s * 8 + dc][...]) for s in range(slots)], axis=1)
            far = jnp.concatenate([unpack(packed[s * 8 + 4 + dc][...]) for s in range(slots)], axis=1)
        both = jnp.concatenate(
            [jnp.where(first, near, far), jnp.where(first, far, near)], axis=1
        )
        part = jnp.dot(both, w_refs[dc][...], preferred_element_type=F32)
        total = part if total is None else total + part
    joined_ref[...] = total.astype(BF)
    near = jnp.concatenate([x[:, HDIM:] for x in own], axis=1)
    far = jnp.concatenate([x[:, HDIM:] for x in other], axis=1)
    gq_ref[...] = jnp.concatenate(
        [jnp.where(first, near, far), jnp.where(first, far, near)], axis=1
    )


def project(place, packed, mine, peer, columns, slots):
    rows = mine[0].shape[0]
    cols = columns[0].shape[1]
    vm = pl.BlockSpec(memory_space=pltpu.VMEM)
    args = [*packed, *mine, *peer, *columns]
    return pl.pallas_call(
        functools.partial(project_kernel, slots),
        in_specs=[pl.BlockSpec(memory_space=pltpu.SMEM)] + [vm] * len(args),
        out_specs=[vm] * 2,
        out_shape=[jax.ShapeDtypeStruct((rows, cols), BF)] * 2,
        compiler_params=params(),
        cost_estimate=cost(2 * rows * cols * 4 * cols, 12 * rows * cols),
    )(place, *args)


def spread_kernel(slots, groups, place_ref, *refs):
    n = 2 * groups
    held = refs[: n * slots]
    out_ref, buf = refs[n * slots], refs[n * slots + 1]
    z, half = place_ref[2], place_ref[0]
    step = held[0].shape[1]
    for s in range(slots):
        for d in range(n):
            buf[s * n + d] = held[s * n + d][...].astype(F32)
    for s in range(slots):
        for y in range(2):
            row = (y * slots + s) * HDIM
            for g in range(groups):
                d = ((g ^ z) * 2) + (y ^ half)
                out_ref[row : row + HDIM, g * step : (g + 1) * step] = buf[s * n + d]


def spread(place, held, slots, groups):
    step = held[0].shape[1]
    vm = pl.BlockSpec(memory_space=pltpu.VMEM)
    return pl.pallas_call(
        functools.partial(spread_kernel, slots, groups),
        in_specs=[pl.BlockSpec(memory_space=pltpu.SMEM)] + [vm] * len(held),
        out_specs=vm,
        out_shape=jax.ShapeDtypeStruct((2 * slots * HDIM, groups * step), F32),
        scratch_shapes=[pltpu.VMEM((2 * groups * slots, HDIM, step), F32)],
        compiler_params=params(),
        cost_estimate=cost(0, len(held) * HDIM * step * 6),
    )(place, *held)


def on_device(
    groups,
    student_query,
    teacher_key,
    teacher_value,
    clip_order,
    band_start,
    band_end,
    output_weight,
    cotangent,
):
    shards = 2 * groups
    me = lax.axis_index("tm")
    clip = lax.axis_index("clip")
    half = me % 2
    z = me // 2
    place = jnp.stack([half, clip, z]).astype(jnp.int32)
    clips = lax.axis_size("clip")
    teacher_rows = teacher_key.shape[0]
    rows, feats = student_query.shape
    piece = teacher_rows // shards
    slots = feats // HDIM // 2
    hw = slots * HDIM

    def swap(x, d):
        return lax.ppermute(x, "tm", [(i, i ^ d) for i in range(shards)])

    def swap_clip(x, d):
        return lax.ppermute(x, "clip", [(i, i ^ d) for i in range(clips)])

    def swap_near(x, dy, dc):
        if dy == 0:
            return swap_clip(x, dc)
        if dc == 0:
            return swap(x, 1)
        n = shards * clips
        return lax.ppermute(
            x, ("tm", "clip"), [(i, i ^ (dy * clips + dc)) for i in range(n)]
        )

    def up(x):
        return lax.ppermute(x, "tm", [(i, i + 2) for i in range(shards - 2)])

    def down(x):
        return lax.ppermute(x, "tm", [(i + 2, i) for i in range(shards - 2)])

    sent = pack(teacher_key, teacher_value, groups, slots)

    qpeer = swap(
        jnp.where(half == 0, student_query[:, hw:], student_query[:, :hw]), 1
    )
    pieces = [
        cotangent if dy == dc == 0 else swap_near(cotangent, dy, dc)
        for dy in range(2)
        for dc in range(4)
    ]
    cot_full, qga, qgb = student_side(place, pieces, output_weight, student_query, qpeer, slots)
    qg_left, qg_right = up(qgb), down(qga)

    band = jnp.stack([band_start, band_end])
    blocks = band.shape[1]
    peer_band = swap(band, 1)
    band_a = jnp.where(half == 0, band, peer_band)
    band_b = jnp.where(half == 0, peer_band, band)
    band_l, band_r = up(band_b), down(band_a)
    total_blocks = shards * blocks
    origin = z * 2 * blocks

    def limits(bands, start):
        b = origin + start + jnp.arange(2 * blocks, dtype=jnp.int32) % blocks
        b = b + jnp.where(jnp.arange(2 * blocks) < blocks, 0, 1) * (bands[2] - start)
        both = jnp.concatenate(bands[:2], axis=1)
        lo = jnp.maximum(b + both[0], 0) - origin
        hi = jnp.minimum(b + both[1], total_blocks - 1) - origin
        return jnp.stack([lo, hi]).astype(jnp.int32)

    own_lim = limits((band_a, band_b, blocks), 0)
    halo_lim = limits((band_l, band_r, 2 * blocks), -blocks)

    def columns_for(d):
        c = (clip ^ d) * feats
        return lax.dynamic_slice_in_dim(output_weight, c, feats, axis=1)

    columns = [columns_for(0)] + [swap_clip(columns_for(d), d) for d in range(1, clips)]

    lookup = lax.dynamic_slice_in_dim(clip_order, z * 2 * teacher_rows, 2 * teacher_rows)
    index = lookup // teacher_rows * piece + lookup % piece

    packed, mine, peer, held = [], [], [], []
    for s in range(slots):
        arrived = lax.all_to_all(
            sent[s].reshape(shards, 2 * piece, 2 * HDIM), "tm", 0, 0
        )
        kv, kvt = put_in_order(arrived, index, teacher_rows)
        far_l, far_r = attend(s, halo_lim, qg_left, qg_right, kv, kvt, BF)
        rema, remb = up(far_r), down(far_l)
        owna, ownb = attend(s, own_lim, qga, qgb, kv, kvt, F32)
        oqa, oqb, pka, pkb, wg = combine(owna, ownb, rema, remb, cot_full, groups)
        mine += [oqa, oqb]
        peer.append(swap(jnp.where(half == 0, oqb, oqa), 1))
        keep = jnp.where(half == 0, pka, pkb)
        give = jnp.where(half == 0, pkb, pka)
        packed += [keep] + [swap_near(keep, 0, dc) for dc in range(1, 4)]
        packed += [give] + [swap_near(give, 1, dc) for dc in range(1, 4)]
        got = [lax.dynamic_index_in_dim(wg, z, 0, False).astype(F32)]
        for d in range(1, groups):
            got.append(swap(lax.dynamic_index_in_dim(wg, z ^ d, 0, False), 2 * d).astype(F32))
        summed = sum(got[1:], got[0]).astype(BF)
        held += [summed] + [swap(summed, d) for d in range(1, shards)]
    joined, grad_query = project(place, packed, mine, peer, columns, slots)
    weight_grad = spread(place, held, slots, groups)
    return joined, grad_query, weight_grad


def solution(mesh):
    return jax.shard_map(
        functools.partial(on_device, mesh.shape["tm"] // 2),
        mesh=mesh,
        in_specs=(
            P("tm", "clip"),
            P("tm", "clip"),
            P("tm", "clip"),
            P(),
            P("tm"),
            P("tm"),
            P("clip", None),
            P("tm", "clip"),
        ),
        out_specs=(P("tm", "clip"), P("tm", "clip"), P("clip", None)),
        check_vma=False,
    )
```

```python
import functools
import math

import jax
import jax.numpy as jnp
from jax import lax
from jax.experimental import pallas as pl
from jax.experimental.pallas import tpu as pltpu
from jax.sharding import PartitionSpec as P

HDIM = 64
SBLK = 32
TBLK = 128
TILE = 128
CHUNK = 1024
NEG = -1e30
STATS = 16
BF = jnp.bfloat16
F32 = jnp.float32
NT = (((1,), (1,)), ((), ()))
NEAR = ((0, 0), (1, 0), (0, 2), (1, 2), (0, 1), (1, 1), (0, 3), (1, 3))
VMEM_LIMIT = 48 * 1024 * 1024


def params(*semantics):
    return pltpu.CompilerParams(
        dimension_semantics=semantics or None, vmem_limit_bytes=VMEM_LIMIT
    )


def cost(flops, nbytes, trans=0):
    return pl.CostEstimate(flops=flops, bytes_accessed=nbytes, transcendentals=trans)


def pack_kernel(slots, slot, k_ref, v_ref, *refs):
    out = refs[-1]
    for half in range(2):
        c = (half * slots + slot) * HDIM
        out[0, half] = jnp.concatenate([k_ref[:, c : c + HDIM], v_ref[:, c : c + HDIM]], axis=1)


def pack(keys, values, groups, slots, slot, *after):
    rows, feats = keys.shape
    part = rows // groups
    block = pl.BlockSpec((part, feats), lambda i: (i, 0))
    return pl.pallas_call(
        functools.partial(pack_kernel, slots, slot),
        grid=(groups,),
        in_specs=[block, block] + [pl.BlockSpec(memory_space=pl.ANY)] * len(after),
        out_specs=pl.BlockSpec((1, 2, part, 2 * HDIM), lambda i: (i, 0, 0, 0)),
        out_shape=jax.ShapeDtypeStruct((groups, 2, part, 2 * HDIM), BF),
        compiler_params=params("arbitrary"),
        cost_estimate=cost(0, 3 * rows * feats * 2),
    )(keys, values, *after)


def order_kernel(idx_ref, arr_ref, kv_ref, kvt_ref, arrt, hot):
    rows = arrt.shape[1]
    arr = arr_ref[...].reshape(rows, 2 * HDIM)
    for j in range(0, rows, 256):
        arrt[:, j : j + 256] = arr[j : j + 256].T
    idx = idx_ref[0]
    iota = lax.broadcasted_iota(jnp.int32, (256, rows), 0).astype(F32).astype(BF)
    for j in range(0, rows, 256):
        near = idx - j
        near = jnp.where((near >= 0) & (near < 256), near, -1).astype(F32).astype(BF)
        hot[j : j + 256] = jnp.where(iota == near, BF(1), BF(0))
    acc = jnp.dot(arrt[...], hot[...], preferred_element_type=F32)
    kvt_ref[...] = acc.astype(BF)
    kv_ref[...] = acc.T.astype(BF)


def put_in_order(arrived, index, rows):
    sources, twice, width = arrived.shape
    return pl.pallas_call(
        order_kernel,
        grid=(2,),
        in_specs=[
            pl.BlockSpec((1, 1, rows), lambda u: (u, 0, 0)),
            pl.BlockSpec((sources, twice // 2, width), lambda u: (0, u, 0)),
        ],
        out_specs=[
            pl.BlockSpec((rows, width), lambda u: (u, 0)),
            pl.BlockSpec((width, rows), lambda u: (0, u)),
        ],
        out_shape=[
            jax.ShapeDtypeStruct((2 * rows, width), BF),
            jax.ShapeDtypeStruct((width, 2 * rows), BF),
        ],
        scratch_shapes=[pltpu.VMEM((width, rows), BF), pltpu.VMEM((rows, rows), BF)],
        compiler_params=params("arbitrary"),
        cost_estimate=cost(4 * rows * rows * width, 6 * rows * width * 2),
    )(index.reshape(2, 1, rows), arrived)


def student_kernel(slots, place_ref, *refs):
    parts_ref = refs[:2]
    w_ref, qmine_ref, qpeer_ref, full_ref, qga_ref, qgb_ref = refs[2:]
    half, clip = place_ref[0], place_ref[1]
    rows, cols = qmine_ref.shape
    hw = slots * HDIM
    for i, (dy, dc) in enumerate(NEAR):
        r = pl.multiple_of((half ^ dy) * rows, rows)
        c = pl.multiple_of((clip ^ dc) * cols, cols)
        full_ref[pl.ds(r, rows), pl.ds(c, cols)] = parts_ref[i // 4][i % 4]
    w = w_ref[pl.ds(pl.multiple_of(half * hw, hw), hw), :]
    qmine = qmine_ref[...]
    qown = jnp.where(half == 0, qmine[:, :hw], qmine[:, hw:])
    qpeer = qpeer_ref[...]
    for u, out in enumerate((qga_ref, qgb_ref)):
        g = lax.dot_general(
            full_ref[u * rows : (u + 1) * rows, :], w, NT, preferred_element_type=F32
        ).astype(BF)
        q = jnp.where(half == u, qown, qpeer) * BF(1.0 / math.sqrt(HDIM))
        parts = []
        for s in range(slots):
            parts += [q[:, s * HDIM : (s + 1) * HDIM], g[:, s * HDIM : (s + 1) * HDIM]]
        out[...] = jnp.concatenate(parts, axis=1)


def student_side(place, parts, weight, qmine, qpeer, slots):
    rows, cols = qmine.shape
    width = 4 * cols
    vm = pl.BlockSpec(memory_space=pltpu.VMEM)
    return pl.pallas_call(
        functools.partial(student_kernel, slots),
        in_specs=[pl.BlockSpec(memory_space=pltpu.SMEM)] + [vm] * 5,
        out_specs=[vm] * 3,
        out_shape=[
            jax.ShapeDtypeStruct((2 * rows, width), BF),
            jax.ShapeDtypeStruct((rows, 2 * slots * HDIM), BF),
            jax.ShapeDtypeStruct((rows, 2 * slots * HDIM), BF),
        ],
        compiler_params=params(),
        cost_estimate=cost(4 * rows * width * slots * HDIM, 10 * rows * width),
    )(place, *parts, weight, qmine, qpeer)


def split3(x):
    a = x.astype(BF).astype(F32)
    b = (x - a).astype(BF).astype(F32)
    c = (x - a - b).astype(BF).astype(F32)
    return [a, b, c]


def attend_kernel(slot, tiles, bases, lohi_ref, qga_ref, qgb_ref, kv_ref, kvt_ref, outa_ref, outb_ref, *scratch):
    s_refs, d_refs = scratch[:tiles], scratch[tiles:]
    rows = qga_ref.shape[0]
    blocks = kv_ref.shape[0] // TBLK
    nblk = TILE // SBLK
    cblk = CHUNK // TBLK
    lane = lax.broadcasted_iota(jnp.int32, (1, TILE), 1)
    rhs_lane = lax.broadcasted_iota(jnp.int32, (TILE, 2 * HDIM), 1)
    row_id = lax.broadcasted_iota(jnp.int32, (STATS, TILE), 0)
    z8 = jnp.zeros((8, TILE), F32)
    for u, (q_ref, o_ref) in enumerate(((qga_ref, outa_ref), (qgb_ref, outb_ref))):

        def group(g, carry):
            held = []
            n = jnp.int32(0)
            for k in range(tiles):
                t = g * tiles + k
                base = bases[u] + t * nblk
                los = [lohi_ref[0, base + i] for i in range(nblk)]
                his = [lohi_ref[1, base + i] for i in range(nblk)]
                lo, hi = los[0], his[0]
                lo_lane = jnp.full((1, TILE), los[0])
                hi_lane = jnp.full((1, TILE), his[0])
                for i in range(1, nblk):
                    lo = jnp.minimum(lo, los[i])
                    hi = jnp.maximum(hi, his[i])
                    lo_lane = jnp.where(lane < i * SBLK, lo_lane, los[i])
                    hi_lane = jnp.where(lane < i * SBLK, hi_lane, his[i])
                lo = jnp.maximum(lo, 0)
                hi = jnp.minimum(hi, blocks - 1)
                n = jnp.maximum(n, jnp.maximum(hi - lo + cblk, 0) // cblk)
                r = pl.multiple_of(t * TILE, TILE)
                qg = q_ref[pl.ds(r, TILE), slot * 2 * HDIM : (slot + 1) * 2 * HDIM]
                zero = jnp.zeros_like(qg)
                rhs = jnp.concatenate(
                    [
                        jnp.where(rhs_lane < HDIM, qg, zero),
                        jnp.where(rhs_lane < HDIM, zero, qg),
                    ],
                    axis=0,
                )
                held.append((lo, lo_lane, hi_lane, rhs, r))

            def start(i, lo):
                kb = jnp.minimum(lo + i * cblk, blocks - cblk)
                return kb, pl.multiple_of(kb * TBLK, TBLK)

            def scores(i, tops):
                s0 = pl.multiple_of(i * CHUNK, CHUNK)
                new = []
                for k, (lo, lo_lane, hi_lane, rhs, _) in enumerate(held):
                    kb0, k0 = start(i, lo)
                    low = jnp.maximum(lo_lane, lo + i * cblk)
                    sd = lax.dot_general(
                        kv_ref[pl.ds(k0, CHUNK), :], rhs, NT, preferred_element_type=F32
                    )
                    d_refs[k][pl.ds(s0, CHUNK), :] = sd[:, TILE:]
                    m = tops[k]
                    for b in range(cblk):
                        ok = (low <= kb0 + b) & (hi_lane >= kb0 + b)
                        s = jnp.where(ok, sd[b * TBLK : (b + 1) * TBLK, :TILE], NEG)
                        s_refs[k][pl.ds(s0 + b * TBLK, TBLK), :] = s
                        m = jnp.maximum(m, jnp.max(s.reshape(TBLK // 8, 8, TILE), axis=0))
                    new.append(m)
                return tuple(new)

            tops = lax.fori_loop(
                0, n, scores, tuple(jnp.full((8, TILE), NEG, F32) for _ in range(tiles))
            )
            tops = [jnp.max(m, axis=0, keepdims=True) for m in tops]

            def expo(i, sums):
                s0 = pl.multiple_of(i * CHUNK, CHUNK)
                new = []
                for k in range(tiles):
                    l, dl = sums[k]
                    p = jnp.exp(s_refs[k][pl.ds(s0, CHUNK), :] - tops[k])
                    s_refs[k][pl.ds(s0, CHUNK), :] = p
                    l = l + jnp.sum(p.reshape(CHUNK // 8, 8, TILE), axis=0)
                    pd = p * d_refs[k][pl.ds(s0, CHUNK), :]
                    dl = dl + jnp.sum(pd.reshape(CHUNK // 8, 8, TILE), axis=0)
                    new.append((l, dl))
                return tuple(new)

            ends = []
            for l, dl in lax.fori_loop(0, n, expo, ((z8, z8),) * tiles):
                l = jnp.sum(l, axis=0, keepdims=True)
                inv = 1.0 / jnp.maximum(l, 1e-30)
                ends.append((l, inv, jnp.sum(dl, axis=0, keepdims=True) * inv))

            def products(i, accs):
                s0 = pl.multiple_of(i * CHUNK, CHUNK)
                new = []
                for k in range(tiles):
                    _, k0 = start(i, held[k][0])
                    p = s_refs[k][pl.ds(s0, CHUNK), :]
                    ds = p * (d_refs[k][pl.ds(s0, CHUNK), :] - ends[k][2])
                    both = jnp.concatenate([p.astype(BF), ds.astype(BF)], axis=1)
                    new.append(
                        accs[k]
                        + jnp.dot(
                            kvt_ref[:, pl.ds(k0, CHUNK)], both, preferred_element_type=F32
                        )
                    )
                return tuple(new)

            accs = lax.fori_loop(
                0, n, products, tuple(jnp.zeros((2 * HDIM, 2 * TILE), F32) for _ in range(tiles))
            )
            for k in range(tiles):
                l, inv, delta = ends[k]
                acc = accs[k] * jnp.concatenate([inv, inv], axis=1)
                stats = jnp.where(row_id == 9, 1.0, 0.0)
                for i, piece in enumerate(split3(tops[k]) + split3(l) + split3(delta)):
                    stats = jnp.where(row_id == i, piece, stats)
                out = jnp.concatenate([acc[:, :TILE], acc[:HDIM, TILE:], stats], axis=0)
                o_ref[:, pl.ds(held[k][4], TILE)] = out.astype(o_ref.dtype)
            return carry

        lax.fori_loop(0, rows // (TILE * tiles), group, 0)


def attend(slot, tiles, bases, lohi, qga, qgb, kv, kvt, out_dtype):
    rows = qga.shape[0]
    keys = kv.shape[0]
    vm = pl.BlockSpec(memory_space=pltpu.VMEM)
    return pl.pallas_call(
        functools.partial(attend_kernel, slot, tiles, bases),
        in_specs=[pl.BlockSpec(memory_space=pltpu.SMEM)] + [vm] * 4,
        out_specs=[vm] * 2,
        out_shape=[jax.ShapeDtypeStruct((3 * HDIM + STATS, rows), out_dtype)] * 2,
        scratch_shapes=[pltpu.VMEM((keys, TILE), F32)] * (2 * tiles),
        compiler_params=params(),
        cost_estimate=cost(
            2 * rows * keys * 512, 4 * keys * 128 + 16 * rows * 256, rows * keys
        ),
    )(lohi, qga, qgb, kv, kvt)


def combine_kernel(groups, last, earlier, place_ref, owna_ref, ownb_ref, rema_ref, remb_ref, cot_ref, *refs):
    before = refs[: 3 * earlier]
    refs = refs[3 * earlier :]
    rows = owna_ref.shape[1]
    total = None
    both = []
    for u, (own_ref, rem_ref) in enumerate(((owna_ref, rema_ref), (ownb_ref, remb_ref))):
        own = own_ref[...]
        rem = rem_ref[...].astype(F32)

        def stat(x, i):
            r = 3 * HDIM + 3 * i
            return x[r : r + 1] + x[r + 1 : r + 2] + x[r + 2 : r + 3]

        flag = rem[3 * HDIM + 9 : 3 * HDIM + 10]
        m_o, m_r = stat(own, 0), jnp.where(flag > 0.5, stat(rem, 0), NEG)
        l_o, l_r = stat(own, 1), stat(rem, 1)
        d_o, d_r = stat(own, 2), stat(rem, 2)
        top = jnp.maximum(m_o, m_r)
        w_o = l_o * jnp.exp(m_o - top)
        w_r = jnp.where(m_r > 0.5 * NEG, l_r * jnp.exp(m_r - top), 0.0)
        norm = 1.0 / (w_o + w_r)
        w_o, w_r = w_o * norm, w_r * norm
        delta = w_o * d_o + w_r * d_r
        attn = w_o * own[HDIM : 2 * HDIM] + w_r * rem[HDIM : 2 * HDIM]
        scale = 1.0 / math.sqrt(HDIM)
        s_o, s_r = scale * w_o, scale * w_r
        dq = s_o * own[2 * HDIM : 3 * HDIM] - (s_o * (delta - d_o)) * own[:HDIM]
        dq += s_r * rem[2 * HDIM : 3 * HDIM] - (s_r * (delta - d_r)) * rem[:HDIM]
        both.append(jnp.concatenate([attn, dq], axis=0).T.astype(BF))
        part = jnp.dot(
            attn.astype(BF), cot_ref[u * rows : (u + 1) * rows, :], preferred_element_type=F32
        )
        total = part if total is None else total + part
    first = place_ref[0] == 0
    keep = jnp.where(first, both[0], both[1])
    give = jnp.where(first, both[1], both[0])
    total = total.astype(BF)
    if not last:
        refs[0][...], refs[1][...], refs[2][...] = keep, give, total
        return
    near = [r[...] for r in before[::3]] + [keep]
    far = [r[...] for r in before[1::3]] + [give]
    refs[0][...] = jnp.concatenate(near, axis=1)
    refs[1][...] = jnp.concatenate(far, axis=1)
    refs[2][...] = jnp.concatenate([x[:, :HDIM] for x in near], axis=1)
    refs[3][...] = jnp.concatenate([x[:, :HDIM] for x in far], axis=1)
    buf = refs[4 + groups]
    step = total.shape[1] // groups
    for g in range(groups):
        for s in range(earlier):
            buf[g, s * HDIM : (s + 1) * HDIM] = before[3 * s + 2][:, g * step : (g + 1) * step]
        buf[g, earlier * HDIM :] = total[:, g * step : (g + 1) * step]
    for d in range(groups):
        refs[4 + d][...] = buf[place_ref[2] ^ d]


def combine(place, owna, ownb, rema, remb, cot_full, groups, before, last):
    rows = owna.shape[1]
    width = cot_full.shape[1]
    earlier = len(before) // 3
    heads = earlier + 1
    vm = pl.BlockSpec(memory_space=pltpu.VMEM)
    if last:
        shapes = [(rows, 2 * heads * HDIM)] * 2 + [(rows, heads * HDIM)] * 2
        shapes += [(heads * HDIM, width // groups)] * groups
        scratch = [pltpu.VMEM((groups, heads * HDIM, width // groups), BF)]
    else:
        shapes = [(rows, 2 * HDIM)] * 2 + [(HDIM, width)]
        scratch = []
    return pl.pallas_call(
        functools.partial(combine_kernel, groups, last, earlier),
        in_specs=[pl.BlockSpec(memory_space=pltpu.SMEM)] + [vm] * (5 + len(before)),
        out_specs=[vm] * len(shapes),
        out_shape=[jax.ShapeDtypeStruct(s, BF) for s in shapes],
        scratch_shapes=scratch,
        compiler_params=params(),
        cost_estimate=cost(4 * rows * HDIM * width, 4 * rows * width + 24 * rows * 256),
    )(place, owna, ownb, rema, remb, cot_full, *before)


def heads_kernel(place_ref, mine_ref, peer_ref, xmine_ref, xpeer_ref, x_ref, gq_ref):
    first = place_ref[0] == 0
    width = gq_ref.shape[1]

    def put(near, far):
        return jnp.concatenate(
            [jnp.where(first, near, far), jnp.where(first, far, near)], axis=1
        )

    def every_other(ref, lo):
        cols = [ref[:, c : c + HDIM] for c in range(lo, width, 2 * HDIM)]
        return jnp.concatenate(cols, axis=1)

    x_ref[:, :width] = put(every_other(mine_ref, 0), every_other(peer_ref, 0))
    x_ref[:, width:] = put(xmine_ref[...], xpeer_ref[...])
    gq_ref[...] = put(every_other(mine_ref, HDIM), every_other(peer_ref, HDIM))


def heads(place, mine, peer, xmine, xpeer):
    rows, width = mine.shape
    vm = pl.BlockSpec(memory_space=pltpu.VMEM)
    return pl.pallas_call(
        heads_kernel,
        in_specs=[pl.BlockSpec(memory_space=pltpu.SMEM)] + [vm] * 4,
        out_specs=[vm] * 2,
        out_shape=[
            jax.ShapeDtypeStruct((rows, 2 * width), BF),
            jax.ShapeDtypeStruct((rows, width), BF),
        ],
        compiler_params=params(),
        cost_estimate=cost(0, 12 * rows * width),
    )(place, mine, peer, xmine, xpeer)


def project_kernel(here_ref, there_ref, *refs):
    columns, out_ref = refs[:-1], refs[-1]
    cols = columns[0].shape[0]
    total = None
    for i, w in enumerate(columns):
        ref = (here_ref, there_ref)[i % 2]
        c = i // 2 * cols
        part = jnp.dot(ref[:, c : c + cols], w[...], preferred_element_type=F32)
        total = part if total is None else total + part
    out_ref[...] = total.astype(BF)


def project(here, there, columns):
    rows, cols = here.shape[0], columns[0].shape[1]
    vm = pl.BlockSpec(memory_space=pltpu.VMEM)
    return pl.pallas_call(
        project_kernel,
        in_specs=[vm] * (2 + len(columns)),
        out_specs=vm,
        out_shape=jax.ShapeDtypeStruct((rows, cols), BF),
        compiler_params=params(),
        cost_estimate=cost(2 * rows * cols * 4 * cols, 12 * rows * cols),
    )(here, there, *columns)


def spread_kernel(groups, place_ref, *refs):
    held, out_ref, buf = refs[: 2 * groups], refs[2 * groups], refs[2 * groups + 1]
    rows, step = held[0].shape
    for d, ref in enumerate(held):
        buf[d] = ref[...].astype(F32)
    for y in range(2):
        for g in range(groups):
            d = 2 * (g ^ place_ref[2]) + (y ^ place_ref[0])
            out_ref[y * rows : (y + 1) * rows, g * step : (g + 1) * step] = buf[d]


def spread(place, held):
    groups = len(held) // 2
    rows, step = held[0].shape
    vm = pl.BlockSpec(memory_space=pltpu.VMEM)
    return pl.pallas_call(
        functools.partial(spread_kernel, groups),
        in_specs=[pl.BlockSpec(memory_space=pltpu.SMEM)] + [vm] * len(held),
        out_specs=vm,
        out_shape=jax.ShapeDtypeStruct((2 * rows, groups * step), F32),
        scratch_shapes=[pltpu.VMEM((2 * groups, rows, step), F32)],
        compiler_params=params(),
        cost_estimate=cost(0, 2 * groups * rows * step * 6),
    )(place, *held)


def on_device(
    groups,
    student_query,
    teacher_key,
    teacher_value,
    clip_order,
    band_start,
    band_end,
    output_weight,
    cotangent,
):
    shards = 2 * groups
    me = lax.axis_index("tm")
    clip = lax.axis_index("clip")
    half = me % 2
    z = me // 2
    place = jnp.stack([half, clip, z]).astype(jnp.int32)
    clips = lax.axis_size("clip")
    teacher_rows = teacher_key.shape[0]
    rows, feats = student_query.shape
    piece = teacher_rows // shards
    slots = feats // HDIM // 2
    hw = slots * HDIM

    def swap(x, d):
        return lax.ppermute(x, "tm", [(i, i ^ d) for i in range(shards)])

    def swap_clip(x, d):
        return lax.ppermute(x, "clip", [(i, i ^ d) for i in range(clips)])

    def swap_both(x, d):
        n = shards * clips
        return lax.ppermute(x, ("tm", "clip"), [(i, i ^ (clips + d)) for i in range(n)])

    def up(x):
        return lax.ppermute(x, "tm", [(i, i + 2) for i in range(shards - 2)])

    def down(x):
        return lax.ppermute(x, "tm", [(i + 2, i) for i in range(shards - 2)])

    sent = [pack(teacher_key, teacher_value, groups, slots, 0)]

    qpeer = swap(
        jnp.where(half == 0, student_query[:, hw:], student_query[:, :hw]), 1
    )
    near = jnp.stack([cotangent, swap(cotangent, 1)])
    near = jnp.concatenate([near, swap_clip(near, 2)])
    parts = (near, swap_clip(near, 1))
    cot_full, qga, qgb = student_side(place, parts, output_weight, student_query, qpeer, slots)
    qg_left, qg_right = up(qgb), down(qga)

    band = jnp.stack([band_start, band_end])
    blocks = band.shape[1]
    peer_band = swap(band, 1)
    band_a = jnp.where(half == 0, band, peer_band)
    band_b = jnp.where(half == 0, peer_band, band)
    bands = jnp.concatenate([up(band_b), band_a, band_b, down(band_a)], axis=1)
    origin = z * 2 * blocks
    frame = origin - blocks + jnp.arange(4 * blocks, dtype=jnp.int32)
    lohi = jnp.stack(
        [
            jnp.maximum(frame + bands[0], 0) - origin,
            jnp.minimum(frame + bands[1], shards * blocks - 1) - origin,
        ]
    ).astype(jnp.int32)

    sent += [
        pack(teacher_key, teacher_value, groups, slots, s, near, lohi)
        for s in range(1, slots)
    ]

    def columns_for(d):
        c = (clip ^ d) * feats
        return lax.dynamic_slice_in_dim(output_weight, c, feats, axis=1)

    columns = [columns_for(0)] + [swap_clip(columns_for(d), d) for d in range(1, clips)]

    lookup = lax.dynamic_slice_in_dim(clip_order, z * 2 * teacher_rows, 2 * teacher_rows)
    index = lookup // teacher_rows * piece + lookup % piece

    parts = []
    for s in range(slots):
        arrived = lax.all_to_all(
            sent[s].reshape(shards, 2 * piece, 2 * HDIM), "tm", 0, 0
        )
        kv, kvt = put_in_order(arrived, index, teacher_rows)
        far_l, far_r = attend(s, 2, (0, 3 * blocks), lohi, qg_left, qg_right, kv, kvt, BF)
        rema, remb = up(far_r), down(far_l)
        owna, ownb = attend(s, 4, (blocks, 2 * blocks), lohi, qga, qgb, kv, kvt, F32)
        parts += combine(
            place, owna, ownb, rema, remb, cot_full, groups, parts, s == slots - 1
        )
    mine, give, xmine, xgive, *got = parts[3 * (slots - 1) :]
    total = got[0].astype(F32)
    for d in range(1, groups):
        total += swap(got[d], 2 * d).astype(F32)
    total = total.astype(BF)
    held = [total] + [swap(total, d) for d in range(1, shards)]
    here, grad_query = heads(
        place, mine, swap(give, 1), swap_clip(xmine, 2), swap_both(xgive, 2)
    )
    joined = project(here, swap_clip(here, 1), columns)
    return joined, grad_query, spread(place, held)


def solution(mesh):
    return jax.shard_map(
        functools.partial(on_device, mesh.shape["tm"] // 2),
        mesh=mesh,
        in_specs=(
            P("tm", "clip"),
            P("tm", "clip"),
            P("tm", "clip"),
            P(),
            P("tm"),
            P("tm"),
            P("clip", None),
            P("tm", "clip"),
        ),
        out_specs=(P("tm", "clip"), P("tm", "clip"), P("clip", None)),
        check_vma=False,
    )
```

```python
import functools
import itertools
import math

import jax
import jax.numpy as jnp
from jax import lax
from jax.experimental import pallas as pl
from jax.experimental.pallas import tpu as pltpu
from jax.sharding import PartitionSpec as P

HDIM = 64
SBLK = 32
TBLK = 128
TILE = 128
CHUNK = 1024
NEG = -1e30
STATS = 16
OUT = 3 * HDIM + STATS
BF = jnp.bfloat16
F32 = jnp.float32
NT = (((1,), (1,)), ((), ()))
CLIPS = (0, 2, 1, 3)
VMEM_LIMIT = 48 * 1024 * 1024


def params(*semantics):
    return pltpu.CompilerParams(
        dimension_semantics=semantics or None, vmem_limit_bytes=VMEM_LIMIT
    )


def cost(flops, nbytes, trans=0):
    return pl.CostEstimate(flops=flops, bytes_accessed=nbytes, transcendentals=trans)


def pack_kernel(slots, slot, k_ref, v_ref, *refs):
    out = refs[-1]
    for half in range(2):
        c = (half * slots + slot) * HDIM
        out[0, half] = jnp.concatenate([k_ref[:, c : c + HDIM], v_ref[:, c : c + HDIM]], axis=1)


def pack(keys, values, groups, slots, slot, *after):
    rows, feats = keys.shape
    part = rows // groups
    block = pl.BlockSpec((part, feats), lambda i: (i, 0))
    return pl.pallas_call(
        functools.partial(pack_kernel, slots, slot),
        grid=(groups,),
        in_specs=[block, block] + [pl.BlockSpec(memory_space=pl.ANY)] * len(after),
        out_specs=pl.BlockSpec((1, 2, part, 2 * HDIM), lambda i: (i, 0, 0, 0)),
        out_shape=jax.ShapeDtypeStruct((groups, 2, part, 2 * HDIM), BF),
        compiler_params=params("arbitrary"),
        cost_estimate=cost(0, 3 * rows * feats * 2),
    )(keys, values, *after)


def order_kernel(idx_ref, arr_ref, *refs):
    kv_ref, kvt_ref, arrt, hot = refs[-4:]
    rows = arrt.shape[1]
    arr = arr_ref[...].reshape(rows, arrt.shape[0])
    for j in range(0, rows, 256):
        arrt[:, j : j + 256] = arr[j : j + 256].T
    idx = idx_ref[0]
    iota = lax.broadcasted_iota(jnp.int32, (256, rows), 0).astype(F32).astype(BF)
    for j in range(0, rows, 256):
        near = idx - j
        near = jnp.where((near >= 0) & (near < 256), near, -1).astype(F32).astype(BF)
        hot[j : j + 256] = jnp.where(iota == near, BF(1), BF(0))
    acc = jnp.dot(arrt[...], hot[...], preferred_element_type=F32)
    kvt_ref[...] = acc.astype(BF)
    kv_ref[...] = acc.T.astype(BF)


def put_in_order(arrived, index, rows, *after):
    sources, twice, width = arrived.shape
    return pl.pallas_call(
        order_kernel,
        grid=(2,),
        in_specs=[
            pl.BlockSpec((1, 1, rows), lambda u: (u, 0, 0)),
            pl.BlockSpec((sources, twice // 2, width), lambda u: (0, u, 0)),
        ]
        + [pl.BlockSpec(memory_space=pl.ANY)] * len(after),
        out_specs=[
            pl.BlockSpec((rows, width), lambda u: (u, 0)),
            pl.BlockSpec((width, rows), lambda u: (0, u)),
        ],
        out_shape=[
            jax.ShapeDtypeStruct((2 * rows, width), BF),
            jax.ShapeDtypeStruct((width, 2 * rows), BF),
        ],
        scratch_shapes=[pltpu.VMEM((width, rows), BF), pltpu.VMEM((rows, rows), BF)],
        compiler_params=params("arbitrary"),
        cost_estimate=cost(4 * rows * rows * width, 6 * rows * width * 2),
    )(index.reshape(2, 1, rows), arrived, *after)


def student_kernel(slots, place_ref, here_ref, there_ref, w_ref, q_ref, band_ref, mine_ref, give_ref):
    rows, feats = q_ref.shape
    half, clip = place_ref[0], place_ref[1]
    total = None
    for i, ref in enumerate((here_ref, here_ref, there_ref, there_ref)):
        c = pl.multiple_of((clip ^ CLIPS[i]) * feats, feats)
        part = lax.dot_general(
            ref[i % 2], w_ref[:, pl.ds(c, feats)], NT, preferred_element_type=F32
        )
        total = part if total is None else total + part
    g = total.astype(BF)
    q = q_ref[...] * BF(1.0 / math.sqrt(HDIM))
    heads = []
    for y in range(2):
        cols = []
        for s in range(slots):
            c = (y * slots + s) * HDIM
            cols += [q[:, c : c + HDIM], g[:, c : c + HDIM]]
        heads.append(jnp.concatenate(cols, axis=1))
    mine_ref[:rows] = jnp.where(half == 0, heads[0], heads[1])
    give_ref[:rows] = jnp.where(half == 0, heads[1], heads[0])
    mine_ref[rows:] = band_ref[...]
    give_ref[rows:] = band_ref[...]


def student_side(place, here, there, weight, query, band, slots):
    rows, feats = query.shape
    vm = pl.BlockSpec(memory_space=pltpu.VMEM)
    return pl.pallas_call(
        functools.partial(student_kernel, slots),
        in_specs=[pl.BlockSpec(memory_space=pltpu.SMEM)] + [vm] * 5,
        out_specs=[vm] * 2,
        out_shape=[jax.ShapeDtypeStruct((rows + band.shape[0], 2 * slots * HDIM), BF)] * 2,
        compiler_params=params(),
        cost_estimate=cost(8 * rows * feats * feats, 16 * rows * feats),
    )(place, here, there, weight, query, band)


def cotangent_kernel(place_ref, here_ref, there_ref, after_ref, out_ref):
    cols = here_ref.shape[2]
    for i, ref in enumerate((here_ref, here_ref, there_ref, there_ref)):
        c = pl.multiple_of((place_ref[1] ^ CLIPS[i]) * cols, cols)
        out_ref[:, pl.ds(c, cols)] = ref[i % 2]


def whole_cotangent(place, here, there, after):
    _, rows, cols = here.shape
    vm = pl.BlockSpec(memory_space=pltpu.VMEM)
    return pl.pallas_call(
        cotangent_kernel,
        in_specs=[
            pl.BlockSpec(memory_space=pltpu.SMEM),
            vm,
            vm,
            pl.BlockSpec(memory_space=pl.ANY),
        ],
        out_specs=vm,
        out_shape=jax.ShapeDtypeStruct((rows, 4 * cols), BF),
        compiler_params=params(),
        cost_estimate=cost(0, 16 * rows * cols),
    )(place, here, there, after)


def edge_kernel(place_ref, mine_ref, peer_ref, after_ref, a_ref, b_ref):
    first = place_ref[0] == 0
    mine, peer = mine_ref[...], peer_ref[...]
    a_ref[...] = jnp.where(first, mine, peer)
    b_ref[...] = jnp.where(first, peer, mine)


def edges(place, mine, peer, after):
    vm = pl.BlockSpec(memory_space=pltpu.VMEM)
    return pl.pallas_call(
        edge_kernel,
        in_specs=[
            pl.BlockSpec(memory_space=pltpu.SMEM),
            vm,
            vm,
            pl.BlockSpec(memory_space=pl.ANY),
        ],
        out_specs=[vm] * 2,
        out_shape=[jax.ShapeDtypeStruct(mine.shape, BF)] * 2,
        compiler_params=params(),
        cost_estimate=cost(0, 8 * mine.size),
    )(place, mine, peer, after)


def split3(x):
    a = x.astype(BF).astype(F32)
    b = (x - a).astype(BF).astype(F32)
    c = (x - a - b).astype(BF).astype(F32)
    return [a, b, c]


def attend_kernel(slots, tiles, lohi_ref, qga_ref, qgb_ref, *refs):
    outa_ref, outb_ref = refs[-2 * tiles - 2 : -2 * tiles]
    s_refs, d_refs = refs[-2 * tiles : -tiles], refs[-tiles:]
    rows = outa_ref.shape[1]
    blocks = refs[0].shape[0] // TBLK
    nblk = TILE // SBLK
    cblk = CHUNK // TBLK
    lane = lax.broadcasted_iota(jnp.int32, (1, TILE), 1)
    rhs_lane = lax.broadcasted_iota(jnp.int32, (TILE, 2 * HDIM), 1)
    row_id = lax.broadcasted_iota(jnp.int32, (STATS, TILE), 0)
    z8 = jnp.zeros((8, TILE), F32)
    for (i, slot), (u, q_ref, o_ref) in itertools.product(
        enumerate(slots), ((0, qga_ref, outa_ref), (1, qgb_ref, outb_ref))
    ):
        kv_ref, kvt_ref = refs[2 * i : 2 * i + 2]
        own = slice(slot * 2 * HDIM, (slot + 1) * 2 * HDIM)
        out_rows = slice(i * OUT, (i + 1) * OUT)

        def group(g, carry):
            held = []
            n = jnp.int32(0)
            for k in range(tiles):
                t = g * tiles + k
                base = u * (rows // SBLK) + t * nblk
                los = [lohi_ref[0, base + i] for i in range(nblk)]
                his = [lohi_ref[1, base + i] for i in range(nblk)]
                lo, hi = los[0], his[0]
                lo_lane = jnp.full((1, TILE), los[0])
                hi_lane = jnp.full((1, TILE), his[0])
                for i in range(1, nblk):
                    lo = jnp.minimum(lo, los[i])
                    hi = jnp.maximum(hi, his[i])
                    lo_lane = jnp.where(lane < i * SBLK, lo_lane, los[i])
                    hi_lane = jnp.where(lane < i * SBLK, hi_lane, his[i])
                lo = jnp.maximum(lo, 0)
                hi = jnp.minimum(hi, blocks - 1)
                n = jnp.maximum(n, jnp.maximum(hi - lo + cblk, 0) // cblk)
                r = pl.multiple_of(t * TILE, TILE)
                qg = q_ref[pl.ds(r, TILE), own]
                zero = jnp.zeros_like(qg)
                rhs = jnp.concatenate(
                    [
                        jnp.where(rhs_lane < HDIM, qg, zero),
                        jnp.where(rhs_lane < HDIM, zero, qg),
                    ],
                    axis=0,
                )
                held.append((lo, lo_lane, hi_lane, rhs, r))

            def start(i, lo):
                kb = jnp.minimum(lo + i * cblk, blocks - cblk)
                return kb, pl.multiple_of(kb * TBLK, TBLK)

            def scores(i, tops):
                s0 = pl.multiple_of(i * CHUNK, CHUNK)
                new = []
                for k, (lo, lo_lane, hi_lane, rhs, _) in enumerate(held):
                    kb0, k0 = start(i, lo)
                    low = jnp.maximum(lo_lane, lo + i * cblk)
                    sd = lax.dot_general(
                        kv_ref[pl.ds(k0, CHUNK), :], rhs, NT, preferred_element_type=F32
                    )
                    d_refs[k][pl.ds(s0, CHUNK), :] = sd[:, TILE:]
                    m = tops[k]
                    for b in range(cblk):
                        ok = (low <= kb0 + b) & (hi_lane >= kb0 + b)
                        s = jnp.where(ok, sd[b * TBLK : (b + 1) * TBLK, :TILE], NEG)
                        s_refs[k][pl.ds(s0 + b * TBLK, TBLK), :] = s
                        m = jnp.maximum(m, jnp.max(s.reshape(TBLK // 8, 8, TILE), axis=0))
                    new.append(m)
                return tuple(new)

            tops = lax.fori_loop(
                0, n, scores, tuple(jnp.full((8, TILE), NEG, F32) for _ in range(tiles))
            )
            tops = [jnp.max(m, axis=0, keepdims=True) for m in tops]

            def expo(i, sums):
                s0 = pl.multiple_of(i * CHUNK, CHUNK)
                new = []
                for k in range(tiles):
                    l, dl = sums[k]
                    p = jnp.exp(s_refs[k][pl.ds(s0, CHUNK), :] - tops[k])
                    s_refs[k][pl.ds(s0, CHUNK), :] = p
                    l = l + jnp.sum(p.reshape(CHUNK // 8, 8, TILE), axis=0)
                    pd = p * d_refs[k][pl.ds(s0, CHUNK), :]
                    dl = dl + jnp.sum(pd.reshape(CHUNK // 8, 8, TILE), axis=0)
                    new.append((l, dl))
                return tuple(new)

            ends = []
            for l, dl in lax.fori_loop(0, n, expo, ((z8, z8),) * tiles):
                l = jnp.sum(l, axis=0, keepdims=True)
                inv = 1.0 / jnp.maximum(l, 1e-30)
                ends.append((l, inv, jnp.sum(dl, axis=0, keepdims=True) * inv))

            def products(i, accs):
                s0 = pl.multiple_of(i * CHUNK, CHUNK)
                new = []
                for k in range(tiles):
                    _, k0 = start(i, held[k][0])
                    p = s_refs[k][pl.ds(s0, CHUNK), :]
                    ds = p * (d_refs[k][pl.ds(s0, CHUNK), :] - ends[k][2])
                    both = jnp.concatenate([p.astype(BF), ds.astype(BF)], axis=1)
                    new.append(
                        accs[k]
                        + jnp.dot(
                            kvt_ref[:, pl.ds(k0, CHUNK)], both, preferred_element_type=F32
                        )
                    )
                return tuple(new)

            accs = lax.fori_loop(
                0, n, products, tuple(jnp.zeros((2 * HDIM, 2 * TILE), F32) for _ in range(tiles))
            )
            for k in range(tiles):
                l, inv, delta = ends[k]
                acc = accs[k] * jnp.concatenate([inv, inv], axis=1)
                stats = jnp.where(row_id == 9, 1.0, 0.0)
                for i, piece in enumerate(split3(tops[k]) + split3(l) + split3(delta)):
                    stats = jnp.where(row_id == i, piece, stats)
                out = jnp.concatenate([acc[:, :TILE], acc[:HDIM, TILE:], stats], axis=0)
                o_ref[out_rows, pl.ds(held[k][4], TILE)] = out.astype(o_ref.dtype)
            return carry

        lax.fori_loop(0, rows // (TILE * tiles), group, 0)


def attend(slots, tiles, rows, lohi, qga, qgb, kvs, out_dtype, *after):
    keys = kvs[0].shape[0]
    n = len(slots)
    vm = pl.BlockSpec(memory_space=pltpu.VMEM)
    return pl.pallas_call(
        functools.partial(attend_kernel, slots, tiles),
        in_specs=[pl.BlockSpec(memory_space=pltpu.SMEM)]
        + [vm] * (2 + 2 * n)
        + [pl.BlockSpec(memory_space=pl.ANY)] * len(after),
        out_specs=[vm] * 2,
        out_shape=[jax.ShapeDtypeStruct((n * OUT, rows), out_dtype)] * 2,
        scratch_shapes=[pltpu.VMEM((keys, TILE), F32)] * (2 * tiles),
        compiler_params=params(),
        cost_estimate=cost(
            n * rows * keys * 1024, n * (4 * keys * 128 + 16 * rows * 256), n * rows * keys
        ),
    )(lohi, qga, qgb, *kvs, *after)


def combine_kernel(groups, slots, place_ref, cot_ref, pcot_ref, *refs):
    parts, refs = refs[: 2 * slots + 2], refs[2 * slots + 2 :]
    oqa_ref, oqb_ref, shares, buf = refs[0], refs[1], refs[2:-1], refs[-1]
    scale = 1.0 / math.sqrt(HDIM)
    for u, oq_ref in enumerate((oqa_ref, oqb_ref)):
        for s in range(slots):
            own = parts[2 * s + u][...]
            rem = parts[2 * slots + u][s * OUT : (s + 1) * OUT].astype(F32)

            def stat(x, i):
                r = 3 * HDIM + 3 * i
                return x[r : r + 1] + x[r + 1 : r + 2] + x[r + 2 : r + 3]

            flag = rem[3 * HDIM + 9 : 3 * HDIM + 10]
            m_o, m_r = stat(own, 0), jnp.where(flag > 0.5, stat(rem, 0), NEG)
            l_o, l_r = stat(own, 1), stat(rem, 1)
            d_o, d_r = stat(own, 2), stat(rem, 2)
            top = jnp.maximum(m_o, m_r)
            w_o = l_o * jnp.exp(m_o - top)
            w_r = jnp.where(m_r > 0.5 * NEG, l_r * jnp.exp(m_r - top), 0.0)
            norm = 1.0 / (w_o + w_r)
            w_o, w_r = w_o * norm, w_r * norm
            delta = w_o * d_o + w_r * d_r
            attn = w_o * own[HDIM : 2 * HDIM] + w_r * rem[HDIM : 2 * HDIM]
            s_o, s_r = scale * w_o, scale * w_r
            dq = s_o * own[2 * HDIM : 3 * HDIM] - (s_o * (delta - d_o)) * own[:HDIM]
            dq += s_r * rem[2 * HDIM : 3 * HDIM] - (s_r * (delta - d_r)) * rem[:HDIM]
            oq_ref[s * HDIM : (s + 1) * HDIM] = attn.astype(BF)
            oq_ref[(slots + s) * HDIM : (slots + s + 1) * HDIM] = dq.astype(BF)
    first = place_ref[0] == 0
    attn_a, attn_b = oqa_ref[: slots * HDIM], oqb_ref[: slots * HDIM]
    total = jnp.dot(
        jnp.where(first, attn_a, attn_b), cot_ref[...], preferred_element_type=F32
    )
    total += jnp.dot(
        jnp.where(first, attn_b, attn_a), pcot_ref[...], preferred_element_type=F32
    )
    total = total.astype(BF)
    step = total.shape[1] // groups
    for g in range(groups):
        buf[g] = total[:, g * step : (g + 1) * step]
    for d in range(groups):
        shares[d][...] = buf[place_ref[2] ^ d]


def combine(place, cot, peer_cot, parts, groups, slots):
    rows = parts[0].shape[1]
    width = cot.shape[1]
    vm = pl.BlockSpec(memory_space=pltpu.VMEM)
    share = (slots * HDIM, width // groups)
    return pl.pallas_call(
        functools.partial(combine_kernel, groups, slots),
        in_specs=[pl.BlockSpec(memory_space=pltpu.SMEM)] + [vm] * (4 + 2 * slots),
        out_specs=[vm] * (2 + groups),
        out_shape=[jax.ShapeDtypeStruct((2 * slots * HDIM, rows), BF)] * 2
        + [jax.ShapeDtypeStruct(share, BF)] * groups,
        scratch_shapes=[pltpu.VMEM((groups, *share), BF)],
        compiler_params=params(),
        cost_estimate=cost(
            4 * rows * slots * HDIM * width, 4 * rows * width + 24 * rows * slots * 256
        ),
    )(place, cot, peer_cot, *parts)


def turn_kernel(place_ref, oqa_ref, oqb_ref, mine_ref, give_ref, xmine_ref, xgive_ref):
    width = xmine_ref.shape[1]
    first = place_ref[0] == 0
    a, b = oqa_ref[...], oqb_ref[...]
    mine = jnp.where(first, a, b).T
    give = jnp.where(first, b, a).T
    mine_ref[...] = mine
    give_ref[...] = give
    xmine_ref[...] = mine[:, :width]
    xgive_ref[...] = give[:, :width]


def turn(place, oqa, oqb):
    width, rows = oqa.shape
    vm = pl.BlockSpec(memory_space=pltpu.VMEM)
    return pl.pallas_call(
        turn_kernel,
        in_specs=[pl.BlockSpec(memory_space=pltpu.SMEM)] + [vm] * 2,
        out_specs=[vm] * 4,
        out_shape=[jax.ShapeDtypeStruct((rows, width), BF)] * 2
        + [jax.ShapeDtypeStruct((rows, width // 2), BF)] * 2,
        compiler_params=params(),
        cost_estimate=cost(0, 10 * rows * width),
    )(place, oqa, oqb)


def heads_kernel(place_ref, mine_ref, peer_ref, xmine_ref, xpeer_ref, x_ref, gq_ref):
    first = place_ref[0] == 0
    width = gq_ref.shape[1]

    def put(near, far):
        return jnp.concatenate(
            [jnp.where(first, near, far), jnp.where(first, far, near)], axis=1
        )

    mine, peer = mine_ref[...], peer_ref[...]
    x_ref[:, :width] = put(mine[:, : width // 2], peer[:, : width // 2])
    x_ref[:, width:] = put(xmine_ref[...], xpeer_ref[...])
    gq_ref[...] = put(mine[:, width // 2 :], peer[:, width // 2 :])


def heads(place, mine, peer, xmine, xpeer):
    rows, width = mine.shape
    vm = pl.BlockSpec(memory_space=pltpu.VMEM)
    return pl.pallas_call(
        heads_kernel,
        in_specs=[pl.BlockSpec(memory_space=pltpu.SMEM)] + [vm] * 4,
        out_specs=[vm] * 2,
        out_shape=[
            jax.ShapeDtypeStruct((rows, 2 * width), BF),
            jax.ShapeDtypeStruct((rows, width), BF),
        ],
        compiler_params=params(),
        cost_estimate=cost(0, 12 * rows * width),
    )(place, mine, peer, xmine, xpeer)


def project_kernel(here_ref, there_ref, *refs):
    columns, out_ref = refs[:-1], refs[-1]
    cols = columns[0].shape[0]
    total = None
    for i, w in enumerate(columns):
        ref = (here_ref, there_ref)[i % 2]
        c = i // 2 * cols
        part = jnp.dot(ref[:, c : c + cols], w[...], preferred_element_type=F32)
        total = part if total is None else total + part
    out_ref[...] = total.astype(BF)


def project(here, there, columns):
    rows, cols = here.shape[0], columns[0].shape[1]
    vm = pl.BlockSpec(memory_space=pltpu.VMEM)
    return pl.pallas_call(
        project_kernel,
        in_specs=[vm] * (2 + len(columns)),
        out_specs=vm,
        out_shape=jax.ShapeDtypeStruct((rows, cols), BF),
        compiler_params=params(),
        cost_estimate=cost(2 * rows * cols * 4 * cols, 12 * rows * cols),
    )(here, there, *columns)


def spread_kernel(groups, place_ref, *refs):
    held, out_ref, buf = refs[:groups], refs[-2], refs[-1]
    _, rows, step = held[0].shape
    for d, ref in enumerate(held):
        buf[d] = ref[...].astype(F32)
    for y in range(2):
        for g in range(groups):
            out_ref[y * rows : (y + 1) * rows, g * step : (g + 1) * step] = buf[
                g ^ place_ref[2], y ^ place_ref[0]
            ]


def spread(place, held, *after):
    groups = len(held)
    _, rows, step = held[0].shape
    vm = pl.BlockSpec(memory_space=pltpu.VMEM)
    return pl.pallas_call(
        functools.partial(spread_kernel, groups),
        in_specs=[pl.BlockSpec(memory_space=pltpu.SMEM)]
        + [vm] * groups
        + [pl.BlockSpec(memory_space=pl.ANY)] * len(after),
        out_specs=vm,
        out_shape=jax.ShapeDtypeStruct((2 * rows, groups * step), F32),
        scratch_shapes=[pltpu.VMEM((groups, 2, rows, step), F32)],
        compiler_params=params(),
        cost_estimate=cost(0, 2 * groups * rows * step * 6),
    )(place, *held, *after)


def on_device(
    groups,
    student_query,
    teacher_key,
    teacher_value,
    clip_order,
    band_start,
    band_end,
    output_weight,
    cotangent,
):
    shards = 2 * groups
    me = lax.axis_index("tm")
    clip = lax.axis_index("clip")
    half = me % 2
    z = me // 2
    place = jnp.stack([half, clip, z]).astype(jnp.int32)
    clips = lax.axis_size("clip")
    teacher_rows = teacher_key.shape[0]
    rows, feats = student_query.shape
    piece = teacher_rows // shards
    slots = feats // HDIM // 2
    hw = slots * HDIM

    def swap(x, d):
        return lax.ppermute(x, "tm", [(i, i ^ d) for i in range(shards)])

    def swap_clip(x, d):
        return lax.ppermute(x, "clip", [(i, i ^ d) for i in range(clips)])

    def swap_both(x, d):
        n = shards * clips
        return lax.ppermute(x, ("tm", "clip"), [(i, i ^ (clips + d)) for i in range(n)])

    def up(x):
        return lax.ppermute(x, "tm", [(i, i + 2) for i in range(shards - 2)])

    def down(x):
        return lax.ppermute(x, "tm", [(i + 2, i) for i in range(shards - 2)])

    here = jnp.stack([cotangent, swap_clip(cotangent, 2)])
    there = swap_clip(here, 1)
    blocks = band_start.shape[0]
    band = jnp.stack([band_start, band_end]).astype(BF)
    band = jnp.pad(band, ((0, 14), (0, 2 * hw - blocks)))
    qg_mine, qg_give = student_side(
        place, here, there, output_weight, student_query, band, slots
    )
    qg_peer = swap(qg_give, 1)
    sent = [pack(teacher_key, teacher_value, groups, slots, 0)]
    sent += [
        pack(teacher_key, teacher_value, groups, slots, s, qg_peer) for s in range(1, slots)
    ]
    qga = jnp.where(half == 0, qg_mine, qg_peer)
    qgb = jnp.where(half == 0, qg_peer, qg_mine)

    origin = z * 2 * blocks

    def limits(first_rows, *firsts):
        bands = [x[rows : rows + 2, :blocks] for x in first_rows]
        bands = jnp.concatenate(bands, axis=1).astype(F32).astype(jnp.int32)
        frame = [origin + f + jnp.arange(blocks, dtype=jnp.int32) for f in firsts]
        frame = jnp.concatenate(frame)
        lo = jnp.maximum(frame + bands[0], 0) - origin
        hi = jnp.minimum(frame + bands[1], shards * blocks - 1) - origin
        return jnp.stack([lo, hi])

    own_limits = limits((qga, qgb), 0, blocks)

    def columns_for(d):
        c = (clip ^ d) * feats
        return lax.dynamic_slice_in_dim(output_weight, c, feats, axis=1)

    columns = [columns_for(0)] + [swap_clip(columns_for(d), d) for d in range(1, clips)]

    lookup = lax.dynamic_slice_in_dim(clip_order, z * 2 * teacher_rows, 2 * teacher_rows)
    index = lookup // teacher_rows * piece + lookup % piece

    kvs, parts = [], []
    for s in range(slots):
        arrived = lax.all_to_all(
            sent[s].reshape(shards, 2 * piece, 2 * HDIM), "tm", 0, 0
        )
        kvs += put_in_order(arrived, index, teacher_rows, *parts[-2:])
        if s == slots - 1:
            far = attend(
                range(slots), 2, rows, halo_limits, qg_left, qg_right, kvs, BF
            )
            parts += attend([s], 4, rows, own_limits, qga, qgb, kvs[-2:], F32, *far)
        else:
            parts += attend([s], 4, rows, own_limits, qga, qgb, kvs[-2:], F32)
        if s == 0:
            edge_a, edge_b = edges(place, qg_mine, qg_peer, parts[0])
            qg_left, qg_right = up(edge_b), down(edge_a)
            halo_limits = limits((qg_left, qg_right), -blocks, 2 * blocks)
            cot = whole_cotangent(place, here, there, parts[0])
    parts += [up(far[1]), down(far[0])]
    oqa, oqb, *got = combine(place, cot, swap(cot, 1), parts, groups, slots)
    mine, give, xmine, xgive = turn(place, oqa, oqb)
    total = got[0].astype(F32)
    for d in range(1, groups):
        total += swap(got[d], 2 * d).astype(F32)
    total = total.astype(BF)
    both = jnp.stack([total, swap(total, 1)])
    held = [both] + [swap(both, 2 * d) for d in range(1, groups)]
    near, grad_query = heads(
        place, mine, swap(give, 1), swap_clip(xmine, 2), swap_both(xgive, 2)
    )
    joined = project(near, swap_clip(near, 1), columns)
    return joined, grad_query, spread(place, held, joined)


def solution(mesh):
    return jax.shard_map(
        functools.partial(on_device, mesh.shape["tm"] // 2),
        mesh=mesh,
        in_specs=(
            P("tm", "clip"),
            P("tm", "clip"),
            P("tm", "clip"),
            P(),
            P("tm"),
            P("tm"),
            P("clip", None),
            P("tm", "clip"),
        ),
        out_specs=(P("tm", "clip"), P("tm", "clip"), P("clip", None)),
        check_vma=False,
    )
```

```python
import functools
import itertools
import math

import jax
import jax.numpy as jnp
from jax import lax
from jax.experimental import pallas as pl
from jax.experimental.pallas import tpu as pltpu
from jax.sharding import PartitionSpec as P

HDIM = 64
SBLK = 32
TBLK = 128
TILE = 128
CHUNK = 1024
NEG = -1e30
STATS = 16
OUT = 3 * HDIM + STATS
BF = jnp.bfloat16
F32 = jnp.float32
NT = (((1,), (1,)), ((), ()))
CLIPS = (0, 2, 1, 3)
VMEM_LIMIT = 48 * 1024 * 1024


def params(*semantics):
    return pltpu.CompilerParams(
        dimension_semantics=semantics or None, vmem_limit_bytes=VMEM_LIMIT
    )


def cost(flops, nbytes, trans=0):
    return pl.CostEstimate(flops=flops, bytes_accessed=nbytes, transcendentals=trans)


def pack_kernel(slots, slot, k_ref, v_ref, *refs):
    out = refs[-1]
    for half in range(2):
        c = (half * slots + slot) * HDIM
        out[0, half] = jnp.concatenate([k_ref[:, c : c + HDIM], v_ref[:, c : c + HDIM]], axis=1)


def pack(keys, values, groups, slots, slot, *after):
    rows, feats = keys.shape
    part = rows // groups
    block = pl.BlockSpec((part, feats), lambda i: (i, 0))
    return pl.pallas_call(
        functools.partial(pack_kernel, slots, slot),
        grid=(groups,),
        in_specs=[block, block] + [pl.BlockSpec(memory_space=pl.ANY)] * len(after),
        out_specs=pl.BlockSpec((1, 2, part, 2 * HDIM), lambda i: (i, 0, 0, 0)),
        out_shape=jax.ShapeDtypeStruct((groups, 2, part, 2 * HDIM), BF),
        compiler_params=params("arbitrary"),
        cost_estimate=cost(0, 3 * rows * feats * 2),
    )(keys, values, *after)


def order_kernel(idx_ref, arr_ref, *refs):
    kv_ref, kvt_ref, arrt, hot = refs[-4:]
    rows = arrt.shape[1]
    arr = arr_ref[...].reshape(rows, arrt.shape[0])
    for j in range(0, rows, 256):
        arrt[:, j : j + 256] = arr[j : j + 256].T
    idx = idx_ref[0]
    iota = lax.broadcasted_iota(jnp.int32, (256, rows), 0).astype(F32).astype(BF)
    for j in range(0, rows, 256):
        near = idx - j
        near = jnp.where((near >= 0) & (near < 256), near, -1).astype(F32).astype(BF)
        hot[j : j + 256] = jnp.where(iota == near, BF(1), BF(0))
    acc = jnp.dot(arrt[...], hot[...], preferred_element_type=F32)
    kvt_ref[...] = acc.astype(BF)
    kv_ref[...] = acc.T.astype(BF)


def put_in_order(arrived, index, rows, *after):
    sources, twice, width = arrived.shape
    return pl.pallas_call(
        order_kernel,
        grid=(2,),
        in_specs=[
            pl.BlockSpec((1, 1, rows), lambda u: (u, 0, 0)),
            pl.BlockSpec((sources, twice // 2, width), lambda u: (0, u, 0)),
        ]
        + [pl.BlockSpec(memory_space=pl.ANY)] * len(after),
        out_specs=[
            pl.BlockSpec((rows, width), lambda u: (u, 0)),
            pl.BlockSpec((width, rows), lambda u: (0, u)),
        ],
        out_shape=[
            jax.ShapeDtypeStruct((2 * rows, width), BF),
            jax.ShapeDtypeStruct((width, 2 * rows), BF),
        ],
        scratch_shapes=[pltpu.VMEM((width, rows), BF), pltpu.VMEM((rows, rows), BF)],
        compiler_params=params("arbitrary"),
        cost_estimate=cost(4 * rows * rows * width, 6 * rows * width * 2),
    )(index.reshape(2, 1, rows), arrived, *after)


def student_kernel(slots, place_ref, here_ref, there_ref, w_ref, q_ref, band_ref, mine_ref, give_ref):
    rows, feats = q_ref.shape
    half, clip = place_ref[0], place_ref[1]
    total = None
    for i, ref in enumerate((here_ref, here_ref, there_ref, there_ref)):
        c = pl.multiple_of((clip ^ CLIPS[i]) * feats, feats)
        part = lax.dot_general(
            ref[i % 2], w_ref[:, pl.ds(c, feats)], NT, preferred_element_type=F32
        )
        total = part if total is None else total + part
    g = total.astype(BF)
    q = q_ref[...] * BF(1.0 / math.sqrt(HDIM))
    heads = []
    for y in range(2):
        cols = []
        for s in range(slots):
            c = (y * slots + s) * HDIM
            cols += [q[:, c : c + HDIM], g[:, c : c + HDIM]]
        heads.append(jnp.concatenate(cols, axis=1))
    mine_ref[:rows] = jnp.where(half == 0, heads[0], heads[1])
    give_ref[:rows] = jnp.where(half == 0, heads[1], heads[0])
    mine_ref[rows:] = band_ref[...]
    give_ref[rows:] = band_ref[...]


def student_side(place, here, there, weight, query, band, slots):
    rows, feats = query.shape
    vm = pl.BlockSpec(memory_space=pltpu.VMEM)
    return pl.pallas_call(
        functools.partial(student_kernel, slots),
        in_specs=[pl.BlockSpec(memory_space=pltpu.SMEM)] + [vm] * 5,
        out_specs=[vm] * 2,
        out_shape=[jax.ShapeDtypeStruct((rows + band.shape[0], 2 * slots * HDIM), BF)] * 2,
        compiler_params=params(),
        cost_estimate=cost(8 * rows * feats * feats, 16 * rows * feats),
    )(place, here, there, weight, query, band)


def cotangent_kernel(place_ref, here_ref, there_ref, after_ref, out_ref):
    cols = here_ref.shape[2]
    for i, ref in enumerate((here_ref, here_ref, there_ref, there_ref)):
        c = pl.multiple_of((place_ref[1] ^ CLIPS[i]) * cols, cols)
        out_ref[:, pl.ds(c, cols)] = ref[i % 2]


def whole_cotangent(place, here, there, after):
    _, rows, cols = here.shape
    vm = pl.BlockSpec(memory_space=pltpu.VMEM)
    return pl.pallas_call(
        cotangent_kernel,
        in_specs=[
            pl.BlockSpec(memory_space=pltpu.SMEM),
            vm,
            vm,
            pl.BlockSpec(memory_space=pl.ANY),
        ],
        out_specs=vm,
        out_shape=jax.ShapeDtypeStruct((rows, 4 * cols), BF),
        compiler_params=params(),
        cost_estimate=cost(0, 16 * rows * cols),
    )(place, here, there, after)


def edge_kernel(place_ref, mine_ref, peer_ref, after_ref, a_ref, b_ref):
    first = place_ref[0] == 0
    mine, peer = mine_ref[...], peer_ref[...]
    a_ref[...] = jnp.where(first, mine, peer)
    b_ref[...] = jnp.where(first, peer, mine)


def edges(place, mine, peer, after):
    vm = pl.BlockSpec(memory_space=pltpu.VMEM)
    return pl.pallas_call(
        edge_kernel,
        in_specs=[
            pl.BlockSpec(memory_space=pltpu.SMEM),
            vm,
            vm,
            pl.BlockSpec(memory_space=pl.ANY),
        ],
        out_specs=[vm] * 2,
        out_shape=[jax.ShapeDtypeStruct(mine.shape, BF)] * 2,
        compiler_params=params(),
        cost_estimate=cost(0, 8 * mine.size),
    )(place, mine, peer, after)


def tails_kernel(left_ref, right_ref, after_ref, out_ref):
    n = out_ref.shape[0] // 2
    out_ref[:n] = left_ref[left_ref.shape[0] - n :]
    out_ref[n:] = right_ref[right_ref.shape[0] - n :]


def tails(left, right, count, after):
    vm = pl.BlockSpec(memory_space=pltpu.VMEM)
    return pl.pallas_call(
        tails_kernel,
        in_specs=[vm, vm, pl.BlockSpec(memory_space=pl.ANY)],
        out_specs=vm,
        out_shape=jax.ShapeDtypeStruct((2 * count, left.shape[1]), BF),
        compiler_params=params(),
        cost_estimate=cost(0, 8 * count * left.shape[1]),
    )(left, right, after)


def split3(x):
    a = x.astype(BF).astype(F32)
    b = (x - a).astype(BF).astype(F32)
    c = (x - a - b).astype(BF).astype(F32)
    return [a, b, c]


def attend_kernel(slots, tiles, by_exchange, place_ref, lohi_ref, qga_ref, qgb_ref, *refs):
    outa_ref, outb_ref = refs[-2 * tiles - 2 : -2 * tiles]
    s_refs, d_refs = refs[-2 * tiles : -tiles], refs[-tiles:]
    rows = outa_ref.shape[1]
    blocks = refs[0].shape[0] // TBLK
    nblk = TILE // SBLK
    cblk = CHUNK // TBLK
    lane = lax.broadcasted_iota(jnp.int32, (1, TILE), 1)
    rhs_lane = lax.broadcasted_iota(jnp.int32, (TILE, 2 * HDIM), 1)
    row_id = lax.broadcasted_iota(jnp.int32, (STATS, TILE), 0)
    z8 = jnp.zeros((8, TILE), F32)
    odd = place_ref[2] % 2 == 1

    def stores(place, out):
        def first():
            outa_ref[place] = out

        def second():
            outb_ref[place] = out

        return first, second

    for (i, slot), (u, q_ref) in itertools.product(
        enumerate(slots), ((0, qga_ref), (1, qgb_ref))
    ):
        kv_ref, kvt_ref = refs[2 * i : 2 * i + 2]
        own = slice(slot * 2 * HDIM, (slot + 1) * 2 * HDIM)
        out_rows = slice(i * OUT, (i + 1) * OUT)

        def group(g, carry):
            held = []
            n = jnp.int32(0)
            for k in range(tiles):
                t = g * tiles + k
                base = u * (rows // SBLK) + t * nblk
                los = [lohi_ref[0, base + i] for i in range(nblk)]
                his = [lohi_ref[1, base + i] for i in range(nblk)]
                lo, hi = los[0], his[0]
                lo_lane = jnp.full((1, TILE), los[0])
                hi_lane = jnp.full((1, TILE), his[0])
                for i in range(1, nblk):
                    lo = jnp.minimum(lo, los[i])
                    hi = jnp.maximum(hi, his[i])
                    lo_lane = jnp.where(lane < i * SBLK, lo_lane, los[i])
                    hi_lane = jnp.where(lane < i * SBLK, hi_lane, his[i])
                lo = jnp.maximum(lo, 0)
                hi = jnp.minimum(hi, blocks - 1)
                n = jnp.maximum(n, jnp.maximum(hi - lo + cblk, 0) // cblk)
                r = pl.multiple_of(t * TILE, TILE)
                qg = q_ref[pl.ds(r, TILE), own]
                zero = jnp.zeros_like(qg)
                rhs = jnp.concatenate(
                    [
                        jnp.where(rhs_lane < HDIM, qg, zero),
                        jnp.where(rhs_lane < HDIM, zero, qg),
                    ],
                    axis=0,
                )
                held.append((lo, lo_lane, hi_lane, rhs, r))

            def start(i, lo):
                kb = jnp.minimum(lo + i * cblk, blocks - cblk)
                return kb, pl.multiple_of(kb * TBLK, TBLK)

            def scores(i, tops):
                s0 = pl.multiple_of(i * CHUNK, CHUNK)
                new = []
                for k, (lo, lo_lane, hi_lane, rhs, _) in enumerate(held):
                    kb0, k0 = start(i, lo)
                    low = jnp.maximum(lo_lane, lo + i * cblk)
                    sd = lax.dot_general(
                        kv_ref[pl.ds(k0, CHUNK), :], rhs, NT, preferred_element_type=F32
                    )
                    d_refs[k][pl.ds(s0, CHUNK), :] = sd[:, TILE:]
                    m = tops[k]
                    for b in range(cblk):
                        ok = (low <= kb0 + b) & (hi_lane >= kb0 + b)
                        s = jnp.where(ok, sd[b * TBLK : (b + 1) * TBLK, :TILE], NEG)
                        s_refs[k][pl.ds(s0 + b * TBLK, TBLK), :] = s
                        m = jnp.maximum(m, jnp.max(s.reshape(TBLK // 8, 8, TILE), axis=0))
                    new.append(m)
                return tuple(new)

            tops = lax.fori_loop(
                0, n, scores, tuple(jnp.full((8, TILE), NEG, F32) for _ in range(tiles))
            )
            tops = [jnp.max(m, axis=0, keepdims=True) for m in tops]

            def expo(i, sums):
                s0 = pl.multiple_of(i * CHUNK, CHUNK)
                new = []
                for k in range(tiles):
                    l, dl = sums[k]
                    p = jnp.exp(s_refs[k][pl.ds(s0, CHUNK), :] - tops[k])
                    s_refs[k][pl.ds(s0, CHUNK), :] = p
                    l = l + jnp.sum(p.reshape(CHUNK // 8, 8, TILE), axis=0)
                    pd = p * d_refs[k][pl.ds(s0, CHUNK), :]
                    dl = dl + jnp.sum(pd.reshape(CHUNK // 8, 8, TILE), axis=0)
                    new.append((l, dl))
                return tuple(new)

            ends = []
            for l, dl in lax.fori_loop(0, n, expo, ((z8, z8),) * tiles):
                l = jnp.sum(l, axis=0, keepdims=True)
                inv = 1.0 / jnp.maximum(l, 1e-30)
                ends.append((l, inv, jnp.sum(dl, axis=0, keepdims=True) * inv))

            def products(i, accs):
                s0 = pl.multiple_of(i * CHUNK, CHUNK)
                new = []
                for k in range(tiles):
                    _, k0 = start(i, held[k][0])
                    p = s_refs[k][pl.ds(s0, CHUNK), :]
                    ds = p * (d_refs[k][pl.ds(s0, CHUNK), :] - ends[k][2])
                    both = jnp.concatenate([p.astype(BF), ds.astype(BF)], axis=1)
                    new.append(
                        accs[k]
                        + jnp.dot(
                            kvt_ref[:, pl.ds(k0, CHUNK)], both, preferred_element_type=F32
                        )
                    )
                return tuple(new)

            accs = lax.fori_loop(
                0, n, products, tuple(jnp.zeros((2 * HDIM, 2 * TILE), F32) for _ in range(tiles))
            )
            for k in range(tiles):
                l, inv, delta = ends[k]
                acc = accs[k] * jnp.concatenate([inv, inv], axis=1)
                stats = jnp.where(row_id == 9, 1.0, 0.0)
                for i, piece in enumerate(split3(tops[k]) + split3(l) + split3(delta)):
                    stats = jnp.where(row_id == i, piece, stats)
                out = jnp.concatenate([acc[:, :TILE], acc[:HDIM, TILE:], stats], axis=0)
                place = (out_rows, pl.ds(held[k][4], TILE))
                out = out.astype(outa_ref.dtype)
                if by_exchange:
                    jax.lax.cond(odd == (u == 0), *stores(place, out))
                else:
                    (outa_ref, outb_ref)[u][place] = out
            return carry

        lax.fori_loop(0, rows // (TILE * tiles), group, 0)


def attend(place, slots, tiles, rows, lohi, qga, qgb, kvs, by_exchange, *after):
    keys = kvs[0].shape[0]
    n = len(slots)
    vm = pl.BlockSpec(memory_space=pltpu.VMEM)
    return pl.pallas_call(
        functools.partial(attend_kernel, slots, tiles, by_exchange),
        in_specs=[pl.BlockSpec(memory_space=pltpu.SMEM)] * 2
        + [vm] * (2 + 2 * n)
        + [pl.BlockSpec(memory_space=pl.ANY)] * len(after),
        out_specs=[vm] * 2,
        out_shape=[jax.ShapeDtypeStruct((n * OUT, rows), BF)] * 2,
        scratch_shapes=[pltpu.VMEM((keys, TILE), F32)] * (2 * tiles),
        compiler_params=params(),
        cost_estimate=cost(
            n * rows * keys * 1024, n * (4 * keys * 128 + 16 * rows * 256), n * rows * keys
        ),
    )(place, lohi, qga, qgb, *kvs, *after)


def combine_kernel(groups, slots, place_ref, cot_ref, pcot_ref, *refs):
    parts, refs = refs[: 2 * slots + 2], refs[2 * slots + 2 :]
    oqa_ref, oqb_ref, shares, buf = refs[0], refs[1], refs[2:-1], refs[-1]
    scale = 1.0 / math.sqrt(HDIM)
    odd = place_ref[2] % 2 == 1
    for u, oq_ref in enumerate((oqa_ref, oqb_ref)):
        for s in range(slots):
            own = parts[2 * s + u][...].astype(F32)
            rem = [r[s * OUT : (s + 1) * OUT] for r in parts[2 * slots :]]
            rem = jnp.where(odd == (u == 0), *rem).astype(F32)

            def stat(x, i):
                r = 3 * HDIM + 3 * i
                return x[r : r + 1] + x[r + 1 : r + 2] + x[r + 2 : r + 3]

            flag = rem[3 * HDIM + 9 : 3 * HDIM + 10]
            m_o, m_r = stat(own, 0), jnp.where(flag > 0.5, stat(rem, 0), NEG)
            l_o, l_r = stat(own, 1), stat(rem, 1)
            d_o, d_r = stat(own, 2), stat(rem, 2)
            top = jnp.maximum(m_o, m_r)
            w_o = l_o * jnp.exp(m_o - top)
            w_r = jnp.where(m_r > 0.5 * NEG, l_r * jnp.exp(m_r - top), 0.0)
            norm = 1.0 / (w_o + w_r)
            w_o, w_r = w_o * norm, w_r * norm
            delta = w_o * d_o + w_r * d_r
            attn = w_o * own[HDIM : 2 * HDIM] + w_r * rem[HDIM : 2 * HDIM]
            s_o, s_r = scale * w_o, scale * w_r
            dq = s_o * own[2 * HDIM : 3 * HDIM] - (s_o * (delta - d_o)) * own[:HDIM]
            dq += s_r * rem[2 * HDIM : 3 * HDIM] - (s_r * (delta - d_r)) * rem[:HDIM]
            oq_ref[s * HDIM : (s + 1) * HDIM] = attn.astype(BF)
            oq_ref[(slots + s) * HDIM : (slots + s + 1) * HDIM] = dq.astype(BF)
    first = place_ref[0] == 0
    attn_a, attn_b = oqa_ref[: slots * HDIM], oqb_ref[: slots * HDIM]
    total = jnp.dot(
        jnp.where(first, attn_a, attn_b), cot_ref[...], preferred_element_type=F32
    )
    total += jnp.dot(
        jnp.where(first, attn_b, attn_a), pcot_ref[...], preferred_element_type=F32
    )
    total = total.astype(BF)
    step = total.shape[1] // groups
    for g in range(groups):
        buf[g] = total[:, g * step : (g + 1) * step]
    for d in range(groups):
        shares[d][...] = buf[place_ref[2] ^ d]


def combine(place, cot, peer_cot, parts, groups, slots):
    rows = parts[0].shape[1]
    width = cot.shape[1]
    vm = pl.BlockSpec(memory_space=pltpu.VMEM)
    share = (slots * HDIM, width // groups)
    return pl.pallas_call(
        functools.partial(combine_kernel, groups, slots),
        in_specs=[pl.BlockSpec(memory_space=pltpu.SMEM)] + [vm] * (4 + 2 * slots),
        out_specs=[vm] * (2 + groups),
        out_shape=[jax.ShapeDtypeStruct((2 * slots * HDIM, rows), BF)] * 2
        + [jax.ShapeDtypeStruct(share, BF)] * groups,
        scratch_shapes=[pltpu.VMEM((groups, *share), BF)],
        compiler_params=params(),
        cost_estimate=cost(
            4 * rows * slots * HDIM * width, 4 * rows * width + 24 * rows * slots * 256
        ),
    )(place, cot, peer_cot, *parts)


def turn_kernel(place_ref, oqa_ref, oqb_ref, mine_ref, give_ref, xmine_ref, xgive_ref):
    width = xmine_ref.shape[1]
    first = place_ref[0] == 0
    a, b = oqa_ref[...], oqb_ref[...]
    mine = jnp.where(first, a, b).T
    give = jnp.where(first, b, a).T
    mine_ref[...] = mine
    give_ref[...] = give
    xmine_ref[...] = mine[:, :width]
    xgive_ref[...] = give[:, :width]


def turn(place, oqa, oqb):
    width, rows = oqa.shape
    vm = pl.BlockSpec(memory_space=pltpu.VMEM)
    return pl.pallas_call(
        turn_kernel,
        in_specs=[pl.BlockSpec(memory_space=pltpu.SMEM)] + [vm] * 2,
        out_specs=[vm] * 4,
        out_shape=[jax.ShapeDtypeStruct((rows, width), BF)] * 2
        + [jax.ShapeDtypeStruct((rows, width // 2), BF)] * 2,
        compiler_params=params(),
        cost_estimate=cost(0, 10 * rows * width),
    )(place, oqa, oqb)


def heads_kernel(place_ref, mine_ref, peer_ref, xmine_ref, xpeer_ref, x_ref, gq_ref):
    first = place_ref[0] == 0
    width = gq_ref.shape[1]

    def put(near, far):
        return jnp.concatenate(
            [jnp.where(first, near, far), jnp.where(first, far, near)], axis=1
        )

    mine, peer = mine_ref[...], peer_ref[...]
    x_ref[:, :width] = put(mine[:, : width // 2], peer[:, : width // 2])
    x_ref[:, width:] = put(xmine_ref[...], xpeer_ref[...])
    gq_ref[...] = put(mine[:, width // 2 :], peer[:, width // 2 :])


def heads(place, mine, peer, xmine, xpeer):
    rows, width = mine.shape
    vm = pl.BlockSpec(memory_space=pltpu.VMEM)
    return pl.pallas_call(
        heads_kernel,
        in_specs=[pl.BlockSpec(memory_space=pltpu.SMEM)] + [vm] * 4,
        out_specs=[vm] * 2,
        out_shape=[
            jax.ShapeDtypeStruct((rows, 2 * width), BF),
            jax.ShapeDtypeStruct((rows, width), BF),
        ],
        compiler_params=params(),
        cost_estimate=cost(0, 12 * rows * width),
    )(place, mine, peer, xmine, xpeer)


def project_kernel(here_ref, there_ref, *refs):
    columns, out_ref = refs[:-1], refs[-1]
    cols = columns[0].shape[0]
    total = None
    for i, w in enumerate(columns):
        ref = (here_ref, there_ref)[i % 2]
        c = i // 2 * cols
        part = jnp.dot(ref[:, c : c + cols], w[...], preferred_element_type=F32)
        total = part if total is None else total + part
    out_ref[...] = total.astype(BF)


def project(here, there, columns):
    rows, cols = here.shape[0], columns[0].shape[1]
    vm = pl.BlockSpec(memory_space=pltpu.VMEM)
    return pl.pallas_call(
        project_kernel,
        in_specs=[vm] * (2 + len(columns)),
        out_specs=vm,
        out_shape=jax.ShapeDtypeStruct((rows, cols), BF),
        compiler_params=params(),
        cost_estimate=cost(2 * rows * cols * 4 * cols, 12 * rows * cols),
    )(here, there, *columns)


def spread_kernel(groups, place_ref, *refs):
    held, out_ref, buf = refs[:groups], refs[-2], refs[-1]
    _, rows, step = held[0].shape
    for d, ref in enumerate(held):
        buf[d] = ref[...].astype(F32)
    for y in range(2):
        for g in range(groups):
            out_ref[y * rows : (y + 1) * rows, g * step : (g + 1) * step] = buf[
                g ^ place_ref[2], y ^ place_ref[0]
            ]


def spread(place, held, *after):
    groups = len(held)
    _, rows, step = held[0].shape
    vm = pl.BlockSpec(memory_space=pltpu.VMEM)
    return pl.pallas_call(
        functools.partial(spread_kernel, groups),
        in_specs=[pl.BlockSpec(memory_space=pltpu.SMEM)]
        + [vm] * groups
        + [pl.BlockSpec(memory_space=pl.ANY)] * len(after),
        out_specs=vm,
        out_shape=jax.ShapeDtypeStruct((2 * rows, groups * step), F32),
        scratch_shapes=[pltpu.VMEM((groups, 2, rows, step), F32)],
        compiler_params=params(),
        cost_estimate=cost(0, 2 * groups * rows * step * 6),
    )(place, *held, *after)


def on_device(
    groups,
    student_query,
    teacher_key,
    teacher_value,
    clip_order,
    band_start,
    band_end,
    output_weight,
    cotangent,
):
    shards = 2 * groups
    me = lax.axis_index("tm")
    clip = lax.axis_index("clip")
    half = me % 2
    z = me // 2
    place = jnp.stack([half, clip, z]).astype(jnp.int32)
    clips = lax.axis_size("clip")
    teacher_rows = teacher_key.shape[0]
    rows, feats = student_query.shape
    piece = teacher_rows // shards
    slots = feats // HDIM // 2
    hw = slots * HDIM

    def swap(x, d):
        return lax.ppermute(x, "tm", [(i, i ^ d) for i in range(shards)])

    def swap_clip(x, d):
        return lax.ppermute(x, "clip", [(i, i ^ d) for i in range(clips)])

    def swap_both(x, d):
        n = shards * clips
        return lax.ppermute(x, ("tm", "clip"), [(i, i ^ (clips + d)) for i in range(n)])

    def up(x):
        return lax.ppermute(x, "tm", [(i, i + 2) for i in range(shards - 2)])

    def down(x):
        return lax.ppermute(x, "tm", [(i + 2, i) for i in range(shards - 2)])

    here = jnp.stack([cotangent, swap_clip(cotangent, 2)])
    there = swap_clip(here, 1)
    blocks = band_start.shape[0]
    band = jnp.stack([band_start, band_end]).astype(BF)
    band = jnp.pad(band, ((0, 14), (0, 2 * hw - blocks)))
    qg_mine, qg_give = student_side(
        place, here, there, output_weight, student_query, band, slots
    )
    qg_peer = swap(qg_give, 1)
    sent = [pack(teacher_key, teacher_value, groups, slots, 0)]
    sent += [
        pack(teacher_key, teacher_value, groups, slots, s, qg_peer) for s in range(1, slots)
    ]
    qga = jnp.where(half == 0, qg_mine, qg_peer)
    qgb = jnp.where(half == 0, qg_peer, qg_mine)

    origin = z * 2 * blocks

    def limits(first_rows, *firsts):
        bands = [x[:2, :blocks] for x in first_rows]
        bands = jnp.concatenate(bands, axis=1).astype(F32).astype(jnp.int32)
        frame = [origin + f + jnp.arange(blocks, dtype=jnp.int32) for f in firsts]
        frame = jnp.concatenate(frame)
        lo = jnp.maximum(frame + bands[0], 0) - origin
        hi = jnp.minimum(frame + bands[1], shards * blocks - 1) - origin
        return jnp.stack([lo, hi])

    own_limits = limits((qga[rows:], qgb[rows:]), 0, blocks)

    def columns_for(d):
        c = (clip ^ d) * feats
        return lax.dynamic_slice_in_dim(output_weight, c, feats, axis=1)

    columns = [columns_for(0)] + [swap_clip(columns_for(d), d) for d in range(1, clips)]

    lookup = lax.dynamic_slice_in_dim(clip_order, z * 2 * teacher_rows, 2 * teacher_rows)
    index = lookup // teacher_rows * piece + lookup % piece

    kvs, parts = [], []
    for s in range(slots):
        arrived = lax.all_to_all(
            sent[s].reshape(shards, 2 * piece, 2 * HDIM), "tm", 0, 0
        )
        kvs += put_in_order(arrived, index, teacher_rows, *parts[-2:])
        if s == slots - 1:
            count = band.shape[0]
            ends = tails(qg_left, qg_right, count, kvs[-1])
            halo_limits = limits((ends[:count], ends[count:]), -blocks, 2 * blocks)
            far = attend(
                place, range(slots), 2, rows, halo_limits, qg_left, qg_right, kvs, True
            )
        own = place, [s], 4, rows, own_limits, qga, qgb, kvs[-2:], False
        parts += attend(*own, *(far if s == slots - 1 else ()))
        if s == 0:
            edge_a, edge_b = edges(place, qg_mine, qg_peer, parts[0])
            qg_left, qg_right = up(edge_b), down(edge_a)
            cot = whole_cotangent(place, here, there, parts[0])
    parts += [swap(far[0], 2)]
    links = [(i, i + 2) for i in range(shards - 2) if i // 2 % 2]
    parts += [lax.ppermute(far[1], "tm", links + [(j, i) for i, j in links])]
    oqa, oqb, *got = combine(place, cot, swap(cot, 1), parts, groups, slots)
    mine, give, xmine, xgive = turn(place, oqa, oqb)
    total = got[0].astype(F32)
    for d in range(1, groups):
        total += swap(got[d], 2 * d).astype(F32)
    total = total.astype(BF)
    both = jnp.stack([total, swap(total, 1)])
    held = [both] + [swap(both, 2 * d) for d in range(1, groups)]
    near, grad_query = heads(
        place, mine, swap(give, 1), swap_clip(xmine, 2), swap_both(xgive, 2)
    )
    joined = project(near, swap_clip(near, 1), columns)
    return joined, grad_query, spread(place, held, joined)


def solution(mesh):
    return jax.shard_map(
        functools.partial(on_device, mesh.shape["tm"] // 2),
        mesh=mesh,
        in_specs=(
            P("tm", "clip"),
            P("tm", "clip"),
            P("tm", "clip"),
            P(),
            P("tm"),
            P("tm"),
            P("clip", None),
            P("tm", "clip"),
        ),
        out_specs=(P("tm", "clip"), P("tm", "clip"), P("clip", None)),
        check_vma=False,
    )
```

```python
import functools
import itertools
import math

import jax
import jax.numpy as jnp
from jax import lax
from jax.experimental import pallas as pl
from jax.experimental.pallas import tpu as pltpu
from jax.sharding import PartitionSpec as P

HDIM = 64
SBLK = 32
TBLK = 128
TILE = 128
CHUNK = 1024
NEG = -1e30
STATS = 16
OUT = 3 * HDIM + STATS
BF = jnp.bfloat16
F32 = jnp.float32
NT = (((1,), (1,)), ((), ()))
CLIPS = (0, 2, 1, 3)
VMEM_LIMIT = 24 * 1024 * 1024


def params(*semantics):
    return pltpu.CompilerParams(
        dimension_semantics=semantics or None, vmem_limit_bytes=VMEM_LIMIT
    )


def cost(flops, nbytes, trans=0):
    return pl.CostEstimate(flops=flops, bytes_accessed=nbytes, transcendentals=trans)


def pack_kernel(slots, slot, k_ref, v_ref, *refs):
    out = refs[-1]
    for half in range(2):
        c = (half * slots + slot) * HDIM
        out[0, half] = jnp.concatenate([k_ref[:, c : c + HDIM], v_ref[:, c : c + HDIM]], axis=1)


def pack(keys, values, groups, slots, slot, *after):
    rows, feats = keys.shape
    part = rows // groups
    block = pl.BlockSpec((part, feats), lambda i: (i, 0))
    return pl.pallas_call(
        functools.partial(pack_kernel, slots, slot),
        grid=(groups,),
        in_specs=[block, block] + [pl.BlockSpec(memory_space=pl.ANY)] * len(after),
        out_specs=pl.BlockSpec((1, 2, part, 2 * HDIM), lambda i: (i, 0, 0, 0)),
        out_shape=jax.ShapeDtypeStruct((groups, 2, part, 2 * HDIM), BF),
        compiler_params=params("arbitrary"),
        cost_estimate=cost(0, 3 * rows * feats * 2),
    )(keys, values, *after)


def gate_kernel(x_ref, after_ref, out_ref):
    pass


def gate(x, after):
    hbm = pl.BlockSpec(memory_space=pltpu.HBM)
    return pl.pallas_call(
        gate_kernel,
        in_specs=[hbm] * 2,
        out_specs=hbm,
        out_shape=jax.ShapeDtypeStruct(x.shape, x.dtype),
        input_output_aliases={0: 0},
        compiler_params=params(),
    )(x, after)


def order_kernel(idx_ref, arr_ref, *refs):
    kv_ref, kvt_ref, arrt, hot = refs[-4:]
    rows = arrt.shape[1]
    arr = arr_ref[...].reshape(rows, arrt.shape[0])
    for j in range(0, rows, 256):
        arrt[:, j : j + 256] = arr[j : j + 256].T
    idx = idx_ref[0]
    iota = lax.broadcasted_iota(jnp.int32, (256, rows), 0).astype(F32).astype(BF)
    for j in range(0, rows, 256):
        near = idx - j
        near = jnp.where((near >= 0) & (near < 256), near, -1).astype(F32).astype(BF)
        hot[j : j + 256] = jnp.where(iota == near, BF(1), BF(0))
    acc = jnp.dot(arrt[...], hot[...], preferred_element_type=F32)
    kvt_ref[...] = acc.astype(BF)
    kv_ref[...] = acc.T.astype(BF)


def put_in_order(arrived, index, rows, *after):
    sources, twice, width = arrived.shape
    return pl.pallas_call(
        order_kernel,
        grid=(2,),
        in_specs=[
            pl.BlockSpec((1, 1, rows), lambda u: (u, 0, 0)),
            pl.BlockSpec((sources, twice // 2, width), lambda u: (0, u, 0)),
        ]
        + [pl.BlockSpec(memory_space=pl.ANY)] * len(after),
        out_specs=[
            pl.BlockSpec((rows, width), lambda u: (u, 0)),
            pl.BlockSpec((width, rows), lambda u: (0, u)),
        ],
        out_shape=[
            jax.ShapeDtypeStruct((2 * rows, width), BF),
            jax.ShapeDtypeStruct((width, 2 * rows), BF),
        ],
        scratch_shapes=[pltpu.VMEM((width, rows), BF), pltpu.VMEM((rows, rows), BF)],
        compiler_params=params("arbitrary"),
        cost_estimate=cost(4 * rows * rows * width, 6 * rows * width * 2),
    )(index.reshape(2, 1, rows), arrived, *after)


def student_kernel(slots, place_ref, here_ref, there_ref, w_ref, q_ref, band_ref, mine_ref, give_ref):
    rows, feats = q_ref.shape
    half, clip = place_ref[0], place_ref[1]
    total = None
    for i, ref in enumerate((here_ref, here_ref, there_ref, there_ref)):
        c = pl.multiple_of((clip ^ CLIPS[i]) * feats, feats)
        part = lax.dot_general(
            ref[i % 2], w_ref[:, pl.ds(c, feats)], NT, preferred_element_type=F32
        )
        total = part if total is None else total + part
    g = total.astype(BF)
    q = q_ref[...] * BF(1.0 / math.sqrt(HDIM))
    heads = []
    for y in range(2):
        cols = []
        for s in range(slots):
            c = (y * slots + s) * HDIM
            cols += [q[:, c : c + HDIM], g[:, c : c + HDIM]]
        heads.append(jnp.concatenate(cols, axis=1))
    mine_ref[:rows] = jnp.where(half == 0, heads[0], heads[1])
    give_ref[:rows] = jnp.where(half == 0, heads[1], heads[0])
    mine_ref[rows:] = band_ref[...]
    give_ref[rows:] = band_ref[...]


def student_side(place, here, there, weight, query, band, slots):
    rows, feats = query.shape
    vm = pl.BlockSpec(memory_space=pltpu.VMEM)
    return pl.pallas_call(
        functools.partial(student_kernel, slots),
        in_specs=[pl.BlockSpec(memory_space=pltpu.SMEM)] + [vm] * 5,
        out_specs=[vm] * 2,
        out_shape=[jax.ShapeDtypeStruct((rows + band.shape[0], 2 * slots * HDIM), BF)] * 2,
        compiler_params=params(),
        cost_estimate=cost(8 * rows * feats * feats, 16 * rows * feats),
    )(place, here, there, weight, query, band)


def cotangent_kernel(place_ref, here_ref, there_ref, after_ref, out_ref):
    cols = here_ref.shape[2]
    for i, ref in enumerate((here_ref, here_ref, there_ref, there_ref)):
        c = pl.multiple_of((place_ref[1] ^ CLIPS[i]) * cols, cols)
        out_ref[:, pl.ds(c, cols)] = ref[i % 2]


def whole_cotangent(place, here, there, after):
    _, rows, cols = here.shape
    vm = pl.BlockSpec(memory_space=pltpu.VMEM)
    return pl.pallas_call(
        cotangent_kernel,
        in_specs=[
            pl.BlockSpec(memory_space=pltpu.SMEM),
            vm,
            vm,
            pl.BlockSpec(memory_space=pl.ANY),
        ],
        out_specs=vm,
        out_shape=jax.ShapeDtypeStruct((rows, 4 * cols), BF),
        compiler_params=params(),
        cost_estimate=cost(0, 16 * rows * cols),
    )(place, here, there, after)


def edge_kernel(place_ref, mine_ref, peer_ref, after_ref, a_ref, b_ref):
    first = place_ref[0] == 0
    mine, peer = mine_ref[...], peer_ref[...]
    a_ref[...] = jnp.where(first, mine, peer)
    b_ref[...] = jnp.where(first, peer, mine)


def edges(place, mine, peer, after):
    vm = pl.BlockSpec(memory_space=pltpu.VMEM)
    return pl.pallas_call(
        edge_kernel,
        in_specs=[
            pl.BlockSpec(memory_space=pltpu.SMEM),
            vm,
            vm,
            pl.BlockSpec(memory_space=pl.ANY),
        ],
        out_specs=[vm] * 2,
        out_shape=[jax.ShapeDtypeStruct(mine.shape, BF)] * 2,
        compiler_params=params(),
        cost_estimate=cost(0, 8 * mine.size),
    )(place, mine, peer, after)


def tails_kernel(left_ref, right_ref, after_ref, out_ref):
    n = out_ref.shape[0] // 2
    out_ref[:n] = left_ref[left_ref.shape[0] - n :]
    out_ref[n:] = right_ref[right_ref.shape[0] - n :]


def tails(left, right, count, after):
    vm = pl.BlockSpec(memory_space=pltpu.VMEM)
    return pl.pallas_call(
        tails_kernel,
        in_specs=[vm, vm, pl.BlockSpec(memory_space=pl.ANY)],
        out_specs=vm,
        out_shape=jax.ShapeDtypeStruct((2 * count, left.shape[1]), BF),
        compiler_params=params(),
        cost_estimate=cost(0, 8 * count * left.shape[1]),
    )(left, right, after)


def split3(x):
    a = x.astype(BF).astype(F32)
    b = (x - a).astype(BF).astype(F32)
    c = (x - a - b).astype(BF).astype(F32)
    return [a, b, c]


def attend_kernel(slots, tiles, by_exchange, place_ref, lohi_ref, qga_ref, qgb_ref, *refs):
    outa_ref, outb_ref = refs[-2 * tiles - 2 : -2 * tiles]
    s_refs, d_refs = refs[-2 * tiles : -tiles], refs[-tiles:]
    rows = outa_ref.shape[1]
    blocks = refs[0].shape[0] // TBLK
    nblk = TILE // SBLK
    cblk = CHUNK // TBLK
    lane = lax.broadcasted_iota(jnp.int32, (1, TILE), 1)
    rhs_lane = lax.broadcasted_iota(jnp.int32, (TILE, 2 * HDIM), 1)
    row_id = lax.broadcasted_iota(jnp.int32, (STATS, TILE), 0)
    z8 = jnp.zeros((8, TILE), F32)
    odd = place_ref[2] % 2 == 1

    def stores(place, out):
        def first():
            outa_ref[place] = out

        def second():
            outb_ref[place] = out

        return first, second

    for (i, slot), (u, q_ref) in itertools.product(
        enumerate(slots), ((0, qga_ref), (1, qgb_ref))
    ):
        kv_ref, kvt_ref = refs[2 * i : 2 * i + 2]
        own = slice(slot * 2 * HDIM, (slot + 1) * 2 * HDIM)
        out_rows = slice(i * OUT, (i + 1) * OUT)

        def group(g, carry):
            held = []
            n = jnp.int32(0)
            for k in range(tiles):
                t = g * tiles + k
                base = u * (rows // SBLK) + t * nblk
                los = [lohi_ref[0, base + i] for i in range(nblk)]
                his = [lohi_ref[1, base + i] for i in range(nblk)]
                lo, hi = los[0], his[0]
                lo_lane = jnp.full((1, TILE), los[0])
                hi_lane = jnp.full((1, TILE), his[0])
                for i in range(1, nblk):
                    lo = jnp.minimum(lo, los[i])
                    hi = jnp.maximum(hi, his[i])
                    lo_lane = jnp.where(lane < i * SBLK, lo_lane, los[i])
                    hi_lane = jnp.where(lane < i * SBLK, hi_lane, his[i])
                lo = jnp.maximum(lo, 0)
                hi = jnp.minimum(hi, blocks - 1)
                n = jnp.maximum(n, jnp.maximum(hi - lo + cblk, 0) // cblk)
                r = pl.multiple_of(t * TILE, TILE)
                qg = q_ref[pl.ds(r, TILE), own]
                zero = jnp.zeros_like(qg)
                rhs = jnp.concatenate(
                    [
                        jnp.where(rhs_lane < HDIM, qg, zero),
                        jnp.where(rhs_lane < HDIM, zero, qg),
                    ],
                    axis=0,
                )
                held.append((lo, lo_lane, hi_lane, rhs, r))

            def start(i, lo):
                kb = jnp.minimum(lo + i * cblk, blocks - cblk)
                return kb, pl.multiple_of(kb * TBLK, TBLK)

            def scores(i, tops):
                s0 = pl.multiple_of(i * CHUNK, CHUNK)
                new = []
                for k, (lo, lo_lane, hi_lane, rhs, _) in enumerate(held):
                    kb0, k0 = start(i, lo)
                    low = jnp.maximum(lo_lane, lo + i * cblk)
                    sd = lax.dot_general(
                        kv_ref[pl.ds(k0, CHUNK), :], rhs, NT, preferred_element_type=F32
                    )
                    d_refs[k][pl.ds(s0, CHUNK), :] = sd[:, TILE:]
                    m = tops[k]
                    for b in range(cblk):
                        ok = (low <= kb0 + b) & (hi_lane >= kb0 + b)
                        s = jnp.where(ok, sd[b * TBLK : (b + 1) * TBLK, :TILE], NEG)
                        s_refs[k][pl.ds(s0 + b * TBLK, TBLK), :] = s
                        m = jnp.maximum(m, jnp.max(s.reshape(TBLK // 8, 8, TILE), axis=0))
                    new.append(m)
                return tuple(new)

            tops = lax.fori_loop(
                0, n, scores, tuple(jnp.full((8, TILE), NEG, F32) for _ in range(tiles))
            )
            tops = [jnp.max(m, axis=0, keepdims=True) for m in tops]

            def expo(i, sums):
                s0 = pl.multiple_of(i * CHUNK, CHUNK)
                new = []
                for k in range(tiles):
                    l, dl = sums[k]
                    p = jnp.exp(s_refs[k][pl.ds(s0, CHUNK), :] - tops[k])
                    s_refs[k][pl.ds(s0, CHUNK), :] = p
                    l = l + jnp.sum(p.reshape(CHUNK // 8, 8, TILE), axis=0)
                    pd = p * d_refs[k][pl.ds(s0, CHUNK), :]
                    dl = dl + jnp.sum(pd.reshape(CHUNK // 8, 8, TILE), axis=0)
                    new.append((l, dl))
                return tuple(new)

            ends = []
            for l, dl in lax.fori_loop(0, n, expo, ((z8, z8),) * tiles):
                l = jnp.sum(l, axis=0, keepdims=True)
                inv = 1.0 / jnp.maximum(l, 1e-30)
                ends.append((l, inv, jnp.sum(dl, axis=0, keepdims=True) * inv))

            def products(i, accs):
                s0 = pl.multiple_of(i * CHUNK, CHUNK)
                new = []
                for k in range(tiles):
                    _, k0 = start(i, held[k][0])
                    p = s_refs[k][pl.ds(s0, CHUNK), :]
                    ds = p * (d_refs[k][pl.ds(s0, CHUNK), :] - ends[k][2])
                    both = jnp.concatenate([p.astype(BF), ds.astype(BF)], axis=1)
                    new.append(
                        accs[k]
                        + jnp.dot(
                            kvt_ref[:, pl.ds(k0, CHUNK)], both, preferred_element_type=F32
                        )
                    )
                return tuple(new)

            accs = lax.fori_loop(
                0, n, products, tuple(jnp.zeros((2 * HDIM, 2 * TILE), F32) for _ in range(tiles))
            )
            for k in range(tiles):
                l, inv, delta = ends[k]
                acc = accs[k] * jnp.concatenate([inv, inv], axis=1)
                stats = jnp.where(row_id == 9, 1.0, 0.0)
                for i, piece in enumerate(split3(tops[k]) + split3(l) + split3(delta)):
                    stats = jnp.where(row_id == i, piece, stats)
                out = jnp.concatenate([acc[:, :TILE], acc[:HDIM, TILE:], stats], axis=0)
                place = (out_rows, pl.ds(held[k][4], TILE))
                out = out.astype(outa_ref.dtype)
                if by_exchange:
                    jax.lax.cond(odd == (u == 0), *stores(place, out))
                else:
                    (outa_ref, outb_ref)[u][place] = out
            return carry

        lax.fori_loop(0, rows // (TILE * tiles), group, 0)


def attend(place, slots, tiles, rows, lohi, qga, qgb, kvs, by_exchange, *after):
    keys = kvs[0].shape[0]
    n = len(slots)
    vm = pl.BlockSpec(memory_space=pltpu.VMEM)
    return pl.pallas_call(
        functools.partial(attend_kernel, slots, tiles, by_exchange),
        in_specs=[pl.BlockSpec(memory_space=pltpu.SMEM)] * 2
        + [vm] * (2 + 2 * n)
        + [pl.BlockSpec(memory_space=pl.ANY)] * len(after),
        out_specs=[vm] * 2,
        out_shape=[jax.ShapeDtypeStruct((n * OUT, rows), BF)] * 2,
        scratch_shapes=[pltpu.VMEM((keys, TILE), F32)] * (2 * tiles),
        compiler_params=params(),
        cost_estimate=cost(
            n * rows * keys * 1024, n * (4 * keys * 128 + 16 * rows * 256), n * rows * keys
        ),
    )(place, lohi, qga, qgb, *kvs, *after)


def combine_kernel(groups, slots, place_ref, cot_ref, pcot_ref, *refs):
    parts, refs = refs[: 2 * slots + 2], refs[2 * slots + 2 :]
    oqa_ref, oqb_ref, shares, buf = refs[0], refs[1], refs[2:-1], refs[-1]
    scale = 1.0 / math.sqrt(HDIM)
    odd = place_ref[2] % 2 == 1
    for u, oq_ref in enumerate((oqa_ref, oqb_ref)):
        for s in range(slots):
            own = parts[2 * s + u][...].astype(F32)
            rem = [r[s * OUT : (s + 1) * OUT] for r in parts[2 * slots :]]
            rem = jnp.where(odd == (u == 0), *rem).astype(F32)

            def stat(x, i):
                r = 3 * HDIM + 3 * i
                return x[r : r + 1] + x[r + 1 : r + 2] + x[r + 2 : r + 3]

            flag = rem[3 * HDIM + 9 : 3 * HDIM + 10]
            m_o, m_r = stat(own, 0), jnp.where(flag > 0.5, stat(rem, 0), NEG)
            l_o, l_r = stat(own, 1), stat(rem, 1)
            d_o, d_r = stat(own, 2), stat(rem, 2)
            top = jnp.maximum(m_o, m_r)
            w_o = l_o * jnp.exp(m_o - top)
            w_r = jnp.where(m_r > 0.5 * NEG, l_r * jnp.exp(m_r - top), 0.0)
            norm = 1.0 / (w_o + w_r)
            w_o, w_r = w_o * norm, w_r * norm
            delta = w_o * d_o + w_r * d_r
            attn = w_o * own[HDIM : 2 * HDIM] + w_r * rem[HDIM : 2 * HDIM]
            s_o, s_r = scale * w_o, scale * w_r
            dq = s_o * own[2 * HDIM : 3 * HDIM] - (s_o * (delta - d_o)) * own[:HDIM]
            dq += s_r * rem[2 * HDIM : 3 * HDIM] - (s_r * (delta - d_r)) * rem[:HDIM]
            oq_ref[s * HDIM : (s + 1) * HDIM] = attn.astype(BF)
            oq_ref[(slots + s) * HDIM : (slots + s + 1) * HDIM] = dq.astype(BF)
    first = place_ref[0] == 0
    attn_a, attn_b = oqa_ref[: slots * HDIM], oqb_ref[: slots * HDIM]
    total = jnp.dot(
        jnp.where(first, attn_a, attn_b), cot_ref[...], preferred_element_type=F32
    )
    total += jnp.dot(
        jnp.where(first, attn_b, attn_a), pcot_ref[...], preferred_element_type=F32
    )
    total = total.astype(BF)
    step = total.shape[1] // groups
    for g in range(groups):
        buf[g] = total[:, g * step : (g + 1) * step]
    for d in range(groups):
        shares[d][...] = buf[place_ref[2] ^ d]


def combine(place, cot, peer_cot, parts, groups, slots):
    rows = parts[0].shape[1]
    width = cot.shape[1]
    vm = pl.BlockSpec(memory_space=pltpu.VMEM)
    share = (slots * HDIM, width // groups)
    return pl.pallas_call(
        functools.partial(combine_kernel, groups, slots),
        in_specs=[pl.BlockSpec(memory_space=pltpu.SMEM)] + [vm] * (4 + 2 * slots),
        out_specs=[vm] * (2 + groups),
        out_shape=[jax.ShapeDtypeStruct((2 * slots * HDIM, rows), BF)] * 2
        + [jax.ShapeDtypeStruct(share, BF)] * groups,
        scratch_shapes=[pltpu.VMEM((groups, *share), BF)],
        compiler_params=params(),
        cost_estimate=cost(
            4 * rows * slots * HDIM * width, 4 * rows * width + 24 * rows * slots * 256
        ),
    )(place, cot, peer_cot, *parts)


def turn_kernel(place_ref, oqa_ref, oqb_ref, mine_ref, give_ref, xmine_ref, xgive_ref):
    width = xmine_ref.shape[1]
    first = place_ref[0] == 0
    a, b = oqa_ref[...], oqb_ref[...]
    mine = jnp.where(first, a, b).T
    give = jnp.where(first, b, a).T
    mine_ref[...] = mine
    give_ref[...] = give
    xmine_ref[...] = mine[:, :width]
    xgive_ref[...] = give[:, :width]


def turn(place, oqa, oqb):
    width, rows = oqa.shape
    vm = pl.BlockSpec(memory_space=pltpu.VMEM)
    return pl.pallas_call(
        turn_kernel,
        in_specs=[pl.BlockSpec(memory_space=pltpu.SMEM)] + [vm] * 2,
        out_specs=[vm] * 4,
        out_shape=[jax.ShapeDtypeStruct((rows, width), BF)] * 2
        + [jax.ShapeDtypeStruct((rows, width // 2), BF)] * 2,
        compiler_params=params(),
        cost_estimate=cost(0, 10 * rows * width),
    )(place, oqa, oqb)


def heads_kernel(place_ref, mine_ref, peer_ref, xmine_ref, xpeer_ref, x_ref, gq_ref):
    first = place_ref[0] == 0
    width = gq_ref.shape[1]

    def put(near, far):
        return jnp.concatenate(
            [jnp.where(first, near, far), jnp.where(first, far, near)], axis=1
        )

    mine, peer = mine_ref[...], peer_ref[...]
    x_ref[:, :width] = put(mine[:, : width // 2], peer[:, : width // 2])
    x_ref[:, width:] = put(xmine_ref[...], xpeer_ref[...])
    gq_ref[...] = put(mine[:, width // 2 :], peer[:, width // 2 :])


def heads(place, mine, peer, xmine, xpeer):
    rows, width = mine.shape
    vm = pl.BlockSpec(memory_space=pltpu.VMEM)
    return pl.pallas_call(
        heads_kernel,
        in_specs=[pl.BlockSpec(memory_space=pltpu.SMEM)] + [vm] * 4,
        out_specs=[vm] * 2,
        out_shape=[
            jax.ShapeDtypeStruct((rows, 2 * width), BF),
            jax.ShapeDtypeStruct((rows, width), BF),
        ],
        compiler_params=params(),
        cost_estimate=cost(0, 12 * rows * width),
    )(place, mine, peer, xmine, xpeer)


def project_kernel(here_ref, there_ref, *refs):
    columns, out_ref, token_ref = refs[:-2], refs[-2], refs[-1]
    token_ref[...] = jnp.zeros_like(token_ref)
    cols = columns[0].shape[0]
    total = None
    for i, w in enumerate(columns):
        ref = (here_ref, there_ref)[i % 2]
        c = i // 2 * cols
        part = jnp.dot(ref[:, c : c + cols], w[...], preferred_element_type=F32)
        total = part if total is None else total + part
    out_ref[...] = total.astype(BF)


def project(here, there, columns):
    rows, cols = here.shape[0], columns[0].shape[1]
    vm = pl.BlockSpec(memory_space=pltpu.VMEM)
    return pl.pallas_call(
        project_kernel,
        in_specs=[vm] * (2 + len(columns)),
        out_specs=[vm] * 2,
        out_shape=[
            jax.ShapeDtypeStruct((rows, cols), BF),
            jax.ShapeDtypeStruct((8, 128), F32),
        ],
        compiler_params=params(),
        cost_estimate=cost(2 * rows * cols * 4 * cols, 12 * rows * cols),
    )(here, there, *columns)


def spread_kernel(groups, place_ref, *refs):
    held, out_ref, buf = refs[:groups], refs[-2], refs[-1]
    _, rows, step = held[0].shape
    for d, ref in enumerate(held):
        buf[d] = ref[...].astype(F32)
    for y in range(2):
        for g in range(groups):
            out_ref[y * rows : (y + 1) * rows, g * step : (g + 1) * step] = buf[
                g ^ place_ref[2], y ^ place_ref[0]
            ]


def spread(place, held, *after):
    groups = len(held)
    _, rows, step = held[0].shape
    vm = pl.BlockSpec(memory_space=pltpu.VMEM)
    return pl.pallas_call(
        functools.partial(spread_kernel, groups),
        in_specs=[pl.BlockSpec(memory_space=pltpu.SMEM)]
        + [vm] * groups
        + [pl.BlockSpec(memory_space=pl.ANY)] * len(after),
        out_specs=vm,
        out_shape=jax.ShapeDtypeStruct((2 * rows, groups * step), F32),
        scratch_shapes=[pltpu.VMEM((groups, 2, rows, step), F32)],
        compiler_params=params(),
        cost_estimate=cost(0, 2 * groups * rows * step * 6),
    )(place, *held, *after)


def on_device(
    groups,
    student_query,
    teacher_key,
    teacher_value,
    clip_order,
    band_start,
    band_end,
    output_weight,
    cotangent,
):
    shards = 2 * groups
    me = lax.axis_index("tm")
    clip = lax.axis_index("clip")
    half = me % 2
    z = me // 2
    place = jnp.stack([half, clip, z]).astype(jnp.int32)
    clips = lax.axis_size("clip")
    teacher_rows = teacher_key.shape[0]
    rows, feats = student_query.shape
    piece = teacher_rows // shards
    slots = feats // HDIM // 2
    hw = slots * HDIM

    def swap(x, d):
        return lax.ppermute(x, "tm", [(i, i ^ d) for i in range(shards)])

    def swap_clip(x, d):
        return lax.ppermute(x, "clip", [(i, i ^ d) for i in range(clips)])

    def swap_both(x, d):
        n = shards * clips
        return lax.ppermute(x, ("tm", "clip"), [(i, i ^ (clips + d)) for i in range(n)])

    def up(x):
        return lax.ppermute(x, "tm", [(i, i + 2) for i in range(shards - 2)])

    def down(x):
        return lax.ppermute(x, "tm", [(i + 2, i) for i in range(shards - 2)])

    here = jnp.stack([cotangent, swap_clip(cotangent, 2)])
    there = swap_clip(here, 1)
    blocks = band_start.shape[0]
    band = jnp.stack([band_start, band_end]).astype(BF)
    band = jnp.pad(band, ((0, 14), (0, 2 * hw - blocks)))
    qg_mine, qg_give = student_side(
        place, here, there, output_weight, student_query, band, slots
    )
    qg_peer = swap(qg_give, 1)
    sent = [pack(teacher_key, teacher_value, groups, slots, 0)]
    sent += [
        gate(pack(teacher_key, teacher_value, groups, slots, s), qg_peer)
        for s in range(1, slots)
    ]
    qga = jnp.where(half == 0, qg_mine, qg_peer)
    qgb = jnp.where(half == 0, qg_peer, qg_mine)

    origin = z * 2 * blocks

    def limits(first_rows, *firsts):
        bands = [x[:2, :blocks] for x in first_rows]
        bands = jnp.concatenate(bands, axis=1).astype(F32).astype(jnp.int32)
        frame = [origin + f + jnp.arange(blocks, dtype=jnp.int32) for f in firsts]
        frame = jnp.concatenate(frame)
        lo = jnp.maximum(frame + bands[0], 0) - origin
        hi = jnp.minimum(frame + bands[1], shards * blocks - 1) - origin
        return jnp.stack([lo, hi])

    own_limits = limits((qga[rows:], qgb[rows:]), 0, blocks)

    def columns_for(d):
        c = (clip ^ d) * feats
        return lax.dynamic_slice_in_dim(output_weight, c, feats, axis=1)

    columns = [columns_for(0)] + [swap_clip(columns_for(d), d) for d in range(1, clips)]

    lookup = lax.dynamic_slice_in_dim(clip_order, z * 2 * teacher_rows, 2 * teacher_rows)
    index = lookup // teacher_rows * piece + lookup % piece

    kvs, parts = [], []
    for s in range(slots):
        arrived = lax.all_to_all(
            sent[s].reshape(shards, 2 * piece, 2 * HDIM), "tm", 0, 0
        )
        kv, kvt = put_in_order(arrived, index, teacher_rows, *parts[-2:-1])
        kvs += [kv, kvt]
        if s == slots - 1:
            count = band.shape[0]
            ends = tails(qg_left, qg_right, count, kvs[-1])
            halo_limits = limits((ends[:count], ends[count:]), -blocks, 2 * blocks)
            far = attend(
                place, range(slots), 2, rows, halo_limits, qg_left, qg_right, kvs, True
            )
        own = place, [s], 4, rows, own_limits, qga, qgb, kvs[-2:], False
        parts += attend(*own, *(far if s == slots - 1 else ()))
        if s == 0:
            edge_a, edge_b = edges(place, qg_mine, qg_peer, kv)
            qg_left, qg_right = up(edge_b), down(edge_a)
            cot = whole_cotangent(place, here, there, parts[0])
    parts += [swap(far[0], 2)]
    links = [(i, i + 2) for i in range(shards - 2) if i // 2 % 2]
    parts += [lax.ppermute(far[1], "tm", links + [(j, i) for i, j in links])]
    oqa, oqb, *got = combine(place, cot, swap(cot, 1), parts, groups, slots)
    mine, give, xmine, xgive = turn(place, oqa, oqb)
    total = got[0].astype(F32)
    for d in range(1, groups):
        total += swap(got[d], 2 * d).astype(F32)
    total = total.astype(BF)
    both = jnp.stack([total, swap(total, 1)])
    held = [both] + [swap(both, 2 * d) for d in range(1, groups)]
    near, grad_query = heads(
        place, mine, swap(give, 1), swap_clip(xmine, 2), swap_both(xgive, 2)
    )
    joined, token = project(near, swap_clip(near, 1), columns)
    return joined, grad_query, spread(place, held, token)


def solution(mesh):
    return jax.shard_map(
        functools.partial(on_device, mesh.shape["tm"] // 2),
        mesh=mesh,
        in_specs=(
            P("tm", "clip"),
            P("tm", "clip"),
            P("tm", "clip"),
            P(),
            P("tm"),
            P("tm"),
            P("clip", None),
            P("tm", "clip"),
        ),
        out_specs=(P("tm", "clip"), P("tm", "clip"), P("clip", None)),
        check_vma=False,
    )
```

```python
import functools
import itertools
import math

import jax
import jax.numpy as jnp
from jax import lax
from jax.experimental import pallas as pl
from jax.experimental.pallas import tpu as pltpu
from jax.sharding import PartitionSpec as P

HDIM = 64
SBLK = 32
TBLK = 128
TILE = 128
CHUNK = 1024
NEG = -1e30
STATS = 16
OUT = 3 * HDIM + STATS
BF = jnp.bfloat16
F32 = jnp.float32
NT = (((1,), (1,)), ((), ()))
CLIPS = (0, 2, 1, 3)
VMEM_LIMIT = 24 * 1024 * 1024


def params(*semantics):
    return pltpu.CompilerParams(
        dimension_semantics=semantics or None, vmem_limit_bytes=VMEM_LIMIT
    )


def cost(flops, nbytes, trans=0):
    return pl.CostEstimate(flops=flops, bytes_accessed=nbytes, transcendentals=trans)


def pack_kernel(slots, slot, k_ref, v_ref, *refs):
    out = refs[-1]
    for half in range(2):
        c = (half * slots + slot) * HDIM
        out[0, half] = jnp.concatenate([k_ref[:, c : c + HDIM], v_ref[:, c : c + HDIM]], axis=1)


def pack(keys, values, groups, slots, slot, *after):
    rows, feats = keys.shape
    part = rows // groups
    block = pl.BlockSpec((part, feats), lambda i: (i, 0))
    return pl.pallas_call(
        functools.partial(pack_kernel, slots, slot),
        grid=(groups,),
        in_specs=[block, block] + [pl.BlockSpec(memory_space=pl.ANY)] * len(after),
        out_specs=pl.BlockSpec((1, 2, part, 2 * HDIM), lambda i: (i, 0, 0, 0)),
        out_shape=jax.ShapeDtypeStruct((groups, 2, part, 2 * HDIM), BF),
        compiler_params=params("arbitrary"),
        cost_estimate=cost(0, 3 * rows * feats * 2),
    )(keys, values, *after)


def gate_kernel(x_ref, after_ref, out_ref):
    pass


def gate(x, after):
    hbm = pl.BlockSpec(memory_space=pltpu.HBM)
    return pl.pallas_call(
        gate_kernel,
        in_specs=[hbm] * 2,
        out_specs=hbm,
        out_shape=jax.ShapeDtypeStruct(x.shape, x.dtype),
        input_output_aliases={0: 0},
        compiler_params=params(),
    )(x, after)


def order_kernel(idx_ref, arr_ref, *refs):
    kv_ref, kvt_ref, arrt, hot = refs[-4:]
    rows = arrt.shape[1]
    arr = arr_ref[...].reshape(rows, arrt.shape[0])
    for j in range(0, rows, 256):
        arrt[:, j : j + 256] = arr[j : j + 256].T
    idx = idx_ref[0]
    iota = lax.broadcasted_iota(jnp.int32, (256, rows), 0).astype(F32).astype(BF)
    for j in range(0, rows, 256):
        near = idx - j
        near = jnp.where((near >= 0) & (near < 256), near, -1).astype(F32).astype(BF)
        hot[j : j + 256] = jnp.where(iota == near, BF(1), BF(0))
    acc = jnp.dot(arrt[...], hot[...], preferred_element_type=F32)
    kvt_ref[...] = acc.astype(BF)
    kv_ref[...] = acc.T.astype(BF)


def put_in_order(arrived, index, rows, *after):
    sources, twice, width = arrived.shape
    return pl.pallas_call(
        order_kernel,
        grid=(2,),
        in_specs=[
            pl.BlockSpec((1, 1, rows), lambda u: (u, 0, 0)),
            pl.BlockSpec((sources, twice // 2, width), lambda u: (0, u, 0)),
        ]
        + [pl.BlockSpec(memory_space=pl.ANY)] * len(after),
        out_specs=[
            pl.BlockSpec((rows, width), lambda u: (u, 0)),
            pl.BlockSpec((width, rows), lambda u: (0, u)),
        ],
        out_shape=[
            jax.ShapeDtypeStruct((2 * rows, width), BF),
            jax.ShapeDtypeStruct((width, 2 * rows), BF),
        ],
        scratch_shapes=[pltpu.VMEM((width, rows), BF), pltpu.VMEM((rows, rows), BF)],
        compiler_params=params("arbitrary"),
        cost_estimate=cost(4 * rows * rows * width, 6 * rows * width * 2),
    )(index.reshape(2, 1, rows), arrived, *after)


def student_kernel(slots, place_ref, here_ref, there_ref, w_ref, q_ref, band_ref, mine_ref, give_ref):
    rows, feats = q_ref.shape
    half, clip = place_ref[0], place_ref[1]
    total = None
    for i, ref in enumerate((here_ref, here_ref, there_ref, there_ref)):
        c = pl.multiple_of((clip ^ CLIPS[i]) * feats, feats)
        part = lax.dot_general(
            ref[i % 2], w_ref[:, pl.ds(c, feats)], NT, preferred_element_type=F32
        )
        total = part if total is None else total + part
    g = total.astype(BF)
    q = q_ref[...] * BF(1.0 / math.sqrt(HDIM))
    heads = []
    for y in range(2):
        cols = []
        for s in range(slots):
            c = (y * slots + s) * HDIM
            cols += [q[:, c : c + HDIM], g[:, c : c + HDIM]]
        heads.append(jnp.concatenate(cols, axis=1))
    mine_ref[:rows] = jnp.where(half == 0, heads[0], heads[1])
    give_ref[:rows] = jnp.where(half == 0, heads[1], heads[0])
    mine_ref[rows:] = band_ref[...]
    give_ref[rows:] = band_ref[...]


def student_side(place, here, there, weight, query, band, slots):
    rows, feats = query.shape
    vm = pl.BlockSpec(memory_space=pltpu.VMEM)
    return pl.pallas_call(
        functools.partial(student_kernel, slots),
        in_specs=[pl.BlockSpec(memory_space=pltpu.SMEM)] + [vm] * 5,
        out_specs=[vm] * 2,
        out_shape=[jax.ShapeDtypeStruct((rows + band.shape[0], 2 * slots * HDIM), BF)] * 2,
        compiler_params=params(),
        cost_estimate=cost(8 * rows * feats * feats, 16 * rows * feats),
    )(place, here, there, weight, query, band)


def cotangent_kernel(place_ref, here_ref, there_ref, after_ref, out_ref):
    cols = here_ref.shape[2]
    for i, ref in enumerate((here_ref, here_ref, there_ref, there_ref)):
        c = pl.multiple_of((place_ref[1] ^ CLIPS[i]) * cols, cols)
        out_ref[:, pl.ds(c, cols)] = ref[i % 2]


def whole_cotangent(place, here, there, after):
    _, rows, cols = here.shape
    vm = pl.BlockSpec(memory_space=pltpu.VMEM)
    return pl.pallas_call(
        cotangent_kernel,
        in_specs=[
            pl.BlockSpec(memory_space=pltpu.SMEM),
            vm,
            vm,
            pl.BlockSpec(memory_space=pl.ANY),
        ],
        out_specs=vm,
        out_shape=jax.ShapeDtypeStruct((rows, 4 * cols), BF),
        compiler_params=params(),
        cost_estimate=cost(0, 16 * rows * cols),
    )(place, here, there, after)


def edge_kernel(place_ref, mine_ref, peer_ref, after_ref, a_ref, b_ref):
    first = place_ref[0] == 0
    mine, peer = mine_ref[...], peer_ref[...]
    a_ref[...] = jnp.where(first, mine, peer)
    b_ref[...] = jnp.where(first, peer, mine)


def edges(place, mine, peer, after):
    vm = pl.BlockSpec(memory_space=pltpu.VMEM)
    return pl.pallas_call(
        edge_kernel,
        in_specs=[
            pl.BlockSpec(memory_space=pltpu.SMEM),
            vm,
            vm,
            pl.BlockSpec(memory_space=pl.ANY),
        ],
        out_specs=[vm] * 2,
        out_shape=[jax.ShapeDtypeStruct(mine.shape, BF)] * 2,
        compiler_params=params(),
        cost_estimate=cost(0, 8 * mine.size),
    )(place, mine, peer, after)


def tails_kernel(left_ref, right_ref, after_ref, out_ref):
    out_ref[0] = left_ref[...]
    out_ref[1] = right_ref[...]


def tails(left, right, count, after):
    width = left.shape[1]
    last = pl.BlockSpec((count, width), lambda i: (left.shape[0] // count - 1, 0))
    return pl.pallas_call(
        tails_kernel,
        grid=(1,),
        in_specs=[last, last, pl.BlockSpec(memory_space=pl.ANY)],
        out_specs=pl.BlockSpec((2, count, width), lambda i: (0, 0, 0)),
        out_shape=jax.ShapeDtypeStruct((2, count, width), BF),
        compiler_params=params("arbitrary"),
        cost_estimate=cost(0, 8 * count * width),
    )(left, right, after)


def split3(x):
    a = x.astype(BF).astype(F32)
    b = (x - a).astype(BF).astype(F32)
    c = (x - a - b).astype(BF).astype(F32)
    return [a, b, c]


def attend_kernel(slots, tiles, by_exchange, place_ref, lohi_ref, qga_ref, qgb_ref, *refs):
    outa_ref, outb_ref = refs[-2 * tiles - 2 : -2 * tiles]
    s_refs, d_refs = refs[-2 * tiles : -tiles], refs[-tiles:]
    rows = outa_ref.shape[1]
    blocks = refs[0].shape[0] // TBLK
    nblk = TILE // SBLK
    cblk = CHUNK // TBLK
    lane = lax.broadcasted_iota(jnp.int32, (1, TILE), 1)
    rhs_lane = lax.broadcasted_iota(jnp.int32, (TILE, 2 * HDIM), 1)
    row_id = lax.broadcasted_iota(jnp.int32, (STATS, TILE), 0)
    z8 = jnp.zeros((8, TILE), F32)
    odd = place_ref[2] % 2 == 1

    def stores(place, out):
        def first():
            outa_ref[place] = out

        def second():
            outb_ref[place] = out

        return first, second

    for (i, slot), (u, q_ref) in itertools.product(
        enumerate(slots), ((0, qga_ref), (1, qgb_ref))
    ):
        kv_ref, kvt_ref = refs[2 * i : 2 * i + 2]
        own = slice(slot * 2 * HDIM, (slot + 1) * 2 * HDIM)
        out_rows = slice(i * OUT, (i + 1) * OUT)

        def group(g, carry):
            held = []
            n = jnp.int32(0)
            for k in range(tiles):
                t = g * tiles + k
                base = u * (rows // SBLK) + t * nblk
                los = [lohi_ref[0, base + i] for i in range(nblk)]
                his = [lohi_ref[1, base + i] for i in range(nblk)]
                lo, hi = los[0], his[0]
                lo_lane = jnp.full((1, TILE), los[0])
                hi_lane = jnp.full((1, TILE), his[0])
                for i in range(1, nblk):
                    lo = jnp.minimum(lo, los[i])
                    hi = jnp.maximum(hi, his[i])
                    lo_lane = jnp.where(lane < i * SBLK, lo_lane, los[i])
                    hi_lane = jnp.where(lane < i * SBLK, hi_lane, his[i])
                lo = jnp.maximum(lo, 0)
                hi = jnp.minimum(hi, blocks - 1)
                n = jnp.maximum(n, jnp.maximum(hi - lo + cblk, 0) // cblk)
                r = pl.multiple_of(t * TILE, TILE)
                qg = q_ref[pl.ds(r, TILE), own]
                zero = jnp.zeros_like(qg)
                rhs = jnp.concatenate(
                    [
                        jnp.where(rhs_lane < HDIM, qg, zero),
                        jnp.where(rhs_lane < HDIM, zero, qg),
                    ],
                    axis=0,
                )
                held.append((lo, lo_lane, hi_lane, rhs, r))

            def start(i, lo):
                kb = jnp.minimum(lo + i * cblk, blocks - cblk)
                return kb, pl.multiple_of(kb * TBLK, TBLK)

            def scores(i, tops):
                s0 = pl.multiple_of(i * CHUNK, CHUNK)
                new = []
                for k, (lo, lo_lane, hi_lane, rhs, _) in enumerate(held):
                    kb0, k0 = start(i, lo)
                    low = jnp.maximum(lo_lane, lo + i * cblk)
                    sd = lax.dot_general(
                        kv_ref[pl.ds(k0, CHUNK), :], rhs, NT, preferred_element_type=F32
                    )
                    d_refs[k][pl.ds(s0, CHUNK), :] = sd[:, TILE:]
                    m = tops[k]
                    for b in range(cblk):
                        ok = (low <= kb0 + b) & (hi_lane >= kb0 + b)
                        s = jnp.where(ok, sd[b * TBLK : (b + 1) * TBLK, :TILE], NEG)
                        s_refs[k][pl.ds(s0 + b * TBLK, TBLK), :] = s
                        m = jnp.maximum(m, jnp.max(s.reshape(TBLK // 8, 8, TILE), axis=0))
                    new.append(m)
                return tuple(new)

            tops = lax.fori_loop(
                0, n, scores, tuple(jnp.full((8, TILE), NEG, F32) for _ in range(tiles))
            )
            tops = [jnp.max(m, axis=0, keepdims=True) for m in tops]

            def expo(i, sums):
                s0 = pl.multiple_of(i * CHUNK, CHUNK)
                new = []
                for k in range(tiles):
                    l, dl = sums[k]
                    p = jnp.exp(s_refs[k][pl.ds(s0, CHUNK), :] - tops[k])
                    s_refs[k][pl.ds(s0, CHUNK), :] = p
                    l = l + jnp.sum(p.reshape(CHUNK // 8, 8, TILE), axis=0)
                    pd = p * d_refs[k][pl.ds(s0, CHUNK), :]
                    dl = dl + jnp.sum(pd.reshape(CHUNK // 8, 8, TILE), axis=0)
                    new.append((l, dl))
                return tuple(new)

            ends = []
            for l, dl in lax.fori_loop(0, n, expo, ((z8, z8),) * tiles):
                l = jnp.sum(l, axis=0, keepdims=True)
                inv = 1.0 / jnp.maximum(l, 1e-30)
                ends.append((l, inv, jnp.sum(dl, axis=0, keepdims=True) * inv))

            def products(i, accs):
                s0 = pl.multiple_of(i * CHUNK, CHUNK)
                new = []
                for k in range(tiles):
                    _, k0 = start(i, held[k][0])
                    p = s_refs[k][pl.ds(s0, CHUNK), :]
                    ds = p * (d_refs[k][pl.ds(s0, CHUNK), :] - ends[k][2])
                    both = jnp.concatenate([p.astype(BF), ds.astype(BF)], axis=1)
                    new.append(
                        accs[k]
                        + jnp.dot(
                            kvt_ref[:, pl.ds(k0, CHUNK)], both, preferred_element_type=F32
                        )
                    )
                return tuple(new)

            accs = lax.fori_loop(
                0, n, products, tuple(jnp.zeros((2 * HDIM, 2 * TILE), F32) for _ in range(tiles))
            )
            for k in range(tiles):
                l, inv, delta = ends[k]
                acc = accs[k] * jnp.concatenate([inv, inv], axis=1)
                stats = jnp.where(row_id == 9, 1.0, 0.0)
                for i, piece in enumerate(split3(tops[k]) + split3(l) + split3(delta)):
                    stats = jnp.where(row_id == i, piece, stats)
                out = jnp.concatenate([acc[:, :TILE], acc[:HDIM, TILE:], stats], axis=0)
                place = (out_rows, pl.ds(held[k][4], TILE))
                out = out.astype(outa_ref.dtype)
                if by_exchange:
                    jax.lax.cond(odd == (u == 0), *stores(place, out))
                else:
                    (outa_ref, outb_ref)[u][place] = out
            return carry

        lax.fori_loop(0, rows // (TILE * tiles), group, 0)


def attend(place, slots, tiles, rows, lohi, qga, qgb, kvs, by_exchange, *after):
    keys = kvs[0].shape[0]
    n = len(slots)
    vm = pl.BlockSpec(memory_space=pltpu.VMEM)
    return pl.pallas_call(
        functools.partial(attend_kernel, slots, tiles, by_exchange),
        in_specs=[pl.BlockSpec(memory_space=pltpu.SMEM)] * 2
        + [vm] * (2 + 2 * n)
        + [pl.BlockSpec(memory_space=pl.ANY)] * len(after),
        out_specs=[vm] * 2,
        out_shape=[jax.ShapeDtypeStruct((n * OUT, rows), BF)] * 2,
        scratch_shapes=[pltpu.VMEM((keys, TILE), F32)] * (2 * tiles),
        compiler_params=params(),
        cost_estimate=cost(
            n * rows * keys * 1024, n * (4 * keys * 128 + 16 * rows * 256), n * rows * keys
        ),
    )(place, lohi, qga, qgb, *kvs, *after)


def combine_kernel(groups, slots, place_ref, cot_ref, pcot_ref, *refs):
    parts, refs = refs[: 2 * slots + 2], refs[2 * slots + 2 :]
    oqa_ref, oqb_ref, shares, buf = refs[0], refs[1], refs[2:-1], refs[-1]
    scale = 1.0 / math.sqrt(HDIM)
    odd = place_ref[2] % 2 == 1
    for u, oq_ref in enumerate((oqa_ref, oqb_ref)):
        for s in range(slots):
            own = parts[2 * s + u][...].astype(F32)
            rem = [r[s * OUT : (s + 1) * OUT] for r in parts[2 * slots :]]
            rem = jnp.where(odd == (u == 0), *rem).astype(F32)

            def stat(x, i):
                r = 3 * HDIM + 3 * i
                return x[r : r + 1] + x[r + 1 : r + 2] + x[r + 2 : r + 3]

            flag = rem[3 * HDIM + 9 : 3 * HDIM + 10]
            m_o, m_r = stat(own, 0), jnp.where(flag > 0.5, stat(rem, 0), NEG)
            l_o, l_r = stat(own, 1), stat(rem, 1)
            d_o, d_r = stat(own, 2), stat(rem, 2)
            top = jnp.maximum(m_o, m_r)
            w_o = l_o * jnp.exp(m_o - top)
            w_r = jnp.where(m_r > 0.5 * NEG, l_r * jnp.exp(m_r - top), 0.0)
            norm = 1.0 / (w_o + w_r)
            w_o, w_r = w_o * norm, w_r * norm
            delta = w_o * d_o + w_r * d_r
            attn = w_o * own[HDIM : 2 * HDIM] + w_r * rem[HDIM : 2 * HDIM]
            s_o, s_r = scale * w_o, scale * w_r
            dq = s_o * own[2 * HDIM : 3 * HDIM] - (s_o * (delta - d_o)) * own[:HDIM]
            dq += s_r * rem[2 * HDIM : 3 * HDIM] - (s_r * (delta - d_r)) * rem[:HDIM]
            oq_ref[s * HDIM : (s + 1) * HDIM] = attn.astype(BF)
            oq_ref[(slots + s) * HDIM : (slots + s + 1) * HDIM] = dq.astype(BF)
    first = place_ref[0] == 0
    attn_a, attn_b = oqa_ref[: slots * HDIM], oqb_ref[: slots * HDIM]
    total = jnp.dot(
        jnp.where(first, attn_a, attn_b), cot_ref[...], preferred_element_type=F32
    )
    total += jnp.dot(
        jnp.where(first, attn_b, attn_a), pcot_ref[...], preferred_element_type=F32
    )
    total = total.astype(BF)
    step = total.shape[1] // groups
    for g in range(groups):
        buf[g] = total[:, g * step : (g + 1) * step]
    for d in range(groups):
        shares[d][...] = buf[place_ref[2] ^ d]


def combine(place, cot, peer_cot, parts, groups, slots):
    rows = parts[0].shape[1]
    width = cot.shape[1]
    vm = pl.BlockSpec(memory_space=pltpu.VMEM)
    share = (slots * HDIM, width // groups)
    return pl.pallas_call(
        functools.partial(combine_kernel, groups, slots),
        in_specs=[pl.BlockSpec(memory_space=pltpu.SMEM)] + [vm] * (4 + 2 * slots),
        out_specs=[vm] * (2 + groups),
        out_shape=[jax.ShapeDtypeStruct((2 * slots * HDIM, rows), BF)] * 2
        + [jax.ShapeDtypeStruct(share, BF)] * groups,
        scratch_shapes=[pltpu.VMEM((groups, *share), BF)],
        compiler_params=params(),
        cost_estimate=cost(
            4 * rows * slots * HDIM * width, 4 * rows * width + 24 * rows * slots * 256
        ),
    )(place, cot, peer_cot, *parts)


def turn_kernel(place_ref, oqa_ref, oqb_ref, mine_ref, give_ref, xmine_ref, xgive_ref):
    width = xmine_ref.shape[1]
    first = place_ref[0] == 0
    a, b = oqa_ref[...], oqb_ref[...]
    mine = jnp.where(first, a, b).T
    give = jnp.where(first, b, a).T
    mine_ref[...] = mine
    give_ref[...] = give
    xmine_ref[...] = mine[:, :width]
    xgive_ref[...] = give[:, :width]


def turn(place, oqa, oqb):
    width, rows = oqa.shape
    vm = pl.BlockSpec(memory_space=pltpu.VMEM)
    return pl.pallas_call(
        turn_kernel,
        in_specs=[pl.BlockSpec(memory_space=pltpu.SMEM)] + [vm] * 2,
        out_specs=[vm] * 4,
        out_shape=[jax.ShapeDtypeStruct((rows, width), BF)] * 2
        + [jax.ShapeDtypeStruct((rows, width // 2), BF)] * 2,
        compiler_params=params(),
        cost_estimate=cost(0, 10 * rows * width),
    )(place, oqa, oqb)


def heads_kernel(place_ref, mine_ref, peer_ref, xmine_ref, xpeer_ref, x_ref, gq_ref):
    first = place_ref[0] == 0
    width = gq_ref.shape[1]

    def put(near, far):
        return jnp.concatenate(
            [jnp.where(first, near, far), jnp.where(first, far, near)], axis=1
        )

    mine, peer = mine_ref[...], peer_ref[...]
    x_ref[:, :width] = put(mine[:, : width // 2], peer[:, : width // 2])
    x_ref[:, width:] = put(xmine_ref[...], xpeer_ref[...])
    gq_ref[...] = put(mine[:, width // 2 :], peer[:, width // 2 :])


def heads(place, mine, peer, xmine, xpeer):
    rows, width = mine.shape
    vm = pl.BlockSpec(memory_space=pltpu.VMEM)
    return pl.pallas_call(
        heads_kernel,
        in_specs=[pl.BlockSpec(memory_space=pltpu.SMEM)] + [vm] * 4,
        out_specs=[vm] * 2,
        out_shape=[
            jax.ShapeDtypeStruct((rows, 2 * width), BF),
            jax.ShapeDtypeStruct((rows, width), BF),
        ],
        compiler_params=params(),
        cost_estimate=cost(0, 12 * rows * width),
    )(place, mine, peer, xmine, xpeer)


def project_kernel(here_ref, there_ref, *refs):
    columns, out_ref, token_ref = refs[:-2], refs[-2], refs[-1]
    token_ref[...] = jnp.zeros_like(token_ref)
    cols = columns[0].shape[0]
    total = None
    for i, w in enumerate(columns):
        ref = (here_ref, there_ref)[i % 2]
        c = i // 2 * cols
        part = jnp.dot(ref[:, c : c + cols], w[...], preferred_element_type=F32)
        total = part if total is None else total + part
    out_ref[...] = total.astype(BF)


def project(here, there, columns):
    rows, cols = here.shape[0], columns[0].shape[1]
    vm = pl.BlockSpec(memory_space=pltpu.VMEM)
    return pl.pallas_call(
        project_kernel,
        in_specs=[vm] * (2 + len(columns)),
        out_specs=[vm] * 2,
        out_shape=[
            jax.ShapeDtypeStruct((rows, cols), BF),
            jax.ShapeDtypeStruct((8, 128), F32),
        ],
        compiler_params=params(),
        cost_estimate=cost(2 * rows * cols * 4 * cols, 12 * rows * cols),
    )(here, there, *columns)


def spread_kernel(groups, place_ref, *refs):
    held, out_ref, buf = refs[:groups], refs[-2], refs[-1]
    step = held[0].shape[2]
    y = pl.program_id(0) ^ place_ref[0]
    for d, ref in enumerate(held):
        buf[d] = ref[y].astype(F32)
    for g in range(groups):
        out_ref[:, g * step : (g + 1) * step] = buf[g ^ place_ref[2]]


def spread(place, held, *after):
    groups = len(held)
    _, rows, step = held[0].shape
    whole = pl.BlockSpec(held[0].shape, lambda i: (0, 0, 0))
    return pl.pallas_call(
        functools.partial(spread_kernel, groups),
        grid=(2,),
        in_specs=[pl.BlockSpec(memory_space=pltpu.SMEM)]
        + [whole] * groups
        + [pl.BlockSpec(memory_space=pl.ANY)] * len(after),
        out_specs=pl.BlockSpec((rows, groups * step), lambda i: (i, 0)),
        out_shape=jax.ShapeDtypeStruct((2 * rows, groups * step), F32),
        scratch_shapes=[pltpu.VMEM((groups, rows, step), F32)],
        compiler_params=params("arbitrary"),
        cost_estimate=cost(0, 2 * groups * rows * step * 6),
    )(place, *held, *after)


def on_device(
    groups,
    student_query,
    teacher_key,
    teacher_value,
    clip_order,
    band_start,
    band_end,
    output_weight,
    cotangent,
):
    shards = 2 * groups
    me = lax.axis_index("tm")
    clip = lax.axis_index("clip")
    half = me % 2
    z = me // 2
    place = jnp.stack([half, clip, z]).astype(jnp.int32)
    clips = lax.axis_size("clip")
    teacher_rows = teacher_key.shape[0]
    rows, feats = student_query.shape
    piece = teacher_rows // shards
    slots = feats // HDIM // 2
    hw = slots * HDIM

    def swap(x, d):
        return lax.ppermute(x, "tm", [(i, i ^ d) for i in range(shards)])

    def swap_clip(x, d):
        return lax.ppermute(x, "clip", [(i, i ^ d) for i in range(clips)])

    def swap_both(x, d):
        n = shards * clips
        return lax.ppermute(x, ("tm", "clip"), [(i, i ^ (clips + d)) for i in range(n)])

    def up(x):
        return lax.ppermute(x, "tm", [(i, i + 2) for i in range(shards - 2)])

    def down(x):
        return lax.ppermute(x, "tm", [(i + 2, i) for i in range(shards - 2)])

    here = jnp.stack([cotangent, swap_clip(cotangent, 2)])
    there = swap_clip(here, 1)
    blocks = band_start.shape[0]
    band = jnp.stack([band_start, band_end]).astype(BF)
    band = jnp.pad(band, ((0, 14), (0, 2 * hw - blocks)))
    qg_mine, qg_give = student_side(
        place, here, there, output_weight, student_query, band, slots
    )
    qg_peer = swap(qg_give, 1)
    sent = [pack(teacher_key, teacher_value, groups, slots, 0)]
    sent += [
        gate(pack(teacher_key, teacher_value, groups, slots, s), qg_peer)
        for s in range(1, slots)
    ]
    qga = jnp.where(half == 0, qg_mine, qg_peer)
    qgb = jnp.where(half == 0, qg_peer, qg_mine)

    origin = z * 2 * blocks

    def limits(first_rows, *firsts):
        bands = [x[:2, :blocks] for x in first_rows]
        bands = jnp.concatenate(bands, axis=1).astype(F32).astype(jnp.int32)
        frame = [origin + f + jnp.arange(blocks, dtype=jnp.int32) for f in firsts]
        frame = jnp.concatenate(frame)
        lo = jnp.maximum(frame + bands[0], 0) - origin
        hi = jnp.minimum(frame + bands[1], shards * blocks - 1) - origin
        return jnp.stack([lo, hi])

    own_limits = limits((qga[rows:], qgb[rows:]), 0, blocks)

    def columns_for(d):
        c = (clip ^ d) * feats
        return lax.dynamic_slice_in_dim(output_weight, c, feats, axis=1)

    columns = [columns_for(0)] + [swap_clip(columns_for(d), d) for d in range(1, clips)]

    lookup = lax.dynamic_slice_in_dim(clip_order, z * 2 * teacher_rows, 2 * teacher_rows)
    index = lookup // teacher_rows * piece + lookup % piece

    kvs, parts = [], []
    for s in range(slots):
        arrived = lax.all_to_all(
            sent[s].reshape(shards, 2 * piece, 2 * HDIM), "tm", 0, 0
        )
        kv, kvt = put_in_order(arrived, index, teacher_rows, *parts[-2:-1])
        kvs += [kv, kvt]
        if s == slots - 1:
            count = band.shape[0]
            ends = tails(qg_left, qg_right, count, kvs[-1])
            halo_limits = limits(ends, -blocks, 2 * blocks)
            far = attend(
                place, range(slots), 2, rows, halo_limits, qg_left, qg_right, kvs, True
            )
        own = place, [s], 4, rows, own_limits, qga, qgb, kvs[-2:], False
        parts += attend(*own, *(far if s == slots - 1 else ()))
        if s == 0:
            edge_a, edge_b = edges(place, qg_mine, qg_peer, kv)
            qg_left, qg_right = up(edge_b), down(edge_a)
            cot = whole_cotangent(place, here, there, parts[0])
    parts += [swap(far[0], 2)]
    links = [(i, i + 2) for i in range(shards - 2) if i // 2 % 2]
    parts += [lax.ppermute(far[1], "tm", links + [(j, i) for i, j in links])]
    oqa, oqb, *got = combine(place, cot, swap(cot, 1), parts, groups, slots)
    mine, give, xmine, xgive = turn(place, oqa, oqb)
    total = got[0].astype(F32)
    for d in range(1, groups):
        total += swap(got[d], 2 * d).astype(F32)
    total = total.astype(BF)
    both = jnp.stack([total, swap(total, 1)])
    held = [both] + [swap(both, 2 * d) for d in range(1, groups)]
    near, grad_query = heads(
        place, mine, swap(give, 1), swap_clip(xmine, 2), swap_both(xgive, 2)
    )
    joined, token = project(near, swap_clip(near, 1), columns)
    return joined, grad_query, spread(place, held, token)


def solution(mesh):
    return jax.shard_map(
        functools.partial(on_device, mesh.shape["tm"] // 2),
        mesh=mesh,
        in_specs=(
            P("tm", "clip"),
            P("tm", "clip"),
            P("tm", "clip"),
            P(),
            P("tm"),
            P("tm"),
            P("clip", None),
            P("tm", "clip"),
        ),
        out_specs=(P("tm", "clip"), P("tm", "clip"), P("clip", None)),
        check_vma=False,
    )
```

```python
import functools
import itertools
import math

import jax
import jax.numpy as jnp
from jax import lax
from jax.experimental import pallas as pl
from jax.experimental.pallas import tpu as pltpu
from jax.sharding import PartitionSpec as P

HDIM = 64
SBLK = 32
TBLK = 128
TILE = 128
CHUNK = 1024
NEG = -1e30
STATS = 16
OUT = 3 * HDIM + STATS
BF = jnp.bfloat16
F32 = jnp.float32
NT = (((1,), (1,)), ((), ()))
CLIPS = (0, 2, 1, 3)
VMEM_LIMIT = 24 * 1024 * 1024


def params(*semantics):
    return pltpu.CompilerParams(
        dimension_semantics=semantics or None, vmem_limit_bytes=VMEM_LIMIT
    )


def cost(flops, nbytes, trans=0):
    return pl.CostEstimate(flops=flops, bytes_accessed=nbytes, transcendentals=trans)


def pack_kernel(slots, slot, k_ref, v_ref, *refs):
    out = refs[-1]
    for half in range(2):
        c = (half * slots + slot) * HDIM
        out[0, half] = jnp.concatenate([k_ref[:, c : c + HDIM], v_ref[:, c : c + HDIM]], axis=1)


def pack(keys, values, groups, slots, slot, *after):
    rows, feats = keys.shape
    part = rows // groups
    block = pl.BlockSpec((part, feats), lambda i: (i, 0))
    return pl.pallas_call(
        functools.partial(pack_kernel, slots, slot),
        grid=(groups,),
        in_specs=[block, block] + [pl.BlockSpec(memory_space=pl.ANY)] * len(after),
        out_specs=pl.BlockSpec((1, 2, part, 2 * HDIM), lambda i: (i, 0, 0, 0)),
        out_shape=jax.ShapeDtypeStruct((groups, 2, part, 2 * HDIM), BF),
        compiler_params=params("arbitrary"),
        cost_estimate=cost(0, 3 * rows * feats * 2),
    )(keys, values, *after)


def gate_kernel(x_ref, after_ref, out_ref):
    pass


def gate(x, after):
    hbm = pl.BlockSpec(memory_space=pltpu.HBM)
    return pl.pallas_call(
        gate_kernel,
        in_specs=[hbm] * 2,
        out_specs=hbm,
        out_shape=jax.ShapeDtypeStruct(x.shape, x.dtype),
        input_output_aliases={0: 0},
        compiler_params=params(),
    )(x, after)


def order_kernel(idx_ref, arr_ref, *refs):
    kv_ref, kvt_ref, arrt, hot = refs[-4:]
    rows = arrt.shape[1]
    arr = arr_ref[...].reshape(rows, arrt.shape[0])
    for j in range(0, rows, 256):
        arrt[:, j : j + 256] = arr[j : j + 256].T
    idx = idx_ref[0]
    iota = lax.broadcasted_iota(jnp.int32, (256, rows), 0).astype(F32).astype(BF)
    for j in range(0, rows, 256):
        near = idx - j
        near = jnp.where((near >= 0) & (near < 256), near, -1).astype(F32).astype(BF)
        hot[j : j + 256] = jnp.where(iota == near, BF(1), BF(0))
    acc = jnp.dot(arrt[...], hot[...], preferred_element_type=F32)
    kvt_ref[...] = acc.astype(BF)
    kv_ref[...] = acc.T.astype(BF)


def put_in_order(arrived, index, rows, *after):
    sources, twice, width = arrived.shape
    return pl.pallas_call(
        order_kernel,
        grid=(2,),
        in_specs=[
            pl.BlockSpec((1, 1, rows), lambda u: (u, 0, 0)),
            pl.BlockSpec((sources, twice // 2, width), lambda u: (0, u, 0)),
        ]
        + [pl.BlockSpec(memory_space=pl.ANY)] * len(after),
        out_specs=[
            pl.BlockSpec((rows, width), lambda u: (u, 0)),
            pl.BlockSpec((width, rows), lambda u: (0, u)),
        ],
        out_shape=[
            jax.ShapeDtypeStruct((2 * rows, width), BF),
            jax.ShapeDtypeStruct((width, 2 * rows), BF),
        ],
        scratch_shapes=[pltpu.VMEM((width, rows), BF), pltpu.VMEM((rows, rows), BF)],
        compiler_params=params("arbitrary"),
        cost_estimate=cost(4 * rows * rows * width, 6 * rows * width * 2),
    )(index.reshape(2, 1, rows), arrived, *after)


def student_kernel(slots, place_ref, here_ref, there_ref, w_ref, q_ref, band_ref, mine_ref, give_ref):
    rows, feats = q_ref.shape
    half, clip = place_ref[0], place_ref[1]
    total = None
    for i, ref in enumerate((here_ref, here_ref, there_ref, there_ref)):
        c = pl.multiple_of((clip ^ CLIPS[i]) * feats, feats)
        part = lax.dot_general(
            ref[i % 2], w_ref[:, pl.ds(c, feats)], NT, preferred_element_type=F32
        )
        total = part if total is None else total + part
    g = total.astype(BF)
    q = q_ref[...] * BF(1.0 / math.sqrt(HDIM))
    heads = []
    for y in range(2):
        cols = []
        for s in range(slots):
            c = (y * slots + s) * HDIM
            cols += [q[:, c : c + HDIM], g[:, c : c + HDIM]]
        heads.append(jnp.concatenate(cols, axis=1))
    mine_ref[:rows] = jnp.where(half == 0, heads[0], heads[1])
    give_ref[:rows] = jnp.where(half == 0, heads[1], heads[0])
    mine_ref[rows:] = band_ref[...]
    give_ref[rows:] = band_ref[...]


def student_side(place, here, there, weight, query, band, slots):
    rows, feats = query.shape
    vm = pl.BlockSpec(memory_space=pltpu.VMEM)
    return pl.pallas_call(
        functools.partial(student_kernel, slots),
        in_specs=[pl.BlockSpec(memory_space=pltpu.SMEM)] + [vm] * 5,
        out_specs=[vm] * 2,
        out_shape=[jax.ShapeDtypeStruct((rows + band.shape[0], 2 * slots * HDIM), BF)] * 2,
        compiler_params=params(),
        cost_estimate=cost(8 * rows * feats * feats, 16 * rows * feats),
    )(place, here, there, weight, query, band)


def cotangent_kernel(place_ref, here_ref, there_ref, after_ref, out_ref):
    cols = here_ref.shape[2]
    for i, ref in enumerate((here_ref, here_ref, there_ref, there_ref)):
        c = pl.multiple_of((place_ref[1] ^ CLIPS[i]) * cols, cols)
        out_ref[:, pl.ds(c, cols)] = ref[i % 2]


def whole_cotangent(place, here, there, after):
    _, rows, cols = here.shape
    vm = pl.BlockSpec(memory_space=pltpu.VMEM)
    return pl.pallas_call(
        cotangent_kernel,
        in_specs=[
            pl.BlockSpec(memory_space=pltpu.SMEM),
            vm,
            vm,
            pl.BlockSpec(memory_space=pl.ANY),
        ],
        out_specs=vm,
        out_shape=jax.ShapeDtypeStruct((rows, 4 * cols), BF),
        compiler_params=params(),
        cost_estimate=cost(0, 16 * rows * cols),
    )(place, here, there, after)


def edge_kernel(place_ref, mine_ref, peer_ref, after_ref, a_ref, b_ref):
    first = place_ref[0] == 0
    mine, peer = mine_ref[...], peer_ref[...]
    a_ref[...] = jnp.where(first, mine, peer)
    b_ref[...] = jnp.where(first, peer, mine)


def edges(place, mine, peer, after):
    vm = pl.BlockSpec(memory_space=pltpu.VMEM)
    return pl.pallas_call(
        edge_kernel,
        in_specs=[
            pl.BlockSpec(memory_space=pltpu.SMEM),
            vm,
            vm,
            pl.BlockSpec(memory_space=pl.ANY),
        ],
        out_specs=[vm] * 2,
        out_shape=[jax.ShapeDtypeStruct(mine.shape, BF)] * 2,
        compiler_params=params(),
        cost_estimate=cost(0, 8 * mine.size),
    )(place, mine, peer, after)


def tails_kernel(left_ref, right_ref, after_ref, out_ref):
    out_ref[0] = left_ref[...]
    out_ref[1] = right_ref[...]


def tails(left, right, count, after):
    width = left.shape[1]
    last = pl.BlockSpec((count, width), lambda i: (left.shape[0] // count - 1, 0))
    return pl.pallas_call(
        tails_kernel,
        grid=(1,),
        in_specs=[last, last, pl.BlockSpec(memory_space=pl.ANY)],
        out_specs=pl.BlockSpec((2, count, width), lambda i: (0, 0, 0)),
        out_shape=jax.ShapeDtypeStruct((2, count, width), BF),
        compiler_params=params("arbitrary"),
        cost_estimate=cost(0, 8 * count * width),
    )(left, right, after)


def split3(x):
    a = x.astype(BF).astype(F32)
    b = (x - a).astype(BF).astype(F32)
    c = (x - a - b).astype(BF).astype(F32)
    return [a, b, c]


def attend_kernel(slots, tiles, by_exchange, place_ref, lohi_ref, qga_ref, qgb_ref, *refs):
    outa_ref, outb_ref = refs[-2 * tiles - 2 : -2 * tiles]
    s_refs, d_refs = refs[-2 * tiles : -tiles], refs[-tiles:]
    rows = outa_ref.shape[1]
    blocks = refs[0].shape[0] // TBLK
    nblk = TILE // SBLK
    cblk = CHUNK // TBLK
    lane = lax.broadcasted_iota(jnp.int32, (1, TILE), 1)
    rhs_lane = lax.broadcasted_iota(jnp.int32, (TILE, 2 * HDIM), 1)
    row_id = lax.broadcasted_iota(jnp.int32, (STATS, TILE), 0)
    z8 = jnp.zeros((8, TILE), F32)
    odd = place_ref[2] % 2 == 1

    def stores(place, out):
        def first():
            outa_ref[place] = out

        def second():
            outb_ref[place] = out

        return first, second

    for (i, slot), (u, q_ref) in itertools.product(
        enumerate(slots), ((0, qga_ref), (1, qgb_ref))
    ):
        kv_ref, kvt_ref = refs[2 * i : 2 * i + 2]
        own = slice(slot * 2 * HDIM, (slot + 1) * 2 * HDIM)
        out_rows = slice(i * OUT, (i + 1) * OUT)

        def group(g, carry):
            held = []
            n = jnp.int32(0)
            for k in range(tiles):
                t = g * tiles + k
                base = u * (rows // SBLK) + t * nblk
                los = [lohi_ref[0, base + i] for i in range(nblk)]
                his = [lohi_ref[1, base + i] for i in range(nblk)]
                lo, hi = los[0], his[0]
                lo_lane = jnp.full((1, TILE), los[0])
                hi_lane = jnp.full((1, TILE), his[0])
                for i in range(1, nblk):
                    lo = jnp.minimum(lo, los[i])
                    hi = jnp.maximum(hi, his[i])
                    lo_lane = jnp.where(lane < i * SBLK, lo_lane, los[i])
                    hi_lane = jnp.where(lane < i * SBLK, hi_lane, his[i])
                lo = jnp.maximum(lo, 0)
                hi = jnp.minimum(hi, blocks - 1)
                n = jnp.maximum(n, jnp.maximum(hi - lo + cblk, 0) // cblk)
                r = pl.multiple_of(t * TILE, TILE)
                qg = q_ref[pl.ds(r, TILE), own]
                zero = jnp.zeros_like(qg)
                rhs = jnp.concatenate(
                    [
                        jnp.where(rhs_lane < HDIM, qg, zero),
                        jnp.where(rhs_lane < HDIM, zero, qg),
                    ],
                    axis=0,
                )
                held.append((lo, lo_lane, hi_lane, rhs, r))

            def start(i, lo):
                kb = jnp.minimum(lo + i * cblk, blocks - cblk)
                return kb, pl.multiple_of(kb * TBLK, TBLK)

            def scores(i, tops):
                s0 = pl.multiple_of(i * CHUNK, CHUNK)
                new = []
                for k, (lo, lo_lane, hi_lane, rhs, _) in enumerate(held):
                    kb0, k0 = start(i, lo)
                    low = jnp.maximum(lo_lane, lo + i * cblk)
                    sd = lax.dot_general(
                        kv_ref[pl.ds(k0, CHUNK), :], rhs, NT, preferred_element_type=F32
                    )
                    d_refs[k][pl.ds(s0, CHUNK), :] = sd[:, TILE:]
                    m = tops[k]
                    for b in range(cblk):
                        ok = (low <= kb0 + b) & (hi_lane >= kb0 + b)
                        s = jnp.where(ok, sd[b * TBLK : (b + 1) * TBLK, :TILE], NEG)
                        s_refs[k][pl.ds(s0 + b * TBLK, TBLK), :] = s
                        m = jnp.maximum(m, jnp.max(s.reshape(TBLK // 8, 8, TILE), axis=0))
                    new.append(m)
                return tuple(new)

            tops = lax.fori_loop(
                0, n, scores, tuple(jnp.full((8, TILE), NEG, F32) for _ in range(tiles))
            )
            tops = [jnp.max(m, axis=0, keepdims=True) for m in tops]

            def expo(i, sums):
                s0 = pl.multiple_of(i * CHUNK, CHUNK)
                new = []
                for k in range(tiles):
                    l, dl = sums[k]
                    p = jnp.exp(s_refs[k][pl.ds(s0, CHUNK), :] - tops[k])
                    s_refs[k][pl.ds(s0, CHUNK), :] = p
                    l = l + jnp.sum(p.reshape(CHUNK // 8, 8, TILE), axis=0)
                    pd = p * d_refs[k][pl.ds(s0, CHUNK), :]
                    dl = dl + jnp.sum(pd.reshape(CHUNK // 8, 8, TILE), axis=0)
                    new.append((l, dl))
                return tuple(new)

            ends = []
            for l, dl in lax.fori_loop(0, n, expo, ((z8, z8),) * tiles):
                l = jnp.sum(l, axis=0, keepdims=True)
                inv = 1.0 / jnp.maximum(l, 1e-30)
                ends.append((l, inv, jnp.sum(dl, axis=0, keepdims=True) * inv))

            def products(i, accs):
                s0 = pl.multiple_of(i * CHUNK, CHUNK)
                new = []
                for k in range(tiles):
                    _, k0 = start(i, held[k][0])
                    p = s_refs[k][pl.ds(s0, CHUNK), :]
                    ds = p * (d_refs[k][pl.ds(s0, CHUNK), :] - ends[k][2])
                    both = jnp.concatenate([p.astype(BF), ds.astype(BF)], axis=1)
                    new.append(
                        accs[k]
                        + jnp.dot(
                            kvt_ref[:, pl.ds(k0, CHUNK)], both, preferred_element_type=F32
                        )
                    )
                return tuple(new)

            accs = lax.fori_loop(
                0, n, products, tuple(jnp.zeros((2 * HDIM, 2 * TILE), F32) for _ in range(tiles))
            )
            for k in range(tiles):
                l, inv, delta = ends[k]
                acc = accs[k] * jnp.concatenate([inv, inv], axis=1)
                stats = jnp.where(row_id == 9, 1.0, 0.0)
                for i, piece in enumerate(split3(tops[k]) + split3(l) + split3(delta)):
                    stats = jnp.where(row_id == i, piece, stats)
                out = jnp.concatenate([acc[:, :TILE], acc[:HDIM, TILE:], stats], axis=0)
                place = (out_rows, pl.ds(held[k][4], TILE))
                out = out.astype(outa_ref.dtype)
                if by_exchange:
                    jax.lax.cond(odd == (u == 0), *stores(place, out))
                else:
                    (outa_ref, outb_ref)[u][place] = out
            return carry

        lax.fori_loop(0, rows // (TILE * tiles), group, 0)


def attend(place, slots, tiles, rows, lohi, qga, qgb, kvs, by_exchange, *after):
    keys = kvs[0].shape[0]
    n = len(slots)
    vm = pl.BlockSpec(memory_space=pltpu.VMEM)
    return pl.pallas_call(
        functools.partial(attend_kernel, slots, tiles, by_exchange),
        in_specs=[pl.BlockSpec(memory_space=pltpu.SMEM)] * 2
        + [vm] * (2 + 2 * n)
        + [pl.BlockSpec(memory_space=pl.ANY)] * len(after),
        out_specs=[vm] * 2,
        out_shape=[jax.ShapeDtypeStruct((n * OUT, rows), BF)] * 2,
        scratch_shapes=[pltpu.VMEM((keys, TILE), F32)] * (2 * tiles),
        compiler_params=params(),
        cost_estimate=cost(
            n * rows * keys * 1024, n * (4 * keys * 128 + 16 * rows * 256), n * rows * keys
        ),
    )(place, lohi, qga, qgb, *kvs, *after)


def combine_kernel(groups, slots, place_ref, cot_ref, pcot_ref, *refs):
    parts, refs = refs[: 2 * slots + 2], refs[2 * slots + 2 :]
    mine_ref, give_ref, xmine_ref, xgive_ref = refs[:4]
    shares, buf, oqa_ref, oqb_ref = refs[4:-3], refs[-3], refs[-2], refs[-1]
    scale = 1.0 / math.sqrt(HDIM)
    odd = place_ref[2] % 2 == 1
    for u, oq_ref in enumerate((oqa_ref, oqb_ref)):
        for s in range(slots):
            own = parts[2 * s + u][...].astype(F32)
            rem = [r[s * OUT : (s + 1) * OUT] for r in parts[2 * slots :]]
            rem = jnp.where(odd == (u == 0), *rem).astype(F32)

            def stat(x, i):
                r = 3 * HDIM + 3 * i
                return x[r : r + 1] + x[r + 1 : r + 2] + x[r + 2 : r + 3]

            flag = rem[3 * HDIM + 9 : 3 * HDIM + 10]
            m_o, m_r = stat(own, 0), jnp.where(flag > 0.5, stat(rem, 0), NEG)
            l_o, l_r = stat(own, 1), stat(rem, 1)
            d_o, d_r = stat(own, 2), stat(rem, 2)
            top = jnp.maximum(m_o, m_r)
            w_o = l_o * jnp.exp(m_o - top)
            w_r = jnp.where(m_r > 0.5 * NEG, l_r * jnp.exp(m_r - top), 0.0)
            norm = 1.0 / (w_o + w_r)
            w_o, w_r = w_o * norm, w_r * norm
            delta = w_o * d_o + w_r * d_r
            attn = w_o * own[HDIM : 2 * HDIM] + w_r * rem[HDIM : 2 * HDIM]
            s_o, s_r = scale * w_o, scale * w_r
            dq = s_o * own[2 * HDIM : 3 * HDIM] - (s_o * (delta - d_o)) * own[:HDIM]
            dq += s_r * rem[2 * HDIM : 3 * HDIM] - (s_r * (delta - d_r)) * rem[:HDIM]
            oq_ref[s * HDIM : (s + 1) * HDIM] = attn.astype(BF)
            oq_ref[(slots + s) * HDIM : (slots + s + 1) * HDIM] = dq.astype(BF)
    first = place_ref[0] == 0
    attn_a, attn_b = oqa_ref[: slots * HDIM], oqb_ref[: slots * HDIM]
    total = jnp.dot(
        jnp.where(first, attn_a, attn_b), cot_ref[...], preferred_element_type=F32
    )
    total += jnp.dot(
        jnp.where(first, attn_b, attn_a), pcot_ref[...], preferred_element_type=F32
    )
    total = total.astype(BF)
    step = total.shape[1] // groups
    for g in range(groups):
        buf[g] = total[:, g * step : (g + 1) * step]
    for d in range(groups):
        shares[d][...] = buf[place_ref[2] ^ d]
    a, b = oqa_ref[...], oqb_ref[...]
    mine, give = jnp.where(first, a, b).T, jnp.where(first, b, a).T
    mine_ref[...] = mine
    give_ref[...] = give
    xmine_ref[...] = mine[:, : slots * HDIM]
    xgive_ref[...] = give[:, : slots * HDIM]


def combine(place, cot, peer_cot, parts, groups, slots):
    rows = parts[0].shape[1]
    width = cot.shape[1]
    vm = pl.BlockSpec(memory_space=pltpu.VMEM)
    share = (slots * HDIM, width // groups)
    return pl.pallas_call(
        functools.partial(combine_kernel, groups, slots),
        in_specs=[pl.BlockSpec(memory_space=pltpu.SMEM)] + [vm] * (4 + 2 * slots),
        out_specs=[vm] * (4 + groups),
        out_shape=[jax.ShapeDtypeStruct((rows, 2 * slots * HDIM), BF)] * 2
        + [jax.ShapeDtypeStruct((rows, slots * HDIM), BF)] * 2
        + [jax.ShapeDtypeStruct(share, BF)] * groups,
        scratch_shapes=[pltpu.VMEM((groups, *share), BF)]
        + [pltpu.VMEM((2 * slots * HDIM, rows), BF)] * 2,
        compiler_params=params(),
        cost_estimate=cost(
            4 * rows * slots * HDIM * width, 4 * rows * width + 24 * rows * slots * 256
        ),
    )(place, cot, peer_cot, *parts)


def heads_kernel(place_ref, mine_ref, peer_ref, xmine_ref, xpeer_ref, x_ref, gq_ref):
    first = place_ref[0] == 0
    width = gq_ref.shape[1]

    def put(near, far):
        return jnp.concatenate(
            [jnp.where(first, near, far), jnp.where(first, far, near)], axis=1
        )

    mine, peer = mine_ref[...], peer_ref[...]
    x_ref[:, :width] = put(mine[:, : width // 2], peer[:, : width // 2])
    x_ref[:, width:] = put(xmine_ref[...], xpeer_ref[...])
    gq_ref[...] = put(mine[:, width // 2 :], peer[:, width // 2 :])


def heads(place, mine, peer, xmine, xpeer):
    rows, width = mine.shape
    vm = pl.BlockSpec(memory_space=pltpu.VMEM)
    return pl.pallas_call(
        heads_kernel,
        in_specs=[pl.BlockSpec(memory_space=pltpu.SMEM)] + [vm] * 4,
        out_specs=[vm] * 2,
        out_shape=[
            jax.ShapeDtypeStruct((rows, 2 * width), BF),
            jax.ShapeDtypeStruct((rows, width), BF),
        ],
        compiler_params=params(),
        cost_estimate=cost(0, 12 * rows * width),
    )(place, mine, peer, xmine, xpeer)


def project_kernel(here_ref, there_ref, *refs):
    columns, out_ref, token_ref = refs[:-2], refs[-2], refs[-1]
    token_ref[...] = jnp.zeros_like(token_ref)
    cols = columns[0].shape[0]
    total = None
    for i, w in enumerate(columns):
        ref = (here_ref, there_ref)[i % 2]
        c = i // 2 * cols
        part = jnp.dot(ref[:, c : c + cols], w[...], preferred_element_type=F32)
        total = part if total is None else total + part
    out_ref[...] = total.astype(BF)


def project(here, there, columns):
    rows, cols = here.shape[0], columns[0].shape[1]
    vm = pl.BlockSpec(memory_space=pltpu.VMEM)
    return pl.pallas_call(
        project_kernel,
        in_specs=[vm] * (2 + len(columns)),
        out_specs=[vm] * 2,
        out_shape=[
            jax.ShapeDtypeStruct((rows, cols), BF),
            jax.ShapeDtypeStruct((8, 128), F32),
        ],
        compiler_params=params(),
        cost_estimate=cost(2 * rows * cols * 4 * cols, 12 * rows * cols),
    )(here, there, *columns)


def spread_kernel(groups, place_ref, *refs):
    held, out_ref, buf = refs[:groups], refs[-2], refs[-1]
    step = held[0].shape[2]
    y = pl.program_id(0) ^ place_ref[0]
    for d, ref in enumerate(held):
        buf[d] = ref[y].astype(F32)
    for g in range(groups):
        out_ref[:, g * step : (g + 1) * step] = buf[g ^ place_ref[2]]


def spread(place, held, *after):
    groups = len(held)
    _, rows, step = held[0].shape
    whole = pl.BlockSpec(held[0].shape, lambda i: (0, 0, 0))
    return pl.pallas_call(
        functools.partial(spread_kernel, groups),
        grid=(2,),
        in_specs=[pl.BlockSpec(memory_space=pltpu.SMEM)]
        + [whole] * groups
        + [pl.BlockSpec(memory_space=pl.ANY)] * len(after),
        out_specs=pl.BlockSpec((rows, groups * step), lambda i: (i, 0)),
        out_shape=jax.ShapeDtypeStruct((2 * rows, groups * step), F32),
        scratch_shapes=[pltpu.VMEM((groups, rows, step), F32)],
        compiler_params=params("arbitrary"),
        cost_estimate=cost(0, 2 * groups * rows * step * 6),
    )(place, *held, *after)


def on_device(
    groups,
    student_query,
    teacher_key,
    teacher_value,
    clip_order,
    band_start,
    band_end,
    output_weight,
    cotangent,
):
    shards = 2 * groups
    me = lax.axis_index("tm")
    clip = lax.axis_index("clip")
    half = me % 2
    z = me // 2
    place = jnp.stack([half, clip, z]).astype(jnp.int32)
    clips = lax.axis_size("clip")
    teacher_rows = teacher_key.shape[0]
    rows, feats = student_query.shape
    piece = teacher_rows // shards
    slots = feats // HDIM // 2
    hw = slots * HDIM

    def swap(x, d):
        return lax.ppermute(x, "tm", [(i, i ^ d) for i in range(shards)])

    def swap_clip(x, d):
        return lax.ppermute(x, "clip", [(i, i ^ d) for i in range(clips)])

    def swap_both(x, d):
        n = shards * clips
        return lax.ppermute(x, ("tm", "clip"), [(i, i ^ (clips + d)) for i in range(n)])

    def up(x):
        return lax.ppermute(x, "tm", [(i, i + 2) for i in range(shards - 2)])

    def down(x):
        return lax.ppermute(x, "tm", [(i + 2, i) for i in range(shards - 2)])

    here = jnp.stack([cotangent, swap_clip(cotangent, 2)])
    there = swap_clip(here, 1)
    blocks = band_start.shape[0]
    band = jnp.stack([band_start, band_end]).astype(BF)
    band = jnp.pad(band, ((0, 14), (0, 2 * hw - blocks)))
    qg_mine, qg_give = student_side(
        place, here, there, output_weight, student_query, band, slots
    )
    qg_peer = swap(qg_give, 1)
    sent = [pack(teacher_key, teacher_value, groups, slots, 0)]
    sent += [
        gate(pack(teacher_key, teacher_value, groups, slots, s), qg_peer)
        for s in range(1, slots)
    ]
    qga = jnp.where(half == 0, qg_mine, qg_peer)
    qgb = jnp.where(half == 0, qg_peer, qg_mine)

    origin = z * 2 * blocks

    def limits(first_rows, *firsts):
        bands = [x[:2, :blocks] for x in first_rows]
        bands = jnp.concatenate(bands, axis=1).astype(F32).astype(jnp.int32)
        frame = [origin + f + jnp.arange(blocks, dtype=jnp.int32) for f in firsts]
        frame = jnp.concatenate(frame)
        lo = jnp.maximum(frame + bands[0], 0) - origin
        hi = jnp.minimum(frame + bands[1], shards * blocks - 1) - origin
        return jnp.stack([lo, hi])

    own_limits = limits((qga[rows:], qgb[rows:]), 0, blocks)

    def columns_for(d):
        c = (clip ^ d) * feats
        return lax.dynamic_slice_in_dim(output_weight, c, feats, axis=1)

    columns = [columns_for(0)] + [swap_clip(columns_for(d), d) for d in range(1, clips)]

    lookup = lax.dynamic_slice_in_dim(clip_order, z * 2 * teacher_rows, 2 * teacher_rows)
    index = lookup // teacher_rows * piece + lookup % piece

    kvs, parts = [], []
    for s in range(slots):
        arrived = lax.all_to_all(
            sent[s].reshape(shards, 2 * piece, 2 * HDIM), "tm", 0, 0
        )
        kv, kvt = put_in_order(arrived, index, teacher_rows, *parts[-2:-1])
        kvs += [kv, kvt]
        if s == slots - 1:
            count = band.shape[0]
            ends = tails(qg_left, qg_right, count, kvs[-1])
            halo_limits = limits(ends, -blocks, 2 * blocks)
            far = attend(
                place, range(slots), 2, rows, halo_limits, qg_left, qg_right, kvs, True
            )
        own = place, [s], 4, rows, own_limits, qga, qgb, kvs[-2:], False
        parts += attend(*own, *(far if s == slots - 1 else ()))
        if s == 0:
            edge_a, edge_b = edges(place, qg_mine, qg_peer, kv)
            qg_left, qg_right = up(edge_b), down(edge_a)
            cot = whole_cotangent(place, here, there, parts[0])
    parts += [swap(far[0], 2)]
    links = [(i, i + 2) for i in range(shards - 2) if i // 2 % 2]
    parts += [lax.ppermute(far[1], "tm", links + [(j, i) for i, j in links])]
    mine, give, xmine, xgive, *got = combine(place, cot, swap(cot, 1), parts, groups, slots)
    total = got[0].astype(F32)
    for d in range(1, groups):
        total += swap(got[d], 2 * d).astype(F32)
    total = total.astype(BF)
    both = jnp.stack([total, swap(total, 1)])
    held = [both] + [swap(both, 2 * d) for d in range(1, groups)]
    near, grad_query = heads(
        place, mine, swap(give, 1), swap_clip(xmine, 2), swap_both(xgive, 2)
    )
    joined, token = project(near, swap_clip(near, 1), columns)
    return joined, grad_query, spread(place, held, token)


def solution(mesh):
    return jax.shard_map(
        functools.partial(on_device, mesh.shape["tm"] // 2),
        mesh=mesh,
        in_specs=(
            P("tm", "clip"),
            P("tm", "clip"),
            P("tm", "clip"),
            P(),
            P("tm"),
            P("tm"),
            P("clip", None),
            P("tm", "clip"),
        ),
        out_specs=(P("tm", "clip"), P("tm", "clip"), P("clip", None)),
        check_vma=False,
    )
```
